128 devices in a mesh: seq: 16 (over y, x), exp: 8 (over z, core).
Axes of the slice: x: 4, y: 4, z: 4, core: 2. Of those that a mesh axis runs over, the one named last changes fastest.
Arguments:
- queries: bfloat16 [2048, 12288], P('seq', 'exp'), may hold values from -160 to 160
- keys: bfloat16 [2048, 1024], P('seq', 'exp'), may hold values from -8 to 8
- values: bfloat16 [2048, 1024], P('seq', 'exp'), may hold values from -6 to 6
- cache_keys: bfloat16 [16384, 1024], P('seq', 'exp'), may hold values from -6 to 6
- cache_values: bfloat16 [16384, 1024], P('seq', 'exp'), may hold values from -6 to 6
- vertical: int32 [8, 16], P('exp'), may hold values from 0 to 255, as said below
- offsets: int32 [8, 4], P('exp'), may hold values from 1 to 6, as said below
- o_weight: bfloat16 [12288, 6144], P('exp', 'seq'), may hold values from -0.0546875 to 0.0546875
- residual: bfloat16 [2048, 6144], P(('seq', 'exp')), may hold values from -2 to 2
- norm_gain: float32 [6144], replicated, may hold values from 0.5 to 1.5
- expert_ids: int32 [2048, 2], P(('seq', 'exp')), may hold values from 0 to 15, all different within a row; in each aligned block of 16 rows (0 to 15, 16 to 31, ...) at most 4 rows name the same one
- gate_weights: float32 [2048, 2], P(('seq', 'exp')), may hold values from 0.1 to 1
- w_gate: bfloat16 [16, 6144, 2560], P('seq', None, 'exp'), may hold values from -0.078125 to 0.078125
- w_up: bfloat16 [16, 6144, 2560], P('seq', None, 'exp'), may hold values from -0.078125 to 0.078125
- w_down: bfloat16 [16, 2560, 6144], P('seq', 'exp'), may hold values from -0.125 to 0.125
Outputs:
- output: bfloat16 [2048, 6144], P(('seq', 'exp'))
The draws below stay inside these ranges and needn't reach their ends.
Inputs may be any that keep to these rules, and one draw needn't show every extreme that they name: `vertical`: each row lists 16 different cache block numbers. Each row holds 4 different offsets. `expert_ids`: each row names 2 different experts; in each aligned block of 16 rows (the rows of one device) no expert is named by more than 4 rows.
All inputs are finite; a program needn't handle non-finite values.
Results may differ from the reference program's by a relative error of at most 0.025.
Values may be sent and summed in bfloat16 or wider, within the bound.
A program may use at most 128 MiB of HBM per device.

```python
import math
import jax
import jax.numpy as jnp
import numpy as np
from jax import lax

D = 6144
QH = 96
KVH = 8
HD = 128
FF = 2560
BLK = 64
NV = 16
NS = 4
TOPK = 2
EXPERTS = 16
STRETCH = 2048
CTX = 16384
MAXOFF = 6
ROWS = 16
CAP = 4
N_SEQ = 16
N_EXP = 8


def draw_queries(key, part):
    key = jax.random.fold_in(key, 1)
    base = 2.0 * jnp.clip(jax.random.normal(key, (STRETCH, QH * HD), jnp.float32), -6.0, 6.0)
    return base.astype(jnp.bfloat16)


def draw_keys(key, part):
    key = jax.random.fold_in(key, 2)
    base = jnp.clip(jax.random.normal(key, (STRETCH, KVH * HD), jnp.float32), -6.0, 6.0)
    return base.astype(jnp.bfloat16)


def draw_vertical(key, part):
    key = jax.random.fold_in(key, 3)
    blocks = CTX // BLK

    def single(subkey):
        picked = jax.random.permutation(subkey, blocks - 1)[:NV - 1].astype(jnp.int32)
        return jnp.concatenate([picked, jnp.full((1,), blocks - 1, jnp.int32)])
    return jax.vmap(single)(jax.random.split(key, KVH))


def draw_offsets(key, part):
    key = jax.random.fold_in(key, 4)

    def single(subkey):
        picked = jax.random.permutation(subkey, MAXOFF - 1)[:NS - 1].astype(jnp.int32) + 1
        return jnp.concatenate([picked, jnp.full((1,), MAXOFF, jnp.int32)])
    return jax.vmap(single)(jax.random.split(key, KVH))


def block_scale(rng, dims, cuts, smallest, high):
    level = 1.0
    for dim, parts in cuts:
        draws = jax.random.uniform(jax.random.fold_in(jax.random.fold_in(rng, 6), dim), (parts,), jnp.float32, smallest / len(cuts), high / len(cuts))
        level = level * jnp.repeat(jnp.exp(draws), dims[dim] // parts).reshape((-1,) + (1,) * (len(dims) - 1 - dim))
    return level


def shared_out(own_key, own, number, rows, number_of, top, most, lean):
    ranking = jax.random.permutation(own_key, number_of)
    heavy_load, ordinary = portions_of(number_of, rows * top, most, lean, True), portions_of(number_of, rows * top, most, lean, False)
    places = jnp.arange(number_of)

    def named(tallies, rotation):
        used = int((tallies > 0).sum())
        fixed = max(1, used // 4)
        passed = fixed + (places - fixed + rotation * (used - fixed)) % max(1, number_of - fixed)
        return jnp.zeros((number_of,), jnp.int32).at[ranking[jnp.where(places < fixed, places, passed)]].set(jnp.asarray(tallies, jnp.int32))

    tallies = jnp.where(number % 4 == 0, named(heavy_load, number // 4), named(ordinary, number - number // 4 - 1))
    mixed = jax.random.permutation(jax.random.fold_in(own, 3), number_of)
    source_of, receiver = mixed[0:number_of // 2 * 2:2], mixed[1:number_of // 2 * 2:2]
    room = jnp.minimum(tallies[source_of] - 1, most - tallies[receiver]) // 2
    room = jnp.where((source_of == ranking[0]) | (receiver == ranking[0]) | (tallies[receiver] == 0), 0, jnp.maximum(room, 0))
    passed = jax.random.randint(jax.random.fold_in(own, 4), (number_of // 2,), 0, 1 << 20) % (room + 1)
    tallies = tallies.at[source_of].add(-passed).at[receiver].add(passed)
    items = jnp.searchsorted(jnp.cumsum(tallies), jnp.arange(rows * top), side="right").astype(jnp.int32)
    listing = items.reshape(top, rows).T
    listing = listing[jax.random.permutation(jax.random.fold_in(own, 1), rows)]
    rotation = jax.random.randint(jax.random.fold_in(own, 2), (rows, 1), 0, top)
    return jnp.take_along_axis(listing, (jnp.arange(top)[None, :] + rotation) % top, axis=1)


def portions_of(count, total, bound, skew, full):
    portions = [(1 << 20) // math.isqrt(standing ** skew) + 1 for standing in range(1, count + 1)]
    largest = bound if full else min(bound, max(-(-total // count), total * portions[0] // sum(portions)))
    least = 1 if total - largest >= count - 1 else 0
    given, spare = [largest] + [least] * (count - 1), total - largest - least * (count - 1)
    while spare > 0:
        movable = [i for i in range(1, count) if given[i] < largest] or [i for i in range(1, count) if given[i] < bound]
        pool, remaining = sum([portions[i] for i in movable]), spare
        for i in movable:
            addition = min(bound - given[i], max(1, remaining * portions[i] // pool), spare)
            given[i] = given[i] + addition
            spare = spare - addition
    return np.array(given)


def scatter_about(own_key, shape, spread, most, cuts=(), kind=jnp.bfloat16):
    entries = jax.random.normal(own_key, shape, jnp.float32) * spread
    if len(cuts) > 0:
        entries = block_scale(own_key, shape, cuts, -0.22, 0.18) * entries
    return jnp.clip(entries, min=-most, max=most).astype(kind)


def setup_inputs(seed: int = 0) -> dict:
    key_of = jax.random.split(jax.random.key(seed), 16)
    queries = draw_queries(jax.random.fold_in(key_of[15], 71), 0)
    keys = draw_keys(jax.random.fold_in(key_of[15], 71), 0)
    values = scatter_about(key_of[2], (STRETCH, KVH * HD), 1.0, 6.0, ((0, 16), (1, 8)))
    cache_keys = scatter_about(key_of[3], (CTX, KVH * HD), 1.0, 6.0, ((0, 16), (1, 8)))
    cache_values = scatter_about(key_of[4], (CTX, KVH * HD), 1.0, 6.0, ((0, 16), (1, 8)))
    vertical = draw_vertical(jax.random.fold_in(key_of[15], 71), 0)
    offsets = draw_offsets(jax.random.fold_in(key_of[15], 71), 0)
    o_weight = scatter_about(key_of[7], (QH * HD, D), (QH * HD) ** -0.5, 0.0546875, ((0, 8), (1, 16)))
    residual = scatter_about(key_of[8], (STRETCH, D), 0.25, 2.0, ((0, 128),))
    norm_gain = jnp.clip(1.0 + 0.1 * jax.random.normal(key_of[9], (D,), jnp.float32), 0.5, 1.5)
    expert_ids_keys = jax.random.split(jax.random.fold_in(key_of[10], 1), STRETCH // ROWS)
    expert_ids_turns = jax.random.permutation(jax.random.fold_in(key_of[10], 3), STRETCH // ROWS)
    expert_ids = jax.vmap(lambda own, number: shared_out(jax.random.fold_in(key_of[10], 2), own, number, ROWS, EXPERTS, TOPK, CAP, 2))(expert_ids_keys, expert_ids_turns).reshape((STRETCH, TOPK))
    gate_weights = jnp.clip(jnp.exp(math.log(1.0) - 2.3025851 * jax.random.uniform(key_of[11], (STRETCH, TOPK), jnp.float32) ** block_scale(key_of[11], (STRETCH, TOPK), ((0, 128),), -0.2, 0.2)), 0.1, 1.0)
    w_gate = scatter_about(key_of[12], (EXPERTS, D, FF), D ** -0.5, 0.078125, ((0, 16), (2, 8)))
    w_up = scatter_about(key_of[13], (EXPERTS, D, FF), D ** -0.5, 0.078125, ((0, 16), (2, 8)))
    w_down = scatter_about(key_of[14], (EXPERTS, FF, D), FF ** -0.5, 0.125, ((0, 16), (1, 8)))
    return {"queries": queries, "keys": keys, "values": values, "cache_keys": cache_keys, "cache_values": cache_values, "vertical": vertical, "offsets": offsets, "o_weight": o_weight, "residual": residual, "norm_gain": norm_gain, "expert_ids": expert_ids, "gate_weights": gate_weights, "w_gate": w_gate, "w_up": w_up, "w_down": w_down}


def attend(queries, keys, values, vert_keys, vert_values, offsets, query_block, key_block, block_size):
    query_count, kv_heads, group_size, head_size = queries.shape
    key_count = keys.shape[0]
    scale = 1.0 / math.sqrt(head_size)
    near = jnp.einsum('qhgd,khd->hgqk', queries.astype(jnp.float32), keys.astype(jnp.float32)) * scale
    distant = jnp.einsum('qhgd,hkd->hgqk', queries.astype(jnp.float32), vert_keys.astype(jnp.float32)) * scale
    query_pos = jnp.arange(query_count, dtype=jnp.int32)
    key_pos = jnp.arange(key_count, dtype=jnp.int32)
    query_blocks = query_block + query_pos // block_size
    key_blocks = key_block + key_pos // block_size
    spacing = query_blocks[:, None] - key_blocks[None, :]
    within = (spacing == 0) & ((key_pos % block_size)[None, :] <= (query_pos % block_size)[:, None])
    banded = jnp.any(spacing[None, :, :, None] == offsets[:, None, None, :], axis=3)
    banded = banded & (key_blocks >= 0)[None, None, :]
    allowed = within[None] | banded
    near = jnp.where(allowed[:, None], near, -jnp.inf)
    highest = jnp.maximum(lax.optimization_barrier(jnp.max(near, axis=3)), lax.optimization_barrier(jnp.max(distant, axis=3)))
    near_exp = jnp.exp(near - highest[..., None])
    distant_exp = jnp.exp(distant - highest[..., None])
    denominator = lax.optimization_barrier(jnp.sum(near_exp, axis=3)) + lax.optimization_barrier(jnp.sum(distant_exp, axis=3))
    near_weights = (near_exp / denominator[..., None]).astype(jnp.bfloat16)
    distant_weights = (distant_exp / denominator[..., None]).astype(jnp.bfloat16)
    mixed = jnp.einsum('hgqk,khd->qhgd', near_weights.astype(jnp.float32), values.astype(jnp.float32))
    mixed = mixed + jnp.einsum('hgqk,hkd->qhgd', distant_weights.astype(jnp.float32), vert_values.astype(jnp.float32))
    return mixed.reshape(query_count, kv_heads * group_size * head_size).astype(jnp.bfloat16)

def reference(queries, keys, values, cache_keys, cache_values, vertical, offsets, o_weight, residual, norm_gain, expert_ids, gate_weights, w_gate, w_up, w_down):
    group_size = QH // KVH
    query_heads = queries.reshape(STRETCH, KVH, group_size, HD)
    key_heads = keys.reshape(STRETCH, KVH, HD)
    value_heads = values.reshape(STRETCH, KVH, HD)
    key_blocks = cache_keys.reshape(CTX // BLK, BLK, KVH, HD)
    value_blocks = cache_values.reshape(CTX // BLK, BLK, KVH, HD)
    pieces = []
    for head in range(KVH):
        vert_keys = key_blocks[vertical[head]][:, :, head, :].reshape(1, NV * BLK, HD)
        vert_values = value_blocks[vertical[head]][:, :, head, :].reshape(1, NV * BLK, HD)
        pieces.append(attend(query_heads[:, head:head + 1], key_heads[:, head:head + 1], value_heads[:, head:head + 1], vert_keys, vert_values, offsets[head:head + 1], 0, 0, BLK))
    attention = jnp.concatenate(pieces, axis=1)
    projected = jnp.dot(attention, o_weight, preferred_element_type=jnp.float32)
    stream = residual.astype(jnp.float32) + projected
    normed = (stream * lax.rsqrt(lax.optimization_barrier(jnp.mean(stream * stream, axis=1, keepdims=True)) + 1e-06) * norm_gain.astype(jnp.float32)).astype(jnp.bfloat16)
    limit = CAP * N_SEQ * N_EXP
    slice_width = FF // N_EXP
    mixture = jnp.zeros((STRETCH, D), jnp.float32)
    for expert in range(EXPERTS):
        coefficient = lax.optimization_barrier(jnp.sum(jnp.where(expert_ids == expert, gate_weights, jnp.zeros_like(gate_weights)), axis=1))
        routed = jnp.any(expert_ids == expert, axis=1)
        chosen_rows = jnp.nonzero(routed, size=limit, fill_value=0)[0].astype(jnp.int32)
        valid = jnp.arange(limit, dtype=jnp.int32) < jnp.sum(routed.astype(jnp.int32))
        inputs = normed[chosen_rows]
        gate = jnp.dot(inputs, w_gate[expert], preferred_element_type=jnp.float32)
        upward = jnp.dot(inputs, w_up[expert], preferred_element_type=jnp.float32)
        hidden = (jax.nn.silu(gate) * upward).astype(jnp.bfloat16)
        expert_out = jnp.zeros((limit, D), jnp.float32)
        for part_index in range(N_EXP):
            lower = part_index * slice_width
            term = jnp.dot(hidden[:, lower:lower + slice_width], w_down[expert][lower:lower + slice_width], preferred_element_type=jnp.float32)
            expert_out = expert_out + lax.optimization_barrier(term.astype(jnp.bfloat16)).astype(jnp.float32)
        scaled = jnp.where(valid, coefficient[chosen_rows], jnp.zeros_like(coefficient[chosen_rows]))
        mixture = mixture.at[chosen_rows].add(scaled[:, None] * expert_out)
    return (stream + mixture).astype(jnp.bfloat16)
```

```python
import functools
import math

import jax
import jax.numpy as jnp
from jax import lax
from jax.experimental import pallas as pl
from jax.experimental.pallas import tpu as pltpu
from jax.sharding import PartitionSpec as P

HD = 128
BLK = 64
NV = 16
MAXOFF = 6
SEQ = 16
EXP = 8
GROUP = 12
MESH = pl.DeviceIdType.MESH
BF = jnp.bfloat16
F32 = jnp.float32


def greet(axis, me, size):
    barrier = pltpu.get_barrier_semaphore()

    def one(d, _):
        pl.semaphore_signal(
            barrier, inc=1, device_id={axis: lax.rem(me + d, size)}, device_id_type=MESH
        )
        return 0

    lax.fori_loop(1, size, one, 0)
    return barrier


def attention_kernel(
    offsets, sel, q, k, v, out, got, vert, near, s_sem, r_sem, s2_sem, r2_sem,
    sh_sem, rh_sem,
):
    me = lax.axis_index("seq")
    barrier = greet("seq", me, SEQ)

    near[0, 3] = k[...]
    near[1, 3] = v[...]
    got[:, me] = sel[:, me]

    pl.semaphore_wait(barrier, SEQ - 1)

    def piece(d):
        to = lax.rem(me + d, SEQ)
        return pltpu.make_async_remote_copy(
            src_ref=sel.at[:, to],
            dst_ref=got.at[:, me],
            send_sem=s_sem.at[d],
            recv_sem=r_sem.at[me],
            device_id={"seq": to},
            device_id_type=MESH,
        )

    def start_piece(d, _):
        piece(d).start()
        return 0

    lax.fori_loop(1, SEQ, start_piece, 0)

    def halo(d):
        return pltpu.make_async_remote_copy(
            src_ref=near.at[:, 3],
            dst_ref=near.at[:, 3 - d],
            send_sem=sh_sem.at[d],
            recv_sem=rh_sem.at[d],
            device_id={"seq": lax.rem(me + d, SEQ)},
            device_id_type=MESH,
        )

    for d in (1, 2, 3):
        halo(d).start()

    def arrived_piece(d, _):
        frm = lax.rem(me + d, SEQ)
        pltpu.make_async_remote_copy(
            src_ref=sel.at[:, 0],
            dst_ref=got.at[:, frm],
            send_sem=s_sem.at[0],
            recv_sem=r_sem.at[frm],
            device_id={"seq": frm},
            device_id_type=MESH,
        ).wait_recv()
        return 0

    lax.fori_loop(1, SEQ, arrived_piece, 0)
    total = got[:, 0].astype(F32)
    for j in range(1, SEQ):
        total = total + got[:, j].astype(F32)
    vert[:, me] = total.astype(BF)

    def share(d):
        return pltpu.make_async_remote_copy(
            src_ref=vert.at[:, me],
            dst_ref=vert.at[:, me],
            send_sem=s2_sem.at[d],
            recv_sem=r2_sem.at[me],
            device_id={"seq": lax.rem(me + d, SEQ)},
            device_id_type=MESH,
        )

    def start_share(d, _):
        share(d).start()
        return 0

    lax.fori_loop(1, SEQ, start_share, 0)

    for d in (1, 2, 3):
        halo(d).wait()

    qi = lax.broadcasted_iota(jnp.int32, (2 * BLK, 8 * BLK), 0)
    ki = lax.broadcasted_iota(jnp.int32, (2 * BLK, 8 * BLK), 1)
    spacing = qi // BLK + MAXOFF - ki // BLK
    banded = spacing == offsets[0, 0]
    for t in range(1, 4):
        banded = banded | (spacing == offsets[0, t])
    banded = banded & (ki // BLK + 2 * me >= MAXOFF)
    allowed = banded | ((spacing == 0) & (lax.rem(ki, BLK) <= lax.rem(qi, BLK)))

    def arrived_share(d, _):
        frm = lax.rem(me + d, SEQ)
        pltpu.make_async_remote_copy(
            src_ref=vert.at[:, me],
            dst_ref=vert.at[:, frm],
            send_sem=s2_sem.at[0],
            recv_sem=r2_sem.at[frm],
            device_id={"seq": frm},
            device_id_type=MESH,
        ).wait_recv()
        return 0

    lax.fori_loop(1, SEQ, arrived_share, 0)

    scale = 1.0 / math.sqrt(HD)
    nt = (((1,), (1,)), ((), ()))

    def head(h, _):
        cols = pl.ds(pl.multiple_of(h * HD, HD), HD)
        qh = q[:, cols]
        sn = lax.dot_general(
            qh, near[0].reshape(8 * BLK, HD), nt, preferred_element_type=F32
        ) * scale
        sv = lax.dot_general(
            qh, vert[0].reshape(NV * BLK, HD), nt, preferred_element_type=F32
        ) * scale
        sn = jnp.where(allowed, sn, -jnp.inf)
        top = jnp.maximum(
            jnp.max(sn, axis=1, keepdims=True), jnp.max(sv, axis=1, keepdims=True)
        )
        en = jnp.exp(sn - top)
        ev = jnp.exp(sv - top)
        inv = 1.0 / (jnp.sum(en, axis=1, keepdims=True) + jnp.sum(ev, axis=1, keepdims=True))
        wn = (en * inv).astype(BF)
        wv = (ev * inv).astype(BF)
        o = jnp.dot(wn, near[1].reshape(8 * BLK, HD), preferred_element_type=F32)
        o = o + jnp.dot(wv, vert[1].reshape(NV * BLK, HD), preferred_element_type=F32)
        out[:, cols] = o.astype(BF)
        return 0

    lax.fori_loop(0, GROUP, head, 0)

    def finish(d, _):
        piece(d).wait_send()
        share(d).wait_send()
        return 0

    lax.fori_loop(1, SEQ, finish, 0)


def pick_kernel(vertical, ck, cv, out, raw, sem):
    me = lax.axis_index("seq")

    def copies(j):
        rows = pl.ds(pl.multiple_of(lax.rem(vertical[0, j], NV) * BLK, BLK), BLK)
        return [
            pltpu.make_async_copy(ref.at[rows, :], raw.at[i, j], sem.at[i, j])
            for i, ref in enumerate((ck, cv))
        ]

    for j in range(NV):
        for c in copies(j):
            c.start()
    for j in range(NV):
        listed = jnp.full((BLK, HD), vertical[0, j], jnp.int32)
        here = (listed >= me * NV) & (listed < me * NV + NV)
        for i, c in enumerate(copies(j)):
            c.wait()
            out[i, j] = jnp.where(here, raw[i, j].astype(F32), 0.0).astype(BF)


def attention_of(queries, keys, values, cache_keys, cache_values, vertical, offsets):
    vm = pl.BlockSpec(memory_space=pltpu.VMEM)
    sm = pl.BlockSpec(memory_space=pltpu.SMEM)
    hbm = pl.BlockSpec(memory_space=pl.ANY)
    sel = pl.pallas_call(
        pick_kernel,
        out_shape=jax.ShapeDtypeStruct((2, NV, BLK, HD), BF),
        in_specs=[sm, hbm, hbm],
        out_specs=vm,
        scratch_shapes=[
            pltpu.VMEM((2, NV, BLK, HD), BF),
            pltpu.SemaphoreType.DMA((2, NV)),
        ],
        name="pick",
    )(vertical, cache_keys, cache_values)
    return pl.pallas_call(
        attention_kernel,
        out_shape=jax.ShapeDtypeStruct(queries.shape, BF),
        in_specs=[sm, vm, vm, vm, vm],
        out_specs=vm,
        scratch_shapes=[
            pltpu.VMEM((2, NV, BLK, HD), BF),
            pltpu.VMEM((2, NV, BLK, HD), BF),
            pltpu.VMEM((2, 4, 2 * BLK, HD), BF),
            pltpu.SemaphoreType.DMA((SEQ,)),
            pltpu.SemaphoreType.DMA((SEQ,)),
            pltpu.SemaphoreType.DMA((SEQ,)),
            pltpu.SemaphoreType.DMA((SEQ,)),
            pltpu.SemaphoreType.DMA((4,)),
            pltpu.SemaphoreType.DMA((4,)),
        ],
        compiler_params=pltpu.CompilerParams(
            collective_id=0, has_side_effects=True, vmem_limit_bytes=40 * 2**20
        ),
        name="attention",
    )(offsets, sel, queries, keys, values)


def shards(
    queries,
    keys,
    values,
    cache_keys,
    cache_values,
    vertical,
    offsets,
    o_weight,
    residual,
    norm_gain,
    expert_ids,
    gate_weights,
    w_gate,
    w_up,
    w_down,
):
    local_count = queries.shape[0]
    seq_count = lax.axis_size("seq")
    exp_count = lax.axis_size("exp")
    width = residual.shape[1]
    attention = attention_of(queries, keys, values, cache_keys, cache_values, vertical, offsets)
    column_count = o_weight.shape[1]
    partial_cols = jnp.dot(
        lax.all_gather(attention, "seq", axis=0, tiled=True),
        o_weight,
        preferred_element_type=jnp.float32,
    )
    row_count = local_count // exp_count
    grouped = partial_cols.reshape(seq_count, exp_count, row_count, column_count).transpose(
        1, 0, 2, 3
    )
    grouped = grouped.reshape(exp_count * seq_count * row_count, column_count)
    owned = lax.psum_scatter(
        grouped.astype(jnp.bfloat16), "exp", scatter_dimension=0, tiled=True
    ).astype(jnp.float32)
    projected = lax.all_to_all(
        owned.astype(jnp.bfloat16), "seq", split_axis=0, concat_axis=1, tiled=True
    ).astype(owned.dtype)
    stream = residual.astype(jnp.float32) + projected
    normed = (
        stream * lax.rsqrt(jnp.mean(stream * stream, axis=1, keepdims=True) + 1e-06) * norm_gain
    ).astype(jnp.bfloat16)
    top_count = expert_ids.shape[1]
    capacity = 2 * row_count * top_count // seq_count
    chosen = (
        expert_ids[:, :, None] == jnp.arange(seq_count, dtype=jnp.int32)[None, None, :]
    ).astype(jnp.int32)
    flat_chosen = chosen.reshape(row_count * top_count, seq_count)
    before = jnp.cumsum(flat_chosen, axis=0) - flat_chosen
    slots = jnp.sum(before * flat_chosen, axis=1).reshape(row_count, top_count)
    slot_marks = (
        slots[:, :, None, None] == jnp.arange(capacity, dtype=jnp.int32)[None, None, None, :]
    ).astype(jnp.int32)
    placed = chosen[:, :, :, None] * slot_marks
    routing = jnp.sum(placed, axis=1).transpose(1, 2, 0).astype(jnp.bfloat16)
    weighting = jnp.sum(
        placed.astype(jnp.float32) * gate_weights[:, :, None, None], axis=1
    ).transpose(1, 2, 0)
    gate_local = w_gate[0]
    up_local = w_up[0]
    down_local = w_down[0]
    outgoing = jnp.einsum(
        "ecr,rd->ecd", routing, normed, preferred_element_type=jnp.float32
    ).astype(jnp.bfloat16)
    arrived = lax.all_to_all(outgoing, "seq", split_axis=0, concat_axis=0, tiled=True)
    arrived = arrived.reshape(seq_count * capacity, width)
    piece = lax.all_gather(arrived, "exp", axis=0, tiled=True)
    gate = jnp.dot(piece, gate_local, preferred_element_type=jnp.float32)
    upward = jnp.dot(piece, up_local, preferred_element_type=jnp.float32)
    hidden = (jax.nn.silu(gate) * upward).astype(jnp.bfloat16)
    summed_out = lax.psum_scatter(
        jnp.dot(hidden, down_local, preferred_element_type=jnp.float32).astype(jnp.bfloat16),
        "exp",
        scatter_dimension=0,
        tiled=True,
    ).astype(jnp.float32)
    returned = lax.all_to_all(
        summed_out.reshape(seq_count, capacity, width).astype(jnp.bfloat16),
        "seq",
        split_axis=0,
        concat_axis=0,
        tiled=True,
    ).astype(jnp.float32)
    mixture = jnp.einsum("ecr,ecd->rd", weighting, returned, precision=lax.Precision.HIGHEST)
    return (stream + mixture).astype(jnp.bfloat16)


def solution(mesh):
    in_specs = (
        P("seq", "exp"),
        P("seq", "exp"),
        P("seq", "exp"),
        P("seq", "exp"),
        P("seq", "exp"),
        P("exp", None),
        P("exp", None),
        P("exp", "seq"),
        P(("seq", "exp"), None),
        P(),
        P(("seq", "exp"), None),
        P(("seq", "exp"), None),
        P("seq", None, "exp"),
        P("seq", None, "exp"),
        P("seq", "exp", None),
    )
    out_specs = P(("seq", "exp"), None)
    return jax.shard_map(shards, mesh=mesh, in_specs=in_specs, out_specs=out_specs, check_vma=False)
```

```python
import functools
import math

import jax
import jax.numpy as jnp
from jax import lax
from jax.experimental import pallas as pl
from jax.experimental.pallas import tpu as pltpu
from jax.sharding import PartitionSpec as P

HD = 128
BLK = 64
NV = 16
MAXOFF = 6
SEQ = 16
EXP = 8
GROUP = 12
ROWS = 16
QLEN = 128
DH = 1536
HALF = 768
OC = 384
WIDTH = 6144
MESH = pl.DeviceIdType.MESH
BF = jnp.bfloat16
F32 = jnp.float32
VM = pl.BlockSpec(memory_space=pltpu.VMEM)
SM = pl.BlockSpec(memory_space=pltpu.SMEM)
HBM = pl.BlockSpec(memory_space=pl.ANY)


def greet(axis, me, size):
    barrier = pltpu.get_barrier_semaphore()

    def one(d, _):
        pl.semaphore_signal(
            barrier, inc=1, device_id={axis: lax.rem(me + d, size)}, device_id_type=MESH
        )
        return 0

    lax.fori_loop(1, size, one, 0)


def send(src, dst, s, r, **where):
    return pltpu.make_async_remote_copy(
        src_ref=src, dst_ref=dst, send_sem=s, recv_sem=r, device_id=where, device_id_type=MESH
    )


def pick_kernel(vertical, ck, cv, out, raw, sem):
    me = lax.axis_index("seq")

    def copies(j):
        rows = pl.ds(pl.multiple_of(lax.rem(vertical[0, j], NV) * BLK, BLK), BLK)
        return [
            pltpu.make_async_copy(ref.at[rows, :], raw.at[i, j], sem.at[i, j])
            for i, ref in enumerate((ck, cv))
        ]

    for j in range(NV):
        for c in copies(j):
            c.start()
    for j in range(NV):
        listed = jnp.full((BLK, HD), vertical[0, j], jnp.int32)
        here = (listed >= me * NV) & (listed < me * NV + NV)
        for i, c in enumerate(copies(j)):
            c.wait()
            out[i, j] = jnp.where(here, raw[i, j].astype(F32), 0.0).astype(BF)


def front_kernel(
    offsets, sel_in, q_in, k_in, v_in, w_in, res_in, out,
    sel, q, near, w, res, got, vert, G, P_, keep, sib_s, sib_r, z_s, z_r, fin, proj,
    l_sem, s_sem, r_sem, s2_sem, r2_sem, sh_sem, rh_sem,
    gs_sem, gr_sem, bs_sem, br_sem, zs_sem, zr_sem, ps_sem, pr_sem,
):
    me = lax.axis_index("seq")
    e = lax.axis_index("exp")
    y, x = me // 4, lax.rem(me, 4)
    z, c = e // 2, lax.rem(e, 2)
    greet("seq", me, SEQ)
    greet("exp", e, EXP)

    loads = [
        pltpu.make_async_copy(a, b, l_sem.at[i])
        for i, (a, b) in enumerate(
            [(sel_in, sel), (k_in, near.at[0, 3]), (v_in, near.at[1, 3]), (q_in, q),
             (w_in, w), (res_in, res)]
        )
    ]
    for a in loads:
        a.start()
    for a in loads[:3]:
        a.wait()
    got[:, me] = sel[:, me]
    pl.semaphore_wait(pltpu.get_barrier_semaphore(), SEQ - 1 + EXP - 1)

    def piece(d):
        to = lax.rem(me + d, SEQ)
        return send(sel.at[:, to], got.at[:, me], s_sem.at[d], r_sem.at[me], seq=to)

    def share(d):
        to = lax.rem(me + d, SEQ)
        return send(vert.at[:, me], vert.at[:, me], s2_sem.at[d], r2_sem.at[me], seq=to)

    def halo(d):
        to = lax.rem(me + d, SEQ)
        return send(near.at[:, 3], near.at[:, 3 - d], sh_sem.at[d], rh_sem.at[d], seq=to)

    def start_piece(d, _):
        piece(d).start()
        return 0

    def start_share(d, _):
        share(d).start()
        return 0

    def arrived_piece(d, _):
        frm = lax.rem(me + d, SEQ)
        send(sel.at[:, 0], got.at[:, frm], s_sem.at[0], r_sem.at[frm], seq=frm).wait_recv()
        return 0

    def arrived_share(d, _):
        frm = lax.rem(me + d, SEQ)
        send(vert.at[:, me], vert.at[:, frm], s2_sem.at[0], r2_sem.at[frm], seq=frm).wait_recv()
        return 0

    lax.fori_loop(1, SEQ, start_piece, 0)
    for d in (1, 2, 3):
        halo(d).start()
    lax.fori_loop(1, SEQ, arrived_piece, 0)
    total = got[:, 0].astype(F32)
    for j in range(1, SEQ):
        total = total + got[:, j].astype(F32)
    vert[:, me] = total.astype(BF)
    lax.fori_loop(1, SEQ, start_share, 0)

    loads[3].wait()
    for d in (1, 2, 3):
        halo(d).wait()
    qi = lax.broadcasted_iota(jnp.int32, (2 * BLK, 8 * BLK), 0)
    ki = lax.broadcasted_iota(jnp.int32, (2 * BLK, 8 * BLK), 1)
    spacing = qi // BLK + MAXOFF - ki // BLK
    banded = spacing == offsets[0, 0]
    for t in range(1, 4):
        banded = banded | (spacing == offsets[0, t])
    banded = banded & (ki // BLK + 2 * me >= MAXOFF)
    allowed = banded | ((spacing == 0) & (lax.rem(ki, BLK) <= lax.rem(qi, BLK)))
    lax.fori_loop(1, SEQ, arrived_share, 0)

    scale = 1.0 / math.sqrt(HD)
    nt = (((1,), (1,)), ((), ()))

    def head(h, _):
        cols = pl.ds(pl.multiple_of(h * HD, HD), HD)
        qh = q[:, cols]
        sn = lax.dot_general(
            qh, near[0].reshape(8 * BLK, HD), nt, preferred_element_type=F32
        ) * scale
        sv = lax.dot_general(
            qh, vert[0].reshape(NV * BLK, HD), nt, preferred_element_type=F32
        ) * scale
        sn = jnp.where(allowed, sn, -jnp.inf)
        top = jnp.maximum(
            jnp.max(sn, axis=1, keepdims=True), jnp.max(sv, axis=1, keepdims=True)
        )
        en = jnp.exp(sn - top)
        ev = jnp.exp(sv - top)
        inv = 1.0 / (jnp.sum(en, axis=1, keepdims=True) + jnp.sum(ev, axis=1, keepdims=True))
        wn = (en * inv).astype(BF)
        wv = (ev * inv).astype(BF)
        o = jnp.dot(wn, near[1].reshape(8 * BLK, HD), preferred_element_type=F32)
        o = o + jnp.dot(wv, vert[1].reshape(NV * BLK, HD), preferred_element_type=F32)
        G[me, :, cols] = o.astype(BF)
        return 0

    def at(dy, dx):
        return lax.rem(y + dy + 4, 4) * 4 + lax.rem(x + dx + 4, 4)

    def part(src, half, rows):
        cols = pl.ds(half * HALF, HALF)
        if rows == 2:
            return G.at[src, :, cols]
        return G.at[src, pl.ds(rows * BLK, BLK), cols]

    sent = []

    def forward(dy, dx, half, rows, ty, tx):
        src, to = at(dy, dx), at(ty, tx)
        ref = part(src, half, rows)
        a = send(ref, ref, gs_sem.at[len(sent)], gr_sem.at[src, half, rows], seq=to)
        a.start()
        sent.append(a)

    def swap(half, a, b):
        return (a, b) if half == 0 else (b, a)

    def arrive(dy, dx, half):
        a, b = swap(half, dy, dx)
        split = a == 2 or (a == 0 and b == 2)
        src = at(dy, dx)
        for rows in ((0, 1) if split else (2,)):
            ref = part(src, half, rows)
            send(ref, ref, gs_sem.at[0], gr_sem.at[src, half, rows], seq=src).wait_recv()
        if a == 0 and b in (1, -1):
            forward(dy, dx, half, 0 if b == -1 else 1, *swap(half, 0, -b))
        if a == 0:
            forward(dy, dx, half, 2, *swap(half, 1, 0))
            forward(dy, dx, half, 2, *swap(half, -1, 0))
        elif a in (1, -1):
            forward(dy, dx, half, 0 if a == -1 else 1, *swap(half, -a, 0))

    def launch(half):
        for b in (1, -1):
            forward(0, 0, half, 2, *swap(half, 0, b))
        for a in (1, -1):
            forward(0, 0, half, 2, *swap(half, a, 0))

    lax.fori_loop(0, GROUP // 2, head, 0)
    launch(0)
    lax.fori_loop(GROUP // 2, GROUP, head, 0)
    launch(1)
    loads[4].wait()
    loads[5].wait()

    order = [(0, 0), (0, 1), (0, -1), (1, 0), (-1, 0), (0, 2), (2, 0), (1, 1), (1, -1), (-1, 1),
             (-1, -1), (1, 2), (-1, 2), (2, 1), (2, -1), (2, 2)]

    def sib_copy(g):
        return send(sib_s.at[g], sib_r.at[g], bs_sem.at[g], br_sem.at[g], exp=z * 2 + 1 - c)

    def z_copy(g, dz):
        to = lax.rem(z + dz, 4)
        return send(z_s.at[g, to], z_r.at[g, z], zs_sem.at[g, dz], zr_sem.at[g, z], exp=to * 2 + c)

    def z_arrive(g, dz):
        frm = lax.rem(z + dz, 4)
        send(z_s.at[g, frm], z_r.at[g, frm], zs_sem.at[g, dz], zr_sem.at[g, frm],
             exp=frm * 2 + c).wait_recv()
        return frm

    def p_copy(t):
        to = at(*order[t])
        return send(fin.at[t], proj.at[me], ps_sem.at[t], pr_sem.at[me], seq=to)

    def multiply(t):
        g, b = t // 4, t % 4
        P_[...] = jnp.dot(G[at(*order[t])], w[...], preferred_element_type=F32)
        for zz in range(4):
            keep[g, zz, b] = P_[pl.ds(pl.multiple_of((zz * 2 + c) * ROWS, ROWS), ROWS), :]
            sib_s[g, zz, b] = P_[
                pl.ds(pl.multiple_of((zz * 2 + 1 - c) * ROWS, ROWS), ROWS), :
            ].astype(BF)
        if b == 3:
            sib_copy(g).start()

    def pair(g):
        sib_copy(g).wait_recv()
        both = keep[g] + sib_r[g].astype(F32)
        keep[g] = both
        z_s[g] = both.astype(BF)
        for dz in (1, 3, 2):
            z_copy(g, dz).start()

    def finish(g):
        acc = keep[g, z]
        for dz in (1, 3, 2):
            frm = z_arrive(g, dz)
            acc = acc + z_r[g, frm].astype(F32)
        for b in range(4):
            t = 4 * g + b
            fin[t] = acc[b].astype(BF)
            if t > 0:
                p_copy(t).start()

    multiply(0)
    for dx in (1, -1):
        arrive(0, dx, 0)
        arrive(dx, 0, 1)
    for dx in (1, -1):
        arrive(0, dx, 1)
        arrive(dx, 0, 0)
    for t in (1, 2, 3, 4):
        multiply(t)
    arrive(0, 2, 0)
    arrive(2, 0, 1)
    pair(0)
    for dy in (1, -1):
        for dx in (1, -1):
            arrive(dy, dx, 0)
            arrive(dy, dx, 1)
    arrive(0, 2, 1)
    arrive(2, 0, 0)
    for t in (5, 6, 7):
        multiply(t)
    finish(0)
    for t in (8, 9, 10):
        multiply(t)
    pair(1)
    for s in (1, -1):
        arrive(s, 2, 0)
        arrive(2, s, 1)
    for s in (1, -1):
        arrive(s, 2, 1)
        arrive(2, s, 0)
    multiply(11)
    finish(1)
    for t in (12, 13, 14):
        multiply(t)
    pair(2)
    arrive(2, 2, 0)
    arrive(2, 2, 1)
    multiply(15)
    finish(2)
    pair(3)
    finish(3)

    proj[me] = fin[0]
    for s in range(1, SEQ):
        frm = lax.rem(me + s, SEQ)
        send(fin.at[0], proj.at[frm], ps_sem.at[0], pr_sem.at[frm], seq=frm).wait_recv()
    for s in range(SEQ):
        cols = slice(s * OC, s * OC + OC)
        out[:, cols] = res[:, cols].astype(F32) + proj[s].astype(F32)

    def done(d, _):
        piece(d).wait_send()
        share(d).wait_send()
        return 0

    lax.fori_loop(1, SEQ, done, 0)
    for a in sent:
        a.wait_send()
    for g in range(4):
        sib_copy(g).wait_send()
        for dz in (1, 2, 3):
            z_copy(g, dz).wait_send()
    for t in range(1, SEQ):
        p_copy(t).wait_send()


def front_of(queries, keys, values, cache_keys, cache_values, vertical, offsets, o_weight, residual):
    sel = pl.pallas_call(
        pick_kernel,
        out_shape=jax.ShapeDtypeStruct((2, NV, BLK, HD), BF),
        in_specs=[SM, HBM, HBM],
        out_specs=VM,
        scratch_shapes=[
            pltpu.VMEM((2, NV, BLK, HD), BF),
            pltpu.SemaphoreType.DMA((2, NV)),
        ],
        name="pick",
    )(vertical, cache_keys, cache_values)
    dma = pltpu.SemaphoreType.DMA
    return pl.pallas_call(
        front_kernel,
        out_shape=jax.ShapeDtypeStruct((ROWS, WIDTH), F32),
        in_specs=[SM, HBM, HBM, HBM, HBM, HBM, HBM],
        out_specs=VM,
        scratch_shapes=[
            pltpu.VMEM((2, NV, BLK, HD), BF),
            pltpu.VMEM((QLEN, DH), BF),
            pltpu.VMEM((2, 4, 2 * BLK, HD), BF),
            pltpu.VMEM((DH, OC), BF),
            pltpu.VMEM((ROWS, WIDTH), BF),
            pltpu.VMEM((2, NV, BLK, HD), BF),
            pltpu.VMEM((2, NV, BLK, HD), BF),
            pltpu.VMEM((SEQ, QLEN, DH), BF),
            pltpu.VMEM((QLEN, OC), F32),
            pltpu.VMEM((4, 4, 4, ROWS, OC), F32),
            pltpu.VMEM((4, 4, 4, ROWS, OC), BF),
            pltpu.VMEM((4, 4, 4, ROWS, OC), BF),
            pltpu.VMEM((4, 4, 4, ROWS, OC), BF),
            pltpu.VMEM((4, 4, 4, ROWS, OC), BF),
            pltpu.VMEM((SEQ, ROWS, OC), BF),
            pltpu.VMEM((SEQ, ROWS, OC), BF),
            dma((6,)),
            dma((SEQ,)), dma((SEQ,)), dma((SEQ,)), dma((SEQ,)),
            dma((4,)), dma((4,)),
            dma((40,)), dma((SEQ, 2, 3)),
            dma((4,)), dma((4,)),
            dma((4, 4)), dma((4, 4)),
            dma((SEQ,)), dma((SEQ,)),
        ],
        compiler_params=pltpu.CompilerParams(
            collective_id=0, has_side_effects=True, vmem_limit_bytes=62 * 2**20
        ),
        name="front",
    )(offsets, sel, queries, keys, values, o_weight, residual)


def shards(
    queries,
    keys,
    values,
    cache_keys,
    cache_values,
    vertical,
    offsets,
    o_weight,
    residual,
    norm_gain,
    expert_ids,
    gate_weights,
    w_gate,
    w_up,
    w_down,
):
    local_count = queries.shape[0]
    seq_count = lax.axis_size("seq")
    exp_count = lax.axis_size("exp")
    width = residual.shape[1]
    row_count = local_count // exp_count
    stream = front_of(
        queries, keys, values, cache_keys, cache_values, vertical, offsets, o_weight, residual
    )
    normed = (
        stream * lax.rsqrt(jnp.mean(stream * stream, axis=1, keepdims=True) + 1e-06) * norm_gain
    ).astype(jnp.bfloat16)
    top_count = expert_ids.shape[1]
    capacity = 2 * row_count * top_count // seq_count
    chosen = (
        expert_ids[:, :, None] == jnp.arange(seq_count, dtype=jnp.int32)[None, None, :]
    ).astype(jnp.int32)
    flat_chosen = chosen.reshape(row_count * top_count, seq_count)
    before = jnp.cumsum(flat_chosen, axis=0) - flat_chosen
    slots = jnp.sum(before * flat_chosen, axis=1).reshape(row_count, top_count)
    slot_marks = (
        slots[:, :, None, None] == jnp.arange(capacity, dtype=jnp.int32)[None, None, None, :]
    ).astype(jnp.int32)
    placed = chosen[:, :, :, None] * slot_marks
    routing = jnp.sum(placed, axis=1).transpose(1, 2, 0).astype(jnp.bfloat16)
    weighting = jnp.sum(
        placed.astype(jnp.float32) * gate_weights[:, :, None, None], axis=1
    ).transpose(1, 2, 0)
    gate_local = w_gate[0]
    up_local = w_up[0]
    down_local = w_down[0]
    outgoing = jnp.einsum(
        "ecr,rd->ecd", routing, normed, preferred_element_type=jnp.float32
    ).astype(jnp.bfloat16)
    arrived = lax.all_to_all(outgoing, "seq", split_axis=0, concat_axis=0, tiled=True)
    arrived = arrived.reshape(seq_count * capacity, width)
    piece = lax.all_gather(arrived, "exp", axis=0, tiled=True)
    gate = jnp.dot(piece, gate_local, preferred_element_type=jnp.float32)
    upward = jnp.dot(piece, up_local, preferred_element_type=jnp.float32)
    hidden = (jax.nn.silu(gate) * upward).astype(jnp.bfloat16)
    summed_out = lax.psum_scatter(
        jnp.dot(hidden, down_local, preferred_element_type=jnp.float32).astype(jnp.bfloat16),
        "exp",
        scatter_dimension=0,
        tiled=True,
    ).astype(jnp.float32)
    returned = lax.all_to_all(
        summed_out.reshape(seq_count, capacity, width).astype(jnp.bfloat16),
        "seq",
        split_axis=0,
        concat_axis=0,
        tiled=True,
    ).astype(jnp.float32)
    mixture = jnp.einsum("ecr,ecd->rd", weighting, returned, precision=lax.Precision.HIGHEST)
    return (stream + mixture).astype(jnp.bfloat16)


def solution(mesh):
    in_specs = (
        P("seq", "exp"),
        P("seq", "exp"),
        P("seq", "exp"),
        P("seq", "exp"),
        P("seq", "exp"),
        P("exp", None),
        P("exp", None),
        P("exp", "seq"),
        P(("seq", "exp"), None),
        P(),
        P(("seq", "exp"), None),
        P(("seq", "exp"), None),
        P("seq", None, "exp"),
        P("seq", None, "exp"),
        P("seq", "exp", None),
    )
    out_specs = P(("seq", "exp"), None)
    return jax.shard_map(shards, mesh=mesh, in_specs=in_specs, out_specs=out_specs, check_vma=False)
```

```python
import functools
import math

import jax
import jax.numpy as jnp
from jax import lax
from jax.experimental import pallas as pl
from jax.experimental.pallas import tpu as pltpu
from jax.sharding import PartitionSpec as P

HD = 128
BLK = 64
NV = 16
MAXOFF = 6
SEQ = 16
EXP = 8
GROUP = 12
ROWS = 16
QLEN = 128
DH = 1536
HALF = 768
OC = 384
WIDTH = 6144
MESH = pl.DeviceIdType.MESH
BF = jnp.bfloat16
F32 = jnp.float32
VM = pl.BlockSpec(memory_space=pltpu.VMEM)
SM = pl.BlockSpec(memory_space=pltpu.SMEM)
HBM = pl.BlockSpec(memory_space=pl.ANY)


def greet(axis, me, size):
    barrier = pltpu.get_barrier_semaphore()

    def one(d, _):
        pl.semaphore_signal(
            barrier, inc=1, device_id={axis: lax.rem(me + d, size)}, device_id_type=MESH
        )
        return 0

    lax.fori_loop(1, size, one, 0)


def send(src, dst, s, r, **where):
    return pltpu.make_async_remote_copy(
        src_ref=src, dst_ref=dst, send_sem=s, recv_sem=r, device_id=where, device_id_type=MESH
    )


def pick_kernel(vertical, ck, cv, out, raw, sem):
    me = lax.axis_index("seq")

    def copies(j):
        rows = pl.ds(pl.multiple_of(lax.rem(vertical[0, j], NV) * BLK, BLK), BLK)
        return [
            pltpu.make_async_copy(ref.at[rows, :], raw.at[i, j], sem.at[i, j])
            for i, ref in enumerate((ck, cv))
        ]

    for j in range(NV):
        for c in copies(j):
            c.start()
    for j in range(NV):
        listed = jnp.full((BLK, HD), vertical[0, j], jnp.int32)
        here = (listed >= me * NV) & (listed < me * NV + NV)
        for i, c in enumerate(copies(j)):
            c.wait()
            out[i, j] = jnp.where(here, raw[i, j].astype(F32), 0.0).astype(BF)


def front_kernel(
    offsets, sel_in, q_in, k_in, v_in, w_in, res_in, down_in, out, down,
    sel, q, near, w, res, got, vert, G, P_, keep, sib_s, sib_r, z_s, z_r, fin, proj,
    l_sem, s_sem, r_sem, s2_sem, r2_sem, sh_sem, rh_sem,
    gs_sem, gr_sem, bs_sem, br_sem, zs_sem, zr_sem, ps_sem, pr_sem, ws_sem, wr_sem,
):
    me = lax.axis_index("seq")
    e = lax.axis_index("exp")
    y, x = me // 4, lax.rem(me, 4)
    z, c = e // 2, lax.rem(e, 2)
    greet("seq", me, SEQ)
    greet("exp", e, EXP)

    loads = [
        pltpu.make_async_copy(a, b, l_sem.at[i])
        for i, (a, b) in enumerate(
            [(sel_in, sel), (k_in, near.at[0, 3]), (v_in, near.at[1, 3]), (q_in, q),
             (w_in, w), (res_in, res)]
        )
    ]
    for a in loads:
        a.start()
    for a in loads[:3]:
        a.wait()
    got[:, me] = sel[:, me]
    pl.semaphore_wait(pltpu.get_barrier_semaphore(), SEQ - 1 + EXP - 1)

    def w_copy(d):
        to = lax.rem(e + d, EXP)
        cols = pl.ds(pl.multiple_of(to * HALF, HALF), HALF)
        return send(down_in.at[0, :, cols], down.at[e], ws_sem.at[d], wr_sem.at[e], exp=to)

    def piece(d):
        to = lax.rem(me + d, SEQ)
        return send(sel.at[:, to], got.at[:, me], s_sem.at[d], r_sem.at[me], seq=to)

    def share(d):
        to = lax.rem(me + d, SEQ)
        return send(vert.at[:, me], vert.at[:, me], s2_sem.at[d], r2_sem.at[me], seq=to)

    def halo(d):
        to = lax.rem(me + d, SEQ)
        return send(near.at[:, 3], near.at[:, 3 - d], sh_sem.at[d], rh_sem.at[d], seq=to)

    def start_piece(d, _):
        piece(d).start()
        return 0

    def start_share(d, _):
        share(d).start()
        return 0

    def arrived_piece(d, _):
        frm = lax.rem(me + d, SEQ)
        send(sel.at[:, 0], got.at[:, frm], s_sem.at[0], r_sem.at[frm], seq=frm).wait_recv()
        return 0

    def arrived_share(d, _):
        frm = lax.rem(me + d, SEQ)
        send(vert.at[:, me], vert.at[:, frm], s2_sem.at[0], r2_sem.at[frm], seq=frm).wait_recv()
        return 0

    lax.fori_loop(1, SEQ, start_piece, 0)
    for d in (1, 2, 3):
        halo(d).start()
    for d in range(1, EXP):
        w_copy(d).start()
    w_own = pltpu.make_async_copy(
        down_in.at[0, :, pl.ds(pl.multiple_of(e * HALF, HALF), HALF)], down.at[e], ws_sem.at[0]
    )
    w_own.start()
    lax.fori_loop(1, SEQ, arrived_piece, 0)
    total = got[:, 0].astype(F32)
    for j in range(1, SEQ):
        total = total + got[:, j].astype(F32)
    vert[:, me] = total.astype(BF)
    lax.fori_loop(1, SEQ, start_share, 0)

    loads[3].wait()
    for d in (1, 2, 3):
        halo(d).wait()
    qi = lax.broadcasted_iota(jnp.int32, (2 * BLK, 8 * BLK), 0)
    ki = lax.broadcasted_iota(jnp.int32, (2 * BLK, 8 * BLK), 1)
    spacing = qi // BLK + MAXOFF - ki // BLK
    banded = spacing == offsets[0, 0]
    for t in range(1, 4):
        banded = banded | (spacing == offsets[0, t])
    banded = banded & (ki // BLK + 2 * me >= MAXOFF)
    allowed = banded | ((spacing == 0) & (lax.rem(ki, BLK) <= lax.rem(qi, BLK)))
    lax.fori_loop(1, SEQ, arrived_share, 0)

    scale = 1.0 / math.sqrt(HD)
    nt = (((1,), (1,)), ((), ()))

    def head(h, _):
        cols = pl.ds(pl.multiple_of(h * HD, HD), HD)
        qh = q[:, cols]
        sn = lax.dot_general(
            qh, near[0].reshape(8 * BLK, HD), nt, preferred_element_type=F32
        ) * scale
        sv = lax.dot_general(
            qh, vert[0].reshape(NV * BLK, HD), nt, preferred_element_type=F32
        ) * scale
        sn = jnp.where(allowed, sn, -jnp.inf)
        top = jnp.maximum(
            jnp.max(sn, axis=1, keepdims=True), jnp.max(sv, axis=1, keepdims=True)
        )
        en = jnp.exp(sn - top)
        ev = jnp.exp(sv - top)
        inv = 1.0 / (jnp.sum(en, axis=1, keepdims=True) + jnp.sum(ev, axis=1, keepdims=True))
        wn = (en * inv).astype(BF)
        wv = (ev * inv).astype(BF)
        o = jnp.dot(wn, near[1].reshape(8 * BLK, HD), preferred_element_type=F32)
        o = o + jnp.dot(wv, vert[1].reshape(NV * BLK, HD), preferred_element_type=F32)
        G[me, :, cols] = o.astype(BF)
        return 0

    def at(dy, dx):
        return lax.rem(y + dy + 4, 4) * 4 + lax.rem(x + dx + 4, 4)

    def part(src, half, rows):
        cols = pl.ds(half * HALF, HALF)
        if rows == 2:
            return G.at[src, :, cols]
        return G.at[src, pl.ds(rows * BLK, BLK), cols]

    sent = []

    def forward(dy, dx, half, rows, ty, tx):
        src, to = at(dy, dx), at(ty, tx)
        ref = part(src, half, rows)
        a = send(ref, ref, gs_sem.at[len(sent)], gr_sem.at[src, half, rows], seq=to)
        a.start()
        sent.append(a)

    def swap(half, a, b):
        return (a, b) if half == 0 else (b, a)

    def arrive(dy, dx, half):
        a, b = swap(half, dy, dx)
        split = a == 2 or (a == 0 and b == 2)
        src = at(dy, dx)
        for rows in ((0, 1) if split else (2,)):
            ref = part(src, half, rows)
            send(ref, ref, gs_sem.at[0], gr_sem.at[src, half, rows], seq=src).wait_recv()
        if a == 0 and b in (1, -1):
            forward(dy, dx, half, 0 if b == -1 else 1, *swap(half, 0, -b))
        if a == 0:
            forward(dy, dx, half, 2, *swap(half, 1, 0))
            forward(dy, dx, half, 2, *swap(half, -1, 0))
        elif a in (1, -1):
            forward(dy, dx, half, 0 if a == -1 else 1, *swap(half, -a, 0))

    def launch(half):
        for b in (1, -1):
            forward(0, 0, half, 2, *swap(half, 0, b))
        for a in (1, -1):
            forward(0, 0, half, 2, *swap(half, a, 0))

    lax.fori_loop(0, GROUP // 2, head, 0)
    launch(0)
    lax.fori_loop(GROUP // 2, GROUP, head, 0)
    launch(1)
    loads[4].wait()
    loads[5].wait()

    order = [(0, 0), (0, 1), (0, -1), (1, 0), (-1, 0), (0, 2), (2, 0), (1, 1), (1, -1), (-1, 1),
             (-1, -1), (1, 2), (-1, 2), (2, 1), (2, -1), (2, 2)]

    def sib_copy(g):
        return send(sib_s.at[g], sib_r.at[g], bs_sem.at[g], br_sem.at[g], exp=z * 2 + 1 - c)

    def z_copy(g, dz):
        to = lax.rem(z + dz, 4)
        return send(z_s.at[g, to], z_r.at[g, z], zs_sem.at[g, dz], zr_sem.at[g, z], exp=to * 2 + c)

    def z_arrive(g, dz):
        frm = lax.rem(z + dz, 4)
        send(z_s.at[g, frm], z_r.at[g, frm], zs_sem.at[g, dz], zr_sem.at[g, frm],
             exp=frm * 2 + c).wait_recv()
        return frm

    def p_copy(t):
        to = at(*order[t])
        return send(fin.at[t], proj.at[me], ps_sem.at[t], pr_sem.at[me], seq=to)

    def multiply(t):
        g, b = t // 4, t % 4
        P_[...] = jnp.dot(G[at(*order[t])], w[...], preferred_element_type=F32)
        for zz in range(4):
            keep[g, zz, b] = P_[pl.ds(pl.multiple_of((zz * 2 + c) * ROWS, ROWS), ROWS), :]
            sib_s[g, zz, b] = P_[
                pl.ds(pl.multiple_of((zz * 2 + 1 - c) * ROWS, ROWS), ROWS), :
            ].astype(BF)
        if b == 3:
            sib_copy(g).start()

    def pair(g):
        sib_copy(g).wait_recv()
        both = keep[g] + sib_r[g].astype(F32)
        keep[g] = both
        z_s[g] = both.astype(BF)
        for dz in (1, 3, 2):
            z_copy(g, dz).start()

    def finish(g):
        acc = keep[g, z]
        for dz in (1, 3, 2):
            frm = z_arrive(g, dz)
            acc = acc + z_r[g, frm].astype(F32)
        for b in range(4):
            t = 4 * g + b
            fin[t] = acc[b].astype(BF)
            if t > 0:
                p_copy(t).start()

    multiply(0)
    for dx in (1, -1):
        arrive(0, dx, 0)
        arrive(dx, 0, 1)
    for dx in (1, -1):
        arrive(0, dx, 1)
        arrive(dx, 0, 0)
    for t in (1, 2, 3, 4):
        multiply(t)
    arrive(0, 2, 0)
    arrive(2, 0, 1)
    pair(0)
    for dy in (1, -1):
        for dx in (1, -1):
            arrive(dy, dx, 0)
            arrive(dy, dx, 1)
    arrive(0, 2, 1)
    arrive(2, 0, 0)
    for t in (5, 6, 7):
        multiply(t)
    finish(0)
    for t in (8, 9, 10):
        multiply(t)
    pair(1)
    for s in (1, -1):
        arrive(s, 2, 0)
        arrive(2, s, 1)
    for s in (1, -1):
        arrive(s, 2, 1)
        arrive(2, s, 0)
    multiply(11)
    finish(1)
    for t in (12, 13, 14):
        multiply(t)
    pair(2)
    arrive(2, 2, 0)
    arrive(2, 2, 1)
    multiply(15)
    finish(2)
    pair(3)
    finish(3)

    proj[me] = fin[0]
    for s in range(1, SEQ):
        frm = lax.rem(me + s, SEQ)
        send(fin.at[0], proj.at[frm], ps_sem.at[0], pr_sem.at[frm], seq=frm).wait_recv()
    for s in range(SEQ):
        cols = slice(s * OC, s * OC + OC)
        out[:, cols] = res[:, cols].astype(F32) + proj[s].astype(F32)

    def done(d, _):
        piece(d).wait_send()
        share(d).wait_send()
        return 0

    lax.fori_loop(1, SEQ, done, 0)
    w_own.wait()
    for d in range(1, EXP):
        w_copy(d).wait_send()
        frm = lax.rem(e + d, EXP)
        send(down.at[frm], down.at[frm], ws_sem.at[0], wr_sem.at[frm], exp=frm).wait_recv()
    for a in sent:
        a.wait_send()
    for g in range(4):
        sib_copy(g).wait_send()
        for dz in (1, 2, 3):
            z_copy(g, dz).wait_send()
    for t in range(1, SEQ):
        p_copy(t).wait_send()


def front_of(
    queries, keys, values, cache_keys, cache_values, vertical, offsets, o_weight, residual, w_down
):
    sel = pl.pallas_call(
        pick_kernel,
        out_shape=jax.ShapeDtypeStruct((2, NV, BLK, HD), BF),
        in_specs=[SM, HBM, HBM],
        out_specs=VM,
        scratch_shapes=[
            pltpu.VMEM((2, NV, BLK, HD), BF),
            pltpu.SemaphoreType.DMA((2, NV)),
        ],
        name="pick",
    )(vertical, cache_keys, cache_values)
    dma = pltpu.SemaphoreType.DMA
    return pl.pallas_call(
        front_kernel,
        out_shape=(
            jax.ShapeDtypeStruct((ROWS, WIDTH), F32),
            jax.ShapeDtypeStruct((EXP, 320, HALF), BF),
        ),
        in_specs=[SM, HBM, HBM, HBM, HBM, HBM, HBM, HBM],
        out_specs=(VM, HBM),
        scratch_shapes=[
            pltpu.VMEM((2, NV, BLK, HD), BF),
            pltpu.VMEM((QLEN, DH), BF),
            pltpu.VMEM((2, 4, 2 * BLK, HD), BF),
            pltpu.VMEM((DH, OC), BF),
            pltpu.VMEM((ROWS, WIDTH), BF),
            pltpu.VMEM((2, NV, BLK, HD), BF),
            pltpu.VMEM((2, NV, BLK, HD), BF),
            pltpu.VMEM((SEQ, QLEN, DH), BF),
            pltpu.VMEM((QLEN, OC), F32),
            pltpu.VMEM((4, 4, 4, ROWS, OC), F32),
            pltpu.VMEM((4, 4, 4, ROWS, OC), BF),
            pltpu.VMEM((4, 4, 4, ROWS, OC), BF),
            pltpu.VMEM((4, 4, 4, ROWS, OC), BF),
            pltpu.VMEM((4, 4, 4, ROWS, OC), BF),
            pltpu.VMEM((SEQ, ROWS, OC), BF),
            pltpu.VMEM((SEQ, ROWS, OC), BF),
            dma((6,)),
            dma((SEQ,)), dma((SEQ,)), dma((SEQ,)), dma((SEQ,)),
            dma((4,)), dma((4,)),
            dma((40,)), dma((SEQ, 2, 3)),
            dma((4,)), dma((4,)),
            dma((4, 4)), dma((4, 4)),
            dma((SEQ,)), dma((SEQ,)),
            dma((EXP,)), dma((EXP,)),
        ],
        compiler_params=pltpu.CompilerParams(
            collective_id=0, has_side_effects=True, vmem_limit_bytes=62 * 2**20
        ),
        name="front",
    )(offsets, sel, queries, keys, values, o_weight, residual, w_down)


class Ring:
    def __init__(self, e, part, s_sem, r_sem):
        self.e, self.part, self.s_sem, self.r_sem = e, part, s_sem, r_sem
        self.z, self.c = e // 2, lax.rem(e, 2)
        self.sent = []

    def at(self, dz, dc=0):
        return lax.rem(self.z + dz + 4, 4) * 2 + (self.c if dc == 0 else 1 - self.c)

    def go(self, j, rows, to):
        ref = self.part(j, rows)
        a = send(ref, ref, self.s_sem(len(self.sent)), self.r_sem(j, rows), exp=to)
        a.start()
        self.sent.append(a)

    def wait(self, j, rows):
        ref = self.part(j, rows)
        send(ref, ref, self.s_sem(0), self.r_sem(j, rows), exp=self.at(0, 1)).wait_recv()

    def own(self):
        self.go(self.e, 2, self.at(1))
        self.go(self.e, 2, self.at(-1))
        self.go(self.e, 2, self.at(0, 1))

    def near(self):
        for dz in (-1, 1):
            j = self.at(dz)
            self.wait(j, 2)
            self.go(j, 0 if dz == -1 else 1, self.at(-dz))
            self.go(j, 2, self.at(0, 1))

    def far(self):
        j = self.at(2)
        self.wait(j, 0)
        self.wait(j, 1)
        self.go(j, 2, self.at(0, 1))

    def across(self):
        for dz in (0, 1, -1, 2):
            self.wait(self.at(dz, 1), 2)

    def done(self):
        for a in self.sent:
            a.wait_send()


def back_kernel(
    stream, gain, ids, gates, w_gate, w_up, w_down, out,
    wg, wu, wd, nst, outg, arr, X, accg, accu, H, dacc, O, Z, mats, mall, mix, F,
    l_sem, ds_sem, dr_sem, xs_sem, xr_sem, hs_sem, hr_sem, os_sem, or_sem, ms_sem, mr_sem,
    fs_sem, fr_sem,
):
    me = lax.axis_index("seq")
    e = lax.axis_index("exp")
    greet("seq", me, SEQ)
    greet("exp", e, EXP)
    loads = [
        pltpu.make_async_copy(a, b, l_sem.at[i])
        for i, (a, b) in enumerate([(w_gate.at[0], wg), (w_up.at[0], wu), (w_down, wd)])
    ]
    for a in loads:
        a.start()

    st = stream[...]
    root = lax.rsqrt(jnp.mean(st * st, axis=1, keepdims=True) + 1e-06)
    for q in range(4):
        for s in range(4):
            cols = slice(q * DH + s * OC, q * DH + s * OC + OC)
            nst[q, s * ROWS : (s + 1) * ROWS, :] = (stream[:, cols] * root * gain[:, cols]).astype(BF)

    ids_f = ids[...].astype(F32)
    first, second = ids_f[:, 0:1], ids_f[:, 1:2]

    def iota(shape, dim):
        return lax.broadcasted_iota(jnp.int32, shape, dim)

    def flag(mask):
        return jnp.where(mask, 1.0, 0.0).astype(F32)

    experts = iota((ROWS, SEQ), 1).astype(F32)
    hot0, hot1 = flag(experts == first), flag(experts == second)
    lower = flag(iota((ROWS, ROWS), 1) < iota((ROWS, ROWS), 0)).astype(BF)
    ones = jnp.ones((ROWS, ROWS), BF)
    before0 = jnp.dot(lower, hot0.astype(BF), preferred_element_type=F32)
    before1 = jnp.dot(lower, hot1.astype(BF), preferred_element_type=F32)
    before1 = before1 + jnp.dot(ones, hot0.astype(BF), preferred_element_type=F32)
    slot0 = jnp.sum(before0 * hot0, axis=1, keepdims=True)
    slot1 = jnp.sum(before1 * hot1, axis=1, keepdims=True)

    lanes = iota((4 * ROWS, 256), 1).astype(F32)
    quarter = (iota((4 * ROWS, 1), 0) // ROWS).astype(F32) * 4.0
    t0 = jnp.concatenate([first * 16.0 + slot0] * 4, axis=0) + quarter
    t1 = jnp.concatenate([second * 16.0 + slot1] * 4, axis=0) + quarter
    spread = flag((lanes == t0) | (lanes == t1)).astype(BF)

    place = ((e // 4) * 256 + lax.rem(e, 4) * 4).astype(F32)
    lanes = iota((ROWS, 512), 1).astype(F32)
    weigh = jnp.where(lanes == first * 16.0 + slot0 + place, gates[:, 0:1], 0.0)
    weigh = weigh + jnp.where(lanes == second * 16.0 + slot1 + place, gates[:, 1:2], 0.0)
    high = weigh.astype(BF)
    mats[0] = high
    mats[1] = (weigh - high.astype(F32)).astype(BF)
    mall[:, e] = mats[...]

    def d_copy(q, d):
        to = lax.rem(me + d, SEQ)
        return send(outg.at[q, to], arr.at[q, me], ds_sem.at[q, d], dr_sem.at[q, me], seq=to)

    def m_copy(d):
        to = lax.rem(e + d, EXP)
        return send(mats, mall.at[:, e], ms_sem.at[d], mr_sem.at[e], exp=to)

    pl.semaphore_wait(pltpu.get_barrier_semaphore(), SEQ - 1 + EXP - 1)
    for q in range(4):
        o = lax.dot_general(
            spread, nst[q], (((0,), (0,)), ((), ())), preferred_element_type=F32
        )
        outg[q] = o.astype(BF).reshape(SEQ, ROWS, OC)

        def start_d(d, _, q=q):
            d_copy(q, d).start()
            return 0

        lax.fori_loop(1, SEQ, start_d, 0)
        arr[q, me] = outg[q, me]
    for d in range(1, EXP):
        m_copy(d).start()

    pi, pj = iota((256, 256), 0), iota((256, 256), 1)
    sort = flag(
        (pi // 64 == lax.rem(pj, 16) // 4)
        & (lax.rem(pi, 64) // 4 == pj // 16)
        & (lax.rem(pi, 4) == lax.rem(pj, 4))
    ).astype(BF)

    def x_part(q):
        def part(j, rows):
            cols = pl.ds(q * DH, DH)
            if rows == 2:
                return X.at[j, :, cols]
            return X.at[j, pl.ds(rows * 32, 32), cols]

        return part

    rings = [
        Ring(e, x_part(q), lambda n, q=q: xs_sem.at[q, n], lambda j, r, q=q: xr_sem.at[q, j, r])
        for q in range(4)
    ]

    def begin(q):
        def arrived(d, _):
            frm = lax.rem(me + d, SEQ)
            send(outg.at[q, 0], arr.at[q, frm], ds_sem.at[q, 0], dr_sem.at[q, frm],
                 seq=frm).wait_recv()
            return 0

        lax.fori_loop(1, SEQ, arrived, 0)
        o = jnp.dot(sort, arr[q].reshape(256, OC), preferred_element_type=F32).astype(BF)
        for s in range(4):
            X[e, :, q * DH + s * OC : q * DH + s * OC + OC] = o[s * 64 : (s + 1) * 64]
        rings[q].own()

    def gate_up(q):
        rings[q].far()
        rings[q].across()
        if q == 0:
            loads[0].wait()
            loads[1].wait()
        rows = slice(q * DH, (q + 1) * DH)

        def some(m, _):
            xb = X[pl.ds(m * 4, 4), :, rows].reshape(256, DH)
            at = pl.ds(pl.multiple_of(m * 256, 256), 256)
            g = jnp.dot(xb, wg[rows, :], preferred_element_type=F32)
            u = jnp.dot(xb, wu[rows, :], preferred_element_type=F32)
            if q > 0:
                g = g + accg[at, :]
                u = u + accu[at, :]
            accg[at, :] = g
            accu[at, :] = u
            return 0

        lax.fori_loop(0, 2, some, 0)

    begin(0)
    begin(1)
    rings[0].near()
    begin(2)
    rings[1].near()
    gate_up(0)
    begin(3)
    rings[2].near()
    gate_up(1)
    rings[3].near()
    gate_up(2)
    gate_up(3)

    g = accg[...]
    hidden = (g / (1.0 + jnp.exp(-g)) * accu[...]).astype(BF)

    def h_part(r):
        def part(j, rows):
            if rows == 2:
                return H.at[j, pl.ds(r * 256, 256), :]
            return H.at[j, pl.ds(r * 256 + rows * 128, 128), :]

        return part

    h_rings = [
        Ring(e, h_part(r), lambda n, r=r: hs_sem.at[r, n], lambda j, s, r=r: hr_sem.at[r, j, s])
        for r in range(2)
    ]
    for r in range(2):
        pi, pj = iota((256, 512), 0), iota((256, 512), 1)
        turn = flag(
            (pj // 64 == r * 4 + lax.rem(pi, 16) // 4)
            & (lax.rem(pj, 64) // 4 == pi // 16)
            & (lax.rem(pj, 4) == lax.rem(pi, 4))
        ).astype(BF)
        H[e, r * 256 : (r + 1) * 256, :] = jnp.dot(
            turn, hidden, preferred_element_type=F32
        ).astype(BF)
        h_rings[r].own()
    loads[2].wait()

    def o_copy(r, d):
        to = lax.rem(me + d, SEQ)
        return send(O.at[r, to], Z.at[r, me], os_sem.at[r, d], or_sem.at[r, me], seq=to)

    for r in range(2):
        h_rings[r].near()
    for r in range(2):
        h_rings[r].far()
        h_rings[r].across()
        dacc[...] = jnp.zeros_like(dacc)

        def down(j, _, r=r):
            dacc[...] += jnp.dot(
                H[j, r * 256 : (r + 1) * 256, :], wd[j], preferred_element_type=F32
            )
            return 0

        lax.fori_loop(0, EXP, down, 0)
        O[r] = dacc[...].astype(BF).reshape(SEQ, ROWS, HALF)

        def start_o(d, _, r=r):
            o_copy(r, d).start()
            return 0

        lax.fori_loop(1, SEQ, start_o, 0)
        Z[r, me] = O[r, me]

    for d in range(1, EXP):
        frm = lax.rem(e + d, EXP)
        send(mats, mall.at[:, frm], ms_sem.at[0], mr_sem.at[frm], exp=frm).wait_recv()
    for r in range(2):
        def arrived_o(d, _, r=r):
            frm = lax.rem(me + d, SEQ)
            send(O.at[r, 0], Z.at[r, frm], os_sem.at[r, 0], or_sem.at[r, frm], seq=frm).wait_recv()
            return 0

        lax.fori_loop(1, SEQ, arrived_o, 0)
    m2 = jnp.dot(
        mall[...].reshape(256, 512), Z[...].reshape(512, HALF), preferred_element_type=F32
    )
    mix[...] = (m2[:128] + m2[128:]).astype(BF).reshape(EXP, ROWS, HALF)
    F[e] = mix[e]

    def f_copy(d):
        to = lax.rem(e + d, EXP)
        return send(mix.at[to], F.at[e], fs_sem.at[d], fr_sem.at[e], exp=to)

    for d in range(1, EXP):
        f_copy(d).start()
    for d in range(1, EXP):
        frm = lax.rem(e + d, EXP)
        send(mix.at[0], F.at[frm], fs_sem.at[0], fr_sem.at[frm], exp=frm).wait_recv()
    for j in range(EXP):
        cols = slice(j * HALF, (j + 1) * HALF)
        out[:, cols] = (stream[:, cols] + F[j].astype(F32)).astype(BF)

    def done(d, _):
        for q in range(4):
            d_copy(q, d).wait_send()
        for r in range(2):
            o_copy(r, d).wait_send()
        return 0

    lax.fori_loop(1, SEQ, done, 0)
    for ring in rings + h_rings:
        ring.done()
    for d in range(1, EXP):
        m_copy(d).wait_send()
        f_copy(d).wait_send()


def back_of(stream, norm_gain, expert_ids, gate_weights, w_gate, w_up, w_down):
    dma = pltpu.SemaphoreType.DMA
    return pl.pallas_call(
        back_kernel,
        out_shape=jax.ShapeDtypeStruct((ROWS, WIDTH), BF),
        in_specs=[VM, VM, VM, VM, HBM, HBM, HBM],
        out_specs=VM,
        scratch_shapes=[
            pltpu.VMEM((WIDTH, 320), BF),
            pltpu.VMEM((WIDTH, 320), BF),
            pltpu.VMEM((EXP, 320, HALF), BF),
            pltpu.VMEM((4, 64, OC), BF),
            pltpu.VMEM((4, SEQ, ROWS, OC), BF),
            pltpu.VMEM((4, SEQ, ROWS, OC), BF),
            pltpu.VMEM((EXP, 64, WIDTH), BF),
            pltpu.VMEM((512, 320), F32),
            pltpu.VMEM((512, 320), F32),
            pltpu.VMEM((EXP, 512, 320), BF),
            pltpu.VMEM((256, HALF), F32),
            pltpu.VMEM((2, SEQ, ROWS, HALF), BF),
            pltpu.VMEM((2, SEQ, ROWS, HALF), BF),
            pltpu.VMEM((2, ROWS, 512), BF),
            pltpu.VMEM((2, EXP, ROWS, 512), BF),
            pltpu.VMEM((EXP, ROWS, HALF), BF),
            pltpu.VMEM((EXP, ROWS, HALF), BF),
            dma((3,)),
            dma((4, SEQ)), dma((4, SEQ)),
            dma((4, 8)), dma((4, EXP, 3)),
            dma((2, 8)), dma((2, EXP, 3)),
            dma((2, SEQ)), dma((2, SEQ)),
            dma((EXP,)), dma((EXP,)),
            dma((EXP,)), dma((EXP,)),
        ],
        compiler_params=pltpu.CompilerParams(
            collective_id=1, has_side_effects=True, vmem_limit_bytes=62 * 2**20
        ),
        name="back",
    )(stream, norm_gain.reshape(1, WIDTH), expert_ids, gate_weights, w_gate, w_up, w_down)


def shards(
    queries,
    keys,
    values,
    cache_keys,
    cache_values,
    vertical,
    offsets,
    o_weight,
    residual,
    norm_gain,
    expert_ids,
    gate_weights,
    w_gate,
    w_up,
    w_down,
):
    stream, down = front_of(
        queries, keys, values, cache_keys, cache_values, vertical, offsets, o_weight, residual, w_down
    )
    return back_of(stream, norm_gain, expert_ids, gate_weights, w_gate, w_up, down)


def solution(mesh):
    in_specs = (
        P("seq", "exp"),
        P("seq", "exp"),
        P("seq", "exp"),
        P("seq", "exp"),
        P("seq", "exp"),
        P("exp", None),
        P("exp", None),
        P("exp", "seq"),
        P(("seq", "exp"), None),
        P(),
        P(("seq", "exp"), None),
        P(("seq", "exp"), None),
        P("seq", None, "exp"),
        P("seq", None, "exp"),
        P("seq", "exp", None),
    )
    out_specs = P(("seq", "exp"), None)
    return jax.shard_map(shards, mesh=mesh, in_specs=in_specs, out_specs=out_specs, check_vma=False)
```

```python
import functools
import math

import jax
import jax.numpy as jnp
from jax import lax
from jax.experimental import pallas as pl
from jax.experimental.pallas import tpu as pltpu
from jax.sharding import PartitionSpec as P

HD = 128
BLK = 64
NV = 16
MAXOFF = 6
SEQ = 16
EXP = 8
GROUP = 12
ROWS = 16
QLEN = 128
DH = 1536
HALF = 768
OC = 384
WIDTH = 6144
MESH = pl.DeviceIdType.MESH
BF = jnp.bfloat16
F32 = jnp.float32
VM = pl.BlockSpec(memory_space=pltpu.VMEM)
SM = pl.BlockSpec(memory_space=pltpu.SMEM)
HBM = pl.BlockSpec(memory_space=pl.ANY)


def greet(axis, me, size):
    barrier = pltpu.get_barrier_semaphore()

    def one(d, _):
        pl.semaphore_signal(
            barrier, inc=1, device_id={axis: lax.rem(me + d, size)}, device_id_type=MESH
        )
        return 0

    lax.fori_loop(1, size, one, 0)


def send(src, dst, s, r, **where):
    return pltpu.make_async_remote_copy(
        src_ref=src, dst_ref=dst, send_sem=s, recv_sem=r, device_id=where, device_id_type=MESH
    )


def pick_kernel(vertical, ck, cv, out, raw, sem):
    me = lax.axis_index("seq")

    def copies(j):
        rows = pl.ds(pl.multiple_of(lax.rem(vertical[0, j], NV) * BLK, BLK), BLK)
        return [
            pltpu.make_async_copy(ref.at[rows, :], raw.at[i, j], sem.at[i, j])
            for i, ref in enumerate((ck, cv))
        ]

    for j in range(NV):
        for c in copies(j):
            c.start()
    for j in range(NV):
        listed = jnp.full((BLK, HD), vertical[0, j], jnp.int32)
        here = (listed >= me * NV) & (listed < me * NV + NV)
        for i, c in enumerate(copies(j)):
            c.wait()
            out[i, j] = jnp.where(here, raw[i, j].astype(F32), 0.0).astype(BF)


def front_kernel(
    offsets, sel_in, q_in, k_in, v_in, w_in, res_in, down_in, out, down,
    sel, q, near, w, res, got, vert, G, P_, keep, sib_s, sib_r, z_s, z_r, fin, proj,
    l_sem, s_sem, r_sem, s2_sem, r2_sem, sh_sem, rh_sem,
    gs_sem, gr_sem, bs_sem, br_sem, zs_sem, zr_sem, ps_sem, pr_sem, ws_sem, wr_sem,
):
    me = lax.axis_index("seq")
    e = lax.axis_index("exp")
    y, x = me // 4, lax.rem(me, 4)
    z, c = e // 2, lax.rem(e, 2)
    greet("seq", me, SEQ)
    greet("exp", e, EXP)

    loads = [
        pltpu.make_async_copy(a, b, l_sem.at[i])
        for i, (a, b) in enumerate(
            [(sel_in, sel), (k_in, near.at[0, 3]), (v_in, near.at[1, 3]), (q_in, q),
             (w_in, w), (res_in, res)]
        )
    ]
    for a in loads:
        a.start()
    for a in loads[:3]:
        a.wait()
    got[:, me] = sel[:, me]
    pl.semaphore_wait(pltpu.get_barrier_semaphore(), SEQ - 1 + EXP - 1)

    def w_copy(d):
        to = lax.rem(e + d, EXP)
        cols = pl.ds(pl.multiple_of(to * HALF, HALF), HALF)
        return send(down_in.at[0, :, cols], down.at[e], ws_sem.at[d], wr_sem.at[e], exp=to)

    def piece(d):
        to = lax.rem(me + d, SEQ)
        return send(sel.at[:, to], got.at[:, me], s_sem.at[d], r_sem.at[me], seq=to)

    def share(d):
        to = lax.rem(me + d, SEQ)
        return send(vert.at[:, me], vert.at[:, me], s2_sem.at[d], r2_sem.at[me], seq=to)

    def halo(d):
        to = lax.rem(me + d, SEQ)
        return send(near.at[:, 3], near.at[:, 3 - d], sh_sem.at[d], rh_sem.at[d], seq=to)

    def start_piece(d, _):
        piece(d).start()
        return 0

    def start_share(d, _):
        share(d).start()
        return 0

    def arrived_piece(d, _):
        frm = lax.rem(me + d, SEQ)
        send(sel.at[:, 0], got.at[:, frm], s_sem.at[0], r_sem.at[frm], seq=frm).wait_recv()
        return 0

    def arrived_share(d, _):
        frm = lax.rem(me + d, SEQ)
        send(vert.at[:, me], vert.at[:, frm], s2_sem.at[0], r2_sem.at[frm], seq=frm).wait_recv()
        return 0

    lax.fori_loop(1, SEQ, start_piece, 0)
    for d in (1, 2, 3):
        halo(d).start()
    for d in range(1, EXP):
        w_copy(d).start()
    w_own = pltpu.make_async_copy(
        down_in.at[0, :, pl.ds(pl.multiple_of(e * HALF, HALF), HALF)], down.at[e], ws_sem.at[0]
    )
    w_own.start()
    lax.fori_loop(1, SEQ, arrived_piece, 0)
    total = got[:, 0].astype(F32)
    for j in range(1, SEQ):
        total = total + got[:, j].astype(F32)
    vert[:, me] = total.astype(BF)
    lax.fori_loop(1, SEQ, start_share, 0)

    loads[3].wait()
    for d in (1, 2, 3):
        halo(d).wait()
    qi = lax.broadcasted_iota(jnp.int32, (2 * BLK, 8 * BLK), 0)
    ki = lax.broadcasted_iota(jnp.int32, (2 * BLK, 8 * BLK), 1)
    spacing = qi // BLK + MAXOFF - ki // BLK
    banded = spacing == offsets[0, 0]
    for t in range(1, 4):
        banded = banded | (spacing == offsets[0, t])
    banded = banded & (ki // BLK + 2 * me >= MAXOFF)
    allowed = banded | ((spacing == 0) & (lax.rem(ki, BLK) <= lax.rem(qi, BLK)))
    lax.fori_loop(1, SEQ, arrived_share, 0)

    scale = 1.0 / math.sqrt(HD)
    nt = (((1,), (1,)), ((), ()))

    def head(h, _):
        cols = pl.ds(pl.multiple_of(h * HD, HD), HD)
        qh = q[:, cols]
        sn = lax.dot_general(
            qh, near[0].reshape(8 * BLK, HD), nt, preferred_element_type=F32
        ) * scale
        sv = lax.dot_general(
            qh, vert[0].reshape(NV * BLK, HD), nt, preferred_element_type=F32
        ) * scale
        sn = jnp.where(allowed, sn, -jnp.inf)
        top = jnp.maximum(
            jnp.max(sn, axis=1, keepdims=True), jnp.max(sv, axis=1, keepdims=True)
        )
        en = jnp.exp(sn - top)
        ev = jnp.exp(sv - top)
        inv = 1.0 / (jnp.sum(en, axis=1, keepdims=True) + jnp.sum(ev, axis=1, keepdims=True))
        wn = (en * inv).astype(BF)
        wv = (ev * inv).astype(BF)
        o = jnp.dot(wn, near[1].reshape(8 * BLK, HD), preferred_element_type=F32)
        o = o + jnp.dot(wv, vert[1].reshape(NV * BLK, HD), preferred_element_type=F32)
        G[me, :, cols] = o.astype(BF)
        return 0

    def at(dy, dx):
        return lax.rem(y + dy + 4, 4) * 4 + lax.rem(x + dx + 4, 4)

    def part(src, half, rows):
        cols = pl.ds(half * HALF, HALF)
        if rows == 2:
            return G.at[src, :, cols]
        return G.at[src, pl.ds(rows * BLK, BLK), cols]

    sent = []

    def forward(dy, dx, half, rows, ty, tx):
        src, to = at(dy, dx), at(ty, tx)
        ref = part(src, half, rows)
        a = send(ref, ref, gs_sem.at[len(sent)], gr_sem.at[src, half, rows], seq=to)
        a.start()
        sent.append(a)

    def swap(half, a, b):
        return (a, b) if half == 0 else (b, a)

    def arrive(dy, dx, half):
        a, b = swap(half, dy, dx)
        split = a == 2 or (a == 0 and b == 2)
        src = at(dy, dx)
        for rows in ((0, 1) if split else (2,)):
            ref = part(src, half, rows)
            send(ref, ref, gs_sem.at[0], gr_sem.at[src, half, rows], seq=src).wait_recv()
        if a == 0 and b in (1, -1):
            forward(dy, dx, half, 0 if b == -1 else 1, *swap(half, 0, -b))
        if a == 0:
            forward(dy, dx, half, 2, *swap(half, 1, 0))
            forward(dy, dx, half, 2, *swap(half, -1, 0))
        elif a in (1, -1):
            forward(dy, dx, half, 0 if a == -1 else 1, *swap(half, -a, 0))

    def launch(half):
        for b in (1, -1):
            forward(0, 0, half, 2, *swap(half, 0, b))
        for a in (1, -1):
            forward(0, 0, half, 2, *swap(half, a, 0))

    lax.fori_loop(0, GROUP // 2, head, 0)
    launch(0)
    lax.fori_loop(GROUP // 2, GROUP, head, 0)
    launch(1)
    loads[4].wait()
    loads[5].wait()

    order = [(0, 0), (0, 1), (0, -1), (1, 0), (-1, 0), (0, 2), (2, 0), (1, 1), (1, -1), (-1, 1),
             (-1, -1), (1, 2), (-1, 2), (2, 1), (2, -1), (2, 2)]

    def sib_copy(g):
        return send(sib_s.at[g], sib_r.at[g], bs_sem.at[g], br_sem.at[g], exp=z * 2 + 1 - c)

    def z_copy(g, dz):
        to = lax.rem(z + dz, 4)
        return send(z_s.at[g, to], z_r.at[g, z], zs_sem.at[g, dz], zr_sem.at[g, z], exp=to * 2 + c)

    def z_arrive(g, dz):
        frm = lax.rem(z + dz, 4)
        send(z_s.at[g, frm], z_r.at[g, frm], zs_sem.at[g, dz], zr_sem.at[g, frm],
             exp=frm * 2 + c).wait_recv()
        return frm

    def p_copy(t):
        to = at(*order[t])
        return send(fin.at[t], proj.at[me], ps_sem.at[t], pr_sem.at[me], seq=to)

    def multiply(t):
        g, b = t // 4, t % 4
        P_[...] = jnp.dot(G[at(*order[t])], w[...], preferred_element_type=F32)
        for zz in range(4):
            keep[g, zz, b] = P_[pl.ds(pl.multiple_of((zz * 2 + c) * ROWS, ROWS), ROWS), :]
            sib_s[g, zz, b] = P_[
                pl.ds(pl.multiple_of((zz * 2 + 1 - c) * ROWS, ROWS), ROWS), :
            ].astype(BF)
        if b == 3:
            sib_copy(g).start()

    def pair(g):
        sib_copy(g).wait_recv()
        both = keep[g] + sib_r[g].astype(F32)
        keep[g] = both
        z_s[g] = both.astype(BF)
        for dz in (1, 3, 2):
            z_copy(g, dz).start()

    def finish(g):
        acc = keep[g, z]
        for dz in (1, 3, 2):
            frm = z_arrive(g, dz)
            acc = acc + z_r[g, frm].astype(F32)
        for b in range(4):
            t = 4 * g + b
            fin[t] = acc[b].astype(BF)
            if t > 0:
                p_copy(t).start()

    multiply(0)
    for dx in (1, -1):
        arrive(0, dx, 0)
        arrive(dx, 0, 1)
    for dx in (1, -1):
        arrive(0, dx, 1)
        arrive(dx, 0, 0)
    for t in (1, 2, 3, 4):
        multiply(t)
    arrive(0, 2, 0)
    arrive(2, 0, 1)
    pair(0)
    for dy in (1, -1):
        for dx in (1, -1):
            arrive(dy, dx, 0)
            arrive(dy, dx, 1)
    arrive(0, 2, 1)
    arrive(2, 0, 0)
    for t in (5, 6, 7):
        multiply(t)
    finish(0)
    for t in (8, 9, 10):
        multiply(t)
    pair(1)
    for s in (1, -1):
        arrive(s, 2, 0)
        arrive(2, s, 1)
    for s in (1, -1):
        arrive(s, 2, 1)
        arrive(2, s, 0)
    multiply(11)
    finish(1)
    for t in (12, 13, 14):
        multiply(t)
    pair(2)
    arrive(2, 2, 0)
    arrive(2, 2, 1)
    multiply(15)
    finish(2)
    pair(3)
    finish(3)

    proj[me] = fin[0]
    for s in range(1, SEQ):
        frm = lax.rem(me + s, SEQ)
        send(fin.at[0], proj.at[frm], ps_sem.at[0], pr_sem.at[frm], seq=frm).wait_recv()
    for s in range(SEQ):
        cols = slice(s * OC, s * OC + OC)
        out[:, cols] = res[:, cols].astype(F32) + proj[s].astype(F32)

    def done(d, _):
        piece(d).wait_send()
        share(d).wait_send()
        return 0

    lax.fori_loop(1, SEQ, done, 0)
    w_own.wait()
    for d in range(1, EXP):
        w_copy(d).wait_send()
        frm = lax.rem(e + d, EXP)
        send(down.at[frm], down.at[frm], ws_sem.at[0], wr_sem.at[frm], exp=frm).wait_recv()
    for a in sent:
        a.wait_send()
    for g in range(4):
        sib_copy(g).wait_send()
        for dz in (1, 2, 3):
            z_copy(g, dz).wait_send()
    for t in range(1, SEQ):
        p_copy(t).wait_send()


def front_of(
    queries, keys, values, cache_keys, cache_values, vertical, offsets, o_weight, residual, w_down
):
    sel = pl.pallas_call(
        pick_kernel,
        out_shape=jax.ShapeDtypeStruct((2, NV, BLK, HD), BF),
        in_specs=[SM, HBM, HBM],
        out_specs=VM,
        scratch_shapes=[
            pltpu.VMEM((2, NV, BLK, HD), BF),
            pltpu.SemaphoreType.DMA((2, NV)),
        ],
        name="pick",
    )(vertical, cache_keys, cache_values)
    dma = pltpu.SemaphoreType.DMA
    return pl.pallas_call(
        front_kernel,
        out_shape=(
            jax.ShapeDtypeStruct((ROWS, WIDTH), F32),
            jax.ShapeDtypeStruct((EXP, 320, HALF), BF),
        ),
        in_specs=[SM, HBM, HBM, HBM, HBM, HBM, HBM, HBM],
        out_specs=(VM, HBM),
        scratch_shapes=[
            pltpu.VMEM((2, NV, BLK, HD), BF),
            pltpu.VMEM((QLEN, DH), BF),
            pltpu.VMEM((2, 4, 2 * BLK, HD), BF),
            pltpu.VMEM((DH, OC), BF),
            pltpu.VMEM((ROWS, WIDTH), BF),
            pltpu.VMEM((2, NV, BLK, HD), BF),
            pltpu.VMEM((2, NV, BLK, HD), BF),
            pltpu.VMEM((SEQ, QLEN, DH), BF),
            pltpu.VMEM((QLEN, OC), F32),
            pltpu.VMEM((4, 4, 4, ROWS, OC), F32),
            pltpu.VMEM((4, 4, 4, ROWS, OC), BF),
            pltpu.VMEM((4, 4, 4, ROWS, OC), BF),
            pltpu.VMEM((4, 4, 4, ROWS, OC), BF),
            pltpu.VMEM((4, 4, 4, ROWS, OC), BF),
            pltpu.VMEM((SEQ, ROWS, OC), BF),
            pltpu.VMEM((SEQ, ROWS, OC), BF),
            dma((6,)),
            dma((SEQ,)), dma((SEQ,)), dma((SEQ,)), dma((SEQ,)),
            dma((4,)), dma((4,)),
            dma((40,)), dma((SEQ, 2, 3)),
            dma((4,)), dma((4,)),
            dma((4, 4)), dma((4, 4)),
            dma((SEQ,)), dma((SEQ,)),
            dma((EXP,)), dma((EXP,)),
        ],
        compiler_params=pltpu.CompilerParams(
            collective_id=0, has_side_effects=True, vmem_limit_bytes=62 * 2**20
        ),
        name="front",
    )(offsets, sel, queries, keys, values, o_weight, residual, w_down)


class Ring:
    def __init__(self, e, part, s_sem, r_sem):
        self.e, self.part, self.s_sem, self.r_sem = e, part, s_sem, r_sem
        self.z, self.c = e // 2, lax.rem(e, 2)
        self.sent = []

    def at(self, dz, dc=0):
        return lax.rem(self.z + dz + 4, 4) * 2 + (self.c if dc == 0 else 1 - self.c)

    def go(self, j, rows, to):
        ref = self.part(j, rows)
        a = send(ref, ref, self.s_sem(len(self.sent)), self.r_sem(j, rows), exp=to)
        a.start()
        self.sent.append(a)

    def wait(self, j, rows):
        ref = self.part(j, rows)
        send(ref, ref, self.s_sem(0), self.r_sem(j, rows), exp=self.at(0, 1)).wait_recv()

    def own(self):
        self.go(self.e, 2, self.at(1))
        self.go(self.e, 2, self.at(-1))
        self.go(self.e, 2, self.at(0, 1))

    def near(self):
        for dz in (-1, 1):
            j = self.at(dz)
            self.wait(j, 2)
            self.go(j, 0 if dz == -1 else 1, self.at(-dz))
            self.go(j, 2, self.at(0, 1))

    def far(self):
        j = self.at(2)
        self.wait(j, 0)
        self.wait(j, 1)
        self.go(j, 2, self.at(0, 1))

    def across(self):
        for dz in (0, 1, -1, 2):
            self.wait(self.at(dz, 1), 2)

    def done(self):
        for a in self.sent:
            a.wait_send()


def back_kernel(
    stream, gain, ids, gates, w_gate, w_up, w_down, out,
    wt, wd, nst, outg, arr, X, acc, H, dacc, O, Z, mats, mall, mix, F,
    l_sem, ds_sem, dr_sem, xs_sem, xr_sem, hs_sem, hr_sem, os_sem, or_sem, ms_sem, mr_sem,
    fs_sem, fr_sem,
):
    me = lax.axis_index("seq")
    e = lax.axis_index("exp")
    greet("seq", me, SEQ)
    greet("exp", e, EXP)
    loads = [
        pltpu.make_async_copy(a, b, l_sem.at[i])
        for i, (a, b) in enumerate(
            [
                (w_gate.at[0, :256], wt.at[:256]),
                (w_up.at[0, :256], wt.at[256:512]),
                (w_gate.at[0, 256:], wt.at[512:576]),
                (w_up.at[0, 256:], wt.at[576:]),
                (w_down, wd),
            ]
        )
    ]
    for a in loads:
        a.start()

    st = stream[...]
    root = lax.rsqrt(jnp.mean(st * st, axis=1, keepdims=True) + 1e-06)
    for q in range(4):
        for s in range(4):
            cols = slice(q * DH + s * OC, q * DH + s * OC + OC)
            nst[q, s * ROWS : (s + 1) * ROWS, :] = (stream[:, cols] * root * gain[:, cols]).astype(BF)

    def iota(shape, dim):
        return lax.broadcasted_iota(jnp.int32, shape, dim)

    def flag(mask):
        return jnp.where(mask, 1.0, 0.0).astype(F32)

    def column(row):
        same = iota((ROWS, ROWS), 0) == iota((ROWS, ROWS), 1)
        return jnp.sum(jnp.where(same, row.astype(F32), 0.0), axis=1, keepdims=True)

    first, second = column(ids[0:1, :]), column(ids[1:2, :])
    gate0, gate1 = column(gates[0:1, :]), column(gates[1:2, :])

    experts = iota((ROWS, SEQ), 1).astype(F32)
    hot0, hot1 = flag(experts == first), flag(experts == second)
    lower = flag(iota((ROWS, ROWS), 1) < iota((ROWS, ROWS), 0)).astype(BF)
    ones = jnp.ones((ROWS, ROWS), BF)
    before0 = jnp.dot(lower, hot0.astype(BF), preferred_element_type=F32)
    before1 = jnp.dot(lower, hot1.astype(BF), preferred_element_type=F32)
    before1 = before1 + jnp.dot(ones, hot0.astype(BF), preferred_element_type=F32)
    slot0 = jnp.sum(before0 * hot0, axis=1, keepdims=True)
    slot1 = jnp.sum(before1 * hot1, axis=1, keepdims=True)

    lanes = iota((4 * ROWS, 256), 1).astype(F32)
    quarter = (iota((4 * ROWS, 1), 0) // ROWS).astype(F32) * 4.0
    t0 = jnp.concatenate([first * 16.0 + slot0] * 4, axis=0) + quarter
    t1 = jnp.concatenate([second * 16.0 + slot1] * 4, axis=0) + quarter
    spread = flag((lanes == t0) | (lanes == t1)).astype(BF)

    place = ((e // 4) * 256 + lax.rem(e, 4) * 4).astype(F32)
    lanes = iota((ROWS, 512), 1).astype(F32)
    weigh = jnp.where(lanes == first * 16.0 + slot0 + place, gate0, 0.0)
    weigh = weigh + jnp.where(lanes == second * 16.0 + slot1 + place, gate1, 0.0)
    high = weigh.astype(BF)
    mats[0] = high
    mats[1] = (weigh - high.astype(F32)).astype(BF)
    mall[:, e] = mats[...]

    def d_copy(q, d):
        to = lax.rem(me + d, SEQ)
        return send(outg.at[q, to], arr.at[q, me], ds_sem.at[q, d], dr_sem.at[q, me], seq=to)

    def m_copy(d):
        to = lax.rem(e + d, EXP)
        return send(mats, mall.at[:, e], ms_sem.at[d], mr_sem.at[e], exp=to)

    pl.semaphore_wait(pltpu.get_barrier_semaphore(), SEQ - 1 + EXP - 1)
    for q in range(4):
        o = lax.dot_general(
            spread, nst[q], (((0,), (0,)), ((), ())), preferred_element_type=F32
        )
        outg[q] = o.astype(BF).reshape(SEQ, ROWS, OC)

        def start_d(d, _, q=q):
            d_copy(q, d).start()
            return 0

        lax.fori_loop(1, SEQ, start_d, 0)
        arr[q, me] = outg[q, me]
    for d in range(1, EXP):
        m_copy(d).start()

    pi, pj = iota((256, 256), 0), iota((256, 256), 1)
    sort = flag(
        (pi // 64 == lax.rem(pj, 16) // 4)
        & (lax.rem(pi, 64) // 4 == pj // 16)
        & (lax.rem(pi, 4) == lax.rem(pj, 4))
    ).astype(BF)

    def x_part(q):
        def part(j, rows):
            cols = pl.ds(q * DH, DH)
            if rows == 2:
                return X.at[j, :, cols]
            return X.at[j, pl.ds(rows * 32, 32), cols]

        return part

    rings = [
        Ring(e, x_part(q), lambda n, q=q: xs_sem.at[q, n], lambda j, r, q=q: xr_sem.at[q, j, r])
        for q in range(4)
    ]

    def begin(q):
        def arrived(d, _):
            frm = lax.rem(me + d, SEQ)
            send(outg.at[q, 0], arr.at[q, frm], ds_sem.at[q, 0], dr_sem.at[q, frm],
                 seq=frm).wait_recv()
            return 0

        lax.fori_loop(1, SEQ, arrived, 0)
        o = jnp.dot(sort, arr[q].reshape(256, OC), preferred_element_type=F32).astype(BF)
        for s in range(4):
            X[e, :, q * DH + s * OC : q * DH + s * OC + OC] = o[s * 64 : (s + 1) * 64]
        rings[q].own()

    def gate_up(q):
        rings[q].far()
        rings[q].across()
        if q == 0:
            for a in loads[:4]:
                a.wait()
        rows = slice(q * DH, (q + 1) * DH)

        def some(m, _):
            xb = X[pl.ds(m * 4, 4), :, rows].reshape(256, DH)
            at = pl.ds(pl.multiple_of(m * 256, 256), 256)
            o = lax.dot_general(
                xb, wt[:, rows], (((1,), (1,)), ((), ())), preferred_element_type=F32
            )
            if q > 0:
                o = o + acc[at, :]
            acc[at, :] = o
            return 0

        lax.fori_loop(0, 2, some, 0)

    begin(0)
    begin(1)
    rings[0].near()
    begin(2)
    rings[1].near()
    gate_up(0)
    begin(3)
    rings[2].near()
    gate_up(1)
    rings[3].near()
    gate_up(2)
    gate_up(3)

    def gated(g, u):
        return (g / (1.0 + jnp.exp(-g)) * u).astype(BF)

    hidden = gated(acc[:, :256], acc[:, 256:512])
    rest = gated(acc[:, 512:576], acc[:, 576:])

    def h_part(r):
        def part(j, rows):
            if rows == 2:
                return H.at[j, pl.ds(r * 256, 256), :]
            return H.at[j, pl.ds(r * 256 + rows * 128, 128), :]

        return part

    h_rings = [
        Ring(e, h_part(r), lambda n, r=r: hs_sem.at[r, n], lambda j, s, r=r: hr_sem.at[r, j, s])
        for r in range(2)
    ]
    for r in range(2):
        pi, pj = iota((256, 512), 0), iota((256, 512), 1)
        turn = flag(
            (pj // 64 == r * 4 + lax.rem(pi, 16) // 4)
            & (lax.rem(pj, 64) // 4 == pi // 16)
            & (lax.rem(pj, 4) == lax.rem(pi, 4))
        ).astype(BF)
        for cols, part in ((slice(0, 256), hidden), (slice(256, 320), rest)):
            H[e, r * 256 : (r + 1) * 256, cols] = jnp.dot(
                turn, part, preferred_element_type=F32
            ).astype(BF)
        h_rings[r].own()
    loads[4].wait()

    def o_copy(r, d):
        to = lax.rem(me + d, SEQ)
        return send(O.at[r, to], Z.at[r, me], os_sem.at[r, d], or_sem.at[r, me], seq=to)

    for r in range(2):
        h_rings[r].near()
    for r in range(2):
        h_rings[r].far()
        h_rings[r].across()
        dacc[...] = jnp.zeros_like(dacc)

        def down(j, _, r=r):
            dacc[...] += jnp.dot(
                H[j, r * 256 : (r + 1) * 256, :], wd[j], preferred_element_type=F32
            )
            return 0

        lax.fori_loop(0, EXP, down, 0)
        O[r] = dacc[...].astype(BF).reshape(SEQ, ROWS, HALF)

        def start_o(d, _, r=r):
            o_copy(r, d).start()
            return 0

        lax.fori_loop(1, SEQ, start_o, 0)
        Z[r, me] = O[r, me]

    for d in range(1, EXP):
        frm = lax.rem(e + d, EXP)
        send(mats, mall.at[:, frm], ms_sem.at[0], mr_sem.at[frm], exp=frm).wait_recv()
    for r in range(2):
        def arrived_o(d, _, r=r):
            frm = lax.rem(me + d, SEQ)
            send(O.at[r, 0], Z.at[r, frm], os_sem.at[r, 0], or_sem.at[r, frm], seq=frm).wait_recv()
            return 0

        lax.fori_loop(1, SEQ, arrived_o, 0)
    m2 = jnp.dot(
        mall[...].reshape(256, 512), Z[...].reshape(512, HALF), preferred_element_type=F32
    )
    mix[...] = (m2[:128] + m2[128:]).astype(BF).reshape(EXP, ROWS, HALF)
    F[e] = mix[e]

    def f_copy(d):
        to = lax.rem(e + d, EXP)
        return send(mix.at[to], F.at[e], fs_sem.at[d], fr_sem.at[e], exp=to)

    for d in range(1, EXP):
        f_copy(d).start()
    for d in range(1, EXP):
        frm = lax.rem(e + d, EXP)
        send(mix.at[0], F.at[frm], fs_sem.at[0], fr_sem.at[frm], exp=frm).wait_recv()
    for j in range(EXP):
        cols = slice(j * HALF, (j + 1) * HALF)
        out[:, cols] = (stream[:, cols] + F[j].astype(F32)).astype(BF)

    def done(d, _):
        for q in range(4):
            d_copy(q, d).wait_send()
        for r in range(2):
            o_copy(r, d).wait_send()
        return 0

    lax.fori_loop(1, SEQ, done, 0)
    for ring in rings + h_rings:
        ring.done()
    for d in range(1, EXP):
        m_copy(d).wait_send()
        f_copy(d).wait_send()


def back_of(stream, norm_gain, expert_ids, gate_weights, w_gate, w_up, w_down):
    dma = pltpu.SemaphoreType.DMA
    return pl.pallas_call(
        back_kernel,
        out_shape=jax.ShapeDtypeStruct((ROWS, WIDTH), BF),
        in_specs=[VM, VM, VM, VM, HBM, HBM, HBM],
        out_specs=VM,
        scratch_shapes=[
            pltpu.VMEM((640, WIDTH), BF),
            pltpu.VMEM((EXP, 320, HALF), BF),
            pltpu.VMEM((4, 64, OC), BF),
            pltpu.VMEM((4, SEQ, ROWS, OC), BF),
            pltpu.VMEM((4, SEQ, ROWS, OC), BF),
            pltpu.VMEM((EXP, 64, WIDTH), BF),
            pltpu.VMEM((512, 640), F32),
            pltpu.VMEM((EXP, 512, 320), BF),
            pltpu.VMEM((256, HALF), F32),
            pltpu.VMEM((2, SEQ, ROWS, HALF), BF),
            pltpu.VMEM((2, SEQ, ROWS, HALF), BF),
            pltpu.VMEM((2, ROWS, 512), BF),
            pltpu.VMEM((2, EXP, ROWS, 512), BF),
            pltpu.VMEM((EXP, ROWS, HALF), BF),
            pltpu.VMEM((EXP, ROWS, HALF), BF),
            dma((5,)),
            dma((4, SEQ)), dma((4, SEQ)),
            dma((4, 8)), dma((4, EXP, 3)),
            dma((2, 8)), dma((2, EXP, 3)),
            dma((2, SEQ)), dma((2, SEQ)),
            dma((EXP,)), dma((EXP,)),
            dma((EXP,)), dma((EXP,)),
        ],
        compiler_params=pltpu.CompilerParams(
            collective_id=1, has_side_effects=True, vmem_limit_bytes=62 * 2**20
        ),
        name="back",
    )(
        stream,
        norm_gain.reshape(1, WIDTH),
        expert_ids.T,
        gate_weights.T,
        w_gate.transpose(0, 2, 1),
        w_up.transpose(0, 2, 1),
        w_down,
    )


def shards(
    queries,
    keys,
    values,
    cache_keys,
    cache_values,
    vertical,
    offsets,
    o_weight,
    residual,
    norm_gain,
    expert_ids,
    gate_weights,
    w_gate,
    w_up,
    w_down,
):
    stream, down = front_of(
        queries, keys, values, cache_keys, cache_values, vertical, offsets, o_weight, residual, w_down
    )
    return back_of(stream, norm_gain, expert_ids, gate_weights, w_gate, w_up, down)


def solution(mesh):
    in_specs = (
        P("seq", "exp"),
        P("seq", "exp"),
        P("seq", "exp"),
        P("seq", "exp"),
        P("seq", "exp"),
        P("exp", None),
        P("exp", None),
        P("exp", "seq"),
        P(("seq", "exp"), None),
        P(),
        P(("seq", "exp"), None),
        P(("seq", "exp"), None),
        P("seq", None, "exp"),
        P("seq", None, "exp"),
        P("seq", "exp", None),
    )
    out_specs = P(("seq", "exp"), None)
    return jax.shard_map(shards, mesh=mesh, in_specs=in_specs, out_specs=out_specs, check_vma=False)
```

```python
import functools
import math

import jax
import jax.numpy as jnp
from jax import lax
from jax.experimental import pallas as pl
from jax.experimental.pallas import tpu as pltpu
from jax.sharding import PartitionSpec as P

HD = 128
BLK = 64
NV = 16
MAXOFF = 6
SEQ = 16
EXP = 8
GROUP = 12
ROWS = 16
QLEN = 128
DH = 1536
HALF = 768
OC = 384
WIDTH = 6144
MESH = pl.DeviceIdType.MESH
BF = jnp.bfloat16
F32 = jnp.float32
VM = pl.BlockSpec(memory_space=pltpu.VMEM)
SM = pl.BlockSpec(memory_space=pltpu.SMEM)
HBM = pl.BlockSpec(memory_space=pl.ANY)


def greet(axis, me, size):
    barrier = pltpu.get_barrier_semaphore()

    def one(d, _):
        pl.semaphore_signal(
            barrier, inc=1, device_id={axis: lax.rem(me + d, size)}, device_id_type=MESH
        )
        return 0

    lax.fori_loop(1, size, one, 0)


def send(src, dst, s, r, **where):
    return pltpu.make_async_remote_copy(
        src_ref=src, dst_ref=dst, send_sem=s, recv_sem=r, device_id=where, device_id_type=MESH
    )


class Ring:
    def __init__(self, e, part, s_sem, r_sem):
        self.e, self.part, self.s_sem, self.r_sem = e, part, s_sem, r_sem
        self.z, self.c = e // 2, lax.rem(e, 2)
        self.sent = []

    def at(self, dz, dc=0):
        return lax.rem(self.z + dz + 4, 4) * 2 + (self.c if dc == 0 else 1 - self.c)

    def go(self, j, rows, to):
        ref = self.part(j, rows)
        a = send(ref, ref, self.s_sem(len(self.sent)), self.r_sem(j, rows), exp=to)
        a.start()
        self.sent.append(a)

    def wait(self, j, rows):
        ref = self.part(j, rows)
        send(ref, ref, self.s_sem(0), self.r_sem(j, rows), exp=self.at(0, 1)).wait_recv()

    def own(self):
        self.go(self.e, 2, self.at(1))
        self.go(self.e, 2, self.at(-1))
        self.go(self.e, 2, self.at(0, 1))

    def near(self):
        for dz in (-1, 1):
            j = self.at(dz)
            self.wait(j, 2)
            self.go(j, 0 if dz == -1 else 1, self.at(-dz))
            self.go(j, 2, self.at(0, 1))

    def far(self):
        j = self.at(2)
        self.wait(j, 0)
        self.wait(j, 1)
        self.go(j, 2, self.at(0, 1))

    def across(self):
        for dz in (0, 1, -1, 2):
            self.wait(self.at(dz, 1), 2)

    def done(self):
        for a in self.sent:
            a.wait_send()


def layer_kernel(
    vertical, offsets, ck_in, cv_in, q_in, k_in, v_in, w_in, res_in, gain, ids, gates, w_gate, w_up,
    w_down, out,
    ck, cv, sel, q, near, w, res, got, vert, G, P_, keep, sib_s, sib_r, z_s, z_r, fin, proj, stream,
    wt, wd, nst, outg, arr, X, acc, H, O, Z, mats, mall, mix, F, turn,
    l_sem, s_sem, r_sem, s2_sem, r2_sem, sh_sem, rh_sem,
    gs_sem, gr_sem, bs_sem, br_sem, zs_sem, zr_sem, ps_sem, pr_sem, ws_sem, wr_sem,
    ds_sem, dr_sem, xs_sem, xr_sem, hs_sem, hr_sem, os_sem, or_sem, ms_sem, mr_sem,
    fs_sem, fr_sem,
):
    me = lax.axis_index("seq")
    e = lax.axis_index("exp")
    y, x = me // 4, lax.rem(me, 4)
    z, c = e // 2, lax.rem(e, 2)
    def iota(shape, dim):
        return lax.broadcasted_iota(jnp.int32, shape, dim)

    def flag(mask):
        return jnp.where(mask, 1.0, 0.0).astype(F32)

    greet("seq", me, SEQ)
    greet("exp", e, EXP)

    loads = [
        pltpu.make_async_copy(a, b, l_sem.at[i])
        for i, (a, b) in enumerate(
            [(ck_in, ck), (cv_in, cv), (k_in, near.at[0, 3]), (v_in, near.at[1, 3]), (q_in, q),
             (w_in, w), (res_in, res), (w_gate.at[0], wt.at[:320]), (w_up.at[0], wt.at[320:])]
        )
    ]
    for a in loads:
        a.start()
    loads[0].wait()
    loads[1].wait()
    apart = iota((BLK, NV * BLK), 1) - iota((BLK, NV * BLK), 0)
    for j in range(NV):
        mark = flag(apart == (vertical[0, j] - me * NV) * BLK).astype(BF)
        sel[0, j] = jnp.dot(mark, ck[...], preferred_element_type=F32).astype(BF)
        sel[1, j] = jnp.dot(mark, cv[...], preferred_element_type=F32).astype(BF)
    got[:, me] = sel[:, me]
    loads[2].wait()
    loads[3].wait()
    pl.semaphore_wait(pltpu.get_barrier_semaphore(), SEQ - 1 + EXP - 1)

    def w_copy(d):
        to = lax.rem(e + d, EXP)
        cols = pl.ds(pl.multiple_of(to * HALF, HALF), HALF)
        return send(w_down.at[0, :, cols], wd.at[e], ws_sem.at[d], wr_sem.at[e], exp=to)

    def piece(d):
        to = lax.rem(me + d, SEQ)
        return send(sel.at[:, to], got.at[:, me], s_sem.at[d], r_sem.at[me], seq=to)

    def share(d):
        to = lax.rem(me + d, SEQ)
        return send(vert.at[:, me], vert.at[:, me], s2_sem.at[d], r2_sem.at[me], seq=to)

    def halo(d):
        to = lax.rem(me + d, SEQ)
        return send(near.at[:, 3], near.at[:, 3 - d], sh_sem.at[d], rh_sem.at[d], seq=to)

    def start_piece(d, _):
        piece(d).start()
        return 0

    def start_share(d, _):
        share(d).start()
        return 0

    def arrived_piece(d, _):
        frm = lax.rem(me + d, SEQ)
        send(sel.at[:, 0], got.at[:, frm], s_sem.at[0], r_sem.at[frm], seq=frm).wait_recv()
        return 0

    def arrived_share(d, _):
        frm = lax.rem(me + d, SEQ)
        send(vert.at[:, me], vert.at[:, frm], s2_sem.at[0], r2_sem.at[frm], seq=frm).wait_recv()
        return 0

    lax.fori_loop(1, SEQ, start_piece, 0)
    for d in (1, 2, 3):
        halo(d).start()
    for d in range(1, EXP):
        w_copy(d).start()
    w_own = pltpu.make_async_copy(
        w_down.at[0, :, pl.ds(pl.multiple_of(e * HALF, HALF), HALF)], wd.at[e], ws_sem.at[0]
    )
    w_own.start()
    def column(row):
        same = iota((ROWS, ROWS), 0) == iota((ROWS, ROWS), 1)
        return jnp.sum(jnp.where(same, row.astype(F32), 0.0), axis=1, keepdims=True)

    first, second = column(ids[0:1, :]), column(ids[1:2, :])
    gate0, gate1 = column(gates[0:1, :]), column(gates[1:2, :])

    experts = iota((ROWS, SEQ), 1).astype(F32)
    hot0, hot1 = flag(experts == first), flag(experts == second)
    lower = flag(iota((ROWS, ROWS), 1) < iota((ROWS, ROWS), 0)).astype(BF)
    ones = jnp.ones((ROWS, ROWS), BF)
    before0 = jnp.dot(lower, hot0.astype(BF), preferred_element_type=F32)
    before1 = jnp.dot(lower, hot1.astype(BF), preferred_element_type=F32)
    before1 = before1 + jnp.dot(ones, hot0.astype(BF), preferred_element_type=F32)
    slot0 = jnp.sum(before0 * hot0, axis=1, keepdims=True)
    slot1 = jnp.sum(before1 * hot1, axis=1, keepdims=True)

    lanes = iota((4 * ROWS, 256), 1).astype(F32)
    quarter = (iota((4 * ROWS, 1), 0) >> 4).astype(F32) * 4.0
    t0 = jnp.concatenate([first * 16.0 + slot0] * 4, axis=0) + quarter
    t1 = jnp.concatenate([second * 16.0 + slot1] * 4, axis=0) + quarter
    spread = flag((lanes == t0) | (lanes == t1)).astype(BF)

    place = ((e // 4) * 256 + lax.rem(e, 4) * 4).astype(F32)
    lanes = iota((ROWS, 512), 1).astype(F32)
    weigh = jnp.where(lanes == first * 16.0 + slot0 + place, gate0, 0.0)
    weigh = weigh + jnp.where(lanes == second * 16.0 + slot1 + place, gate1, 0.0)
    high = weigh.astype(BF)
    mats[0] = high
    mats[1] = (weigh - high.astype(F32)).astype(BF)
    mall[:, e] = mats[...]

    def m_copy(d):
        to = lax.rem(e + d, EXP)
        return send(mats, mall.at[:, e], ms_sem.at[d], mr_sem.at[e], exp=to)

    for d in range(1, EXP):
        m_copy(d).start()

    pi, pj = iota((256, 256), 0), iota((256, 256), 1)
    sort = flag(
        ((pi >> 6) == ((pj & 15) >> 2)) & (((pi & 63) >> 2) == (pj >> 4)) & ((pi & 3) == (pj & 3))
    ).astype(BF)
    turn[...] = flag(
        ((pi >> 4) == ((pj & 63) >> 2)) & (((pi & 15) >> 2) == (pj >> 6)) & ((pi & 3) == (pj & 3))
    ).astype(BF)

    lax.fori_loop(1, SEQ, arrived_piece, 0)
    total = got[:, 0].astype(F32)
    for j in range(1, SEQ):
        total = total + got[:, j].astype(F32)
    vert[:, me] = total.astype(BF)
    lax.fori_loop(1, SEQ, start_share, 0)

    loads[4].wait()
    for d in (1, 2, 3):
        halo(d).wait()
    qi = lax.broadcasted_iota(jnp.int32, (2 * BLK, 8 * BLK), 0)
    ki = lax.broadcasted_iota(jnp.int32, (2 * BLK, 8 * BLK), 1)
    spacing = (qi >> 6) + MAXOFF - (ki >> 6)
    banded = spacing == offsets[0, 0]
    for t in range(1, 4):
        banded = banded | (spacing == offsets[0, t])
    banded = banded & ((ki >> 6) + 2 * me >= MAXOFF)
    allowed = banded | ((spacing == 0) & ((ki & 63) <= (qi & 63)))
    lax.fori_loop(1, SEQ, arrived_share, 0)

    scale = 1.0 / math.sqrt(HD)
    nt = (((1,), (1,)), ((), ()))

    def head(h, _):
        cols = pl.ds(pl.multiple_of(h * HD, HD), HD)
        qh = q[:, cols]
        sn = lax.dot_general(
            qh, near[0].reshape(8 * BLK, HD), nt, preferred_element_type=F32
        ) * scale
        sv = lax.dot_general(
            qh, vert[0].reshape(NV * BLK, HD), nt, preferred_element_type=F32
        ) * scale
        sn = jnp.where(allowed, sn, -jnp.inf)
        top = jnp.maximum(
            jnp.max(sn, axis=1, keepdims=True), jnp.max(sv, axis=1, keepdims=True)
        )
        en = jnp.exp(sn - top)
        ev = jnp.exp(sv - top)
        inv = 1.0 / (jnp.sum(en, axis=1, keepdims=True) + jnp.sum(ev, axis=1, keepdims=True))
        wn = (en * inv).astype(BF)
        wv = (ev * inv).astype(BF)
        o = jnp.dot(wn, near[1].reshape(8 * BLK, HD), preferred_element_type=F32)
        o = o + jnp.dot(wv, vert[1].reshape(NV * BLK, HD), preferred_element_type=F32)
        G[me, :, cols] = o.astype(BF)
        return 0

    def at(dy, dx):
        return lax.rem(y + dy + 4, 4) * 4 + lax.rem(x + dx + 4, 4)

    def part(src, half, rows):
        cols = pl.ds(half * HALF, HALF)
        if rows == 2:
            return G.at[src, :, cols]
        return G.at[src, pl.ds(rows * BLK, BLK), cols]

    sent = []

    def forward(dy, dx, half, rows, ty, tx):
        src, to = at(dy, dx), at(ty, tx)
        ref = part(src, half, rows)
        a = send(ref, ref, gs_sem.at[len(sent)], gr_sem.at[src, half, rows], seq=to)
        a.start()
        sent.append(a)

    def swap(half, a, b):
        return (a, b) if half == 0 else (b, a)

    def arrive(dy, dx, half):
        a, b = swap(half, dy, dx)
        split = a == 2 or (a == 0 and b == 2)
        src = at(dy, dx)
        for rows in ((0, 1) if split else (2,)):
            ref = part(src, half, rows)
            send(ref, ref, gs_sem.at[0], gr_sem.at[src, half, rows], seq=src).wait_recv()
        if a == 0 and b in (1, -1):
            forward(dy, dx, half, 0 if b == -1 else 1, *swap(half, 0, -b))
        if a == 0:
            forward(dy, dx, half, 2, *swap(half, 1, 0))
            forward(dy, dx, half, 2, *swap(half, -1, 0))
        elif a in (1, -1):
            forward(dy, dx, half, 0 if a == -1 else 1, *swap(half, -a, 0))

    def launch(half):
        for b in (1, -1):
            forward(0, 0, half, 2, *swap(half, 0, b))
        for a in (1, -1):
            forward(0, 0, half, 2, *swap(half, a, 0))

    lax.fori_loop(0, GROUP // 2, head, 0)
    launch(0)
    lax.fori_loop(GROUP // 2, GROUP, head, 0)
    launch(1)
    loads[5].wait()
    loads[6].wait()

    order = [(0, 0), (0, 1), (0, -1), (1, 0), (-1, 0), (0, 2), (2, 0), (1, 1), (1, -1), (-1, 1),
             (-1, -1), (1, 2), (-1, 2), (2, 1), (2, -1), (2, 2)]

    def sib_copy(g):
        return send(sib_s.at[g], sib_r.at[g], bs_sem.at[g], br_sem.at[g], exp=z * 2 + 1 - c)

    def z_copy(g, dz):
        to = lax.rem(z + dz, 4)
        return send(z_s.at[g, to], z_r.at[g, z], zs_sem.at[g, dz], zr_sem.at[g, z], exp=to * 2 + c)

    def z_arrive(g, dz):
        frm = lax.rem(z + dz, 4)
        send(z_s.at[g, frm], z_r.at[g, frm], zs_sem.at[g, dz], zr_sem.at[g, frm],
             exp=frm * 2 + c).wait_recv()
        return frm

    def p_copy(t):
        to = at(*order[t])
        return send(fin.at[t], proj.at[me], ps_sem.at[t], pr_sem.at[me], seq=to)

    def multiply(t):
        g, b = t // 4, t % 4
        P_[...] = jnp.dot(G[at(*order[t])], w[...], preferred_element_type=F32)
        for zz in range(4):
            keep[g, zz, b] = P_[pl.ds(pl.multiple_of((zz * 2 + c) * ROWS, ROWS), ROWS), :]
            sib_s[g, zz, b] = P_[
                pl.ds(pl.multiple_of((zz * 2 + 1 - c) * ROWS, ROWS), ROWS), :
            ].astype(BF)
        if b == 3:
            sib_copy(g).start()

    def pair(g):
        sib_copy(g).wait_recv()
        both = keep[g] + sib_r[g].astype(F32)
        keep[g] = both
        z_s[g] = both.astype(BF)
        for dz in (1, 3, 2):
            z_copy(g, dz).start()

    def finish(g):
        acc = keep[g, z]
        for dz in (1, 3, 2):
            frm = z_arrive(g, dz)
            acc = acc + z_r[g, frm].astype(F32)
        for b in range(4):
            t = 4 * g + b
            fin[t] = acc[b].astype(BF)
            if t > 0:
                p_copy(t).start()

    multiply(0)
    for dx in (1, -1):
        arrive(0, dx, 0)
        arrive(dx, 0, 1)
    for dx in (1, -1):
        arrive(0, dx, 1)
        arrive(dx, 0, 0)
    for t in (1, 2, 3, 4):
        multiply(t)
    arrive(0, 2, 0)
    arrive(2, 0, 1)
    pair(0)
    for dy in (1, -1):
        for dx in (1, -1):
            arrive(dy, dx, 0)
            arrive(dy, dx, 1)
    arrive(0, 2, 1)
    arrive(2, 0, 0)
    for t in (5, 6, 7):
        multiply(t)
    finish(0)
    for t in (8, 9, 10):
        multiply(t)
    pair(1)
    for s in (1, -1):
        arrive(s, 2, 0)
        arrive(2, s, 1)
    for s in (1, -1):
        arrive(s, 2, 1)
        arrive(2, s, 0)
    multiply(11)
    finish(1)
    for t in (12, 13, 14):
        multiply(t)
    pair(2)
    arrive(2, 2, 0)
    arrive(2, 2, 1)
    multiply(15)
    finish(2)
    pair(3)
    finish(3)

    proj[me] = fin[0]
    for s in range(1, SEQ):
        frm = lax.rem(me + s, SEQ)
        send(fin.at[0], proj.at[frm], ps_sem.at[0], pr_sem.at[frm], seq=frm).wait_recv()
    for s in range(SEQ):
        cols = slice(s * OC, s * OC + OC)
        stream[:, cols] = res[:, cols].astype(F32) + proj[s].astype(F32)

    st = stream[...]
    root = lax.rsqrt(jnp.mean(st * st, axis=1, keepdims=True) + 1e-06)
    for q in range(4):
        for s in range(4):
            cols = slice(q * DH + s * OC, q * DH + s * OC + OC)
            nst[q, s * ROWS : (s + 1) * ROWS, :] = (stream[:, cols] * root * gain[:, cols]).astype(BF)

    def d_copy(q, d):
        to = lax.rem(me + d, SEQ)
        return send(outg.at[q, to], arr.at[q, me], ds_sem.at[q, d], dr_sem.at[q, me], seq=to)


    for q in range(4):
        o = lax.dot_general(
            spread, nst[q], (((0,), (0,)), ((), ())), preferred_element_type=F32
        )
        outg[q] = o.astype(BF).reshape(SEQ, ROWS, OC)

        def start_d(d, _, q=q):
            d_copy(q, d).start()
            return 0

        lax.fori_loop(1, SEQ, start_d, 0)
        arr[q, me] = outg[q, me]

    def x_part(q):
        def part(j, rows):
            cols = pl.ds(q * DH, DH)
            if rows == 2:
                return X.at[j, :, cols]
            return X.at[j, pl.ds(rows * 32, 32), cols]

        return part

    rings = [
        Ring(e, x_part(q), lambda n, q=q: xs_sem.at[q, n], lambda j, r, q=q: xr_sem.at[q, j, r])
        for q in range(4)
    ]

    def begin(q):
        def arrived(d, _):
            frm = lax.rem(me + d, SEQ)
            send(outg.at[q, 0], arr.at[q, frm], ds_sem.at[q, 0], dr_sem.at[q, frm],
                 seq=frm).wait_recv()
            return 0

        lax.fori_loop(1, SEQ, arrived, 0)
        o = jnp.dot(sort, arr[q].reshape(256, OC), preferred_element_type=F32).astype(BF)
        for s in range(4):
            X[e, :, q * DH + s * OC : q * DH + s * OC + OC] = o[s * 64 : (s + 1) * 64]
        rings[q].own()

    def gate_up(q):
        rings[q].far()
        rings[q].across()
        if q == 0:
            loads[7].wait()
            loads[8].wait()
        cols = slice(q * DH, (q + 1) * DH)

        def some(m, _):
            xb = X[pl.ds(m * 4, 4), :, cols].reshape(256, DH)
            o = lax.dot_general(wt[:, cols], xb, nt, preferred_element_type=F32)
            if q > 0:
                o = o + acc[m]
            acc[m] = o
            return 0

        lax.fori_loop(0, 2, some, 0)

    begin(0)
    begin(1)
    rings[0].near()
    begin(2)
    rings[1].near()
    gate_up(0)
    begin(3)
    rings[2].near()
    gate_up(1)
    rings[3].near()
    gate_up(2)
    gate_up(3)

    def h_part(r):
        def part(j, rows):
            if rows == 2:
                return H.at[r, pl.ds(j * 320, 320), :]
            return H.at[r, pl.ds(j * 320 + rows * 160, 160), :]

        return part

    h_rings = [
        Ring(e, h_part(r), lambda n, r=r: hs_sem.at[r, n], lambda j, s, r=r: hr_sem.at[r, j, s])
        for r in range(2)
    ]
    for r in range(2):
        g, u = acc[r, :320], acc[r, 320:]
        hidden = (g / (1.0 + jnp.exp(-g)) * u).astype(BF)
        H[r, pl.ds(pl.multiple_of(e * 320, 64), 320), :] = lax.dot_general(
            hidden, turn[...], nt, preferred_element_type=F32
        ).astype(BF)
        h_rings[r].own()
    w_own.wait()
    for d in range(1, EXP):
        frm = lax.rem(e + d, EXP)
        send(wd.at[frm], wd.at[frm], ws_sem.at[0], wr_sem.at[frm], exp=frm).wait_recv()

    def o_copy(r, d):
        to = lax.rem(me + d, SEQ)
        return send(O.at[r, to], Z.at[r, me], os_sem.at[r, d], or_sem.at[r, me], seq=to)

    for r in range(2):
        h_rings[r].near()
    for r in range(2):
        h_rings[r].far()
        h_rings[r].across()
        o = lax.dot_general(
            H[r], wd[...].reshape(EXP * 320, HALF), (((0,), (0,)), ((), ())),
            preferred_element_type=F32,
        )
        O[r] = o.astype(BF).reshape(SEQ, ROWS, HALF)

        def start_o(d, _, r=r):
            o_copy(r, d).start()
            return 0

        lax.fori_loop(1, SEQ, start_o, 0)
        Z[r, me] = O[r, me]

    for d in range(1, EXP):
        frm = lax.rem(e + d, EXP)
        send(mats, mall.at[:, frm], ms_sem.at[0], mr_sem.at[frm], exp=frm).wait_recv()
    for r in range(2):
        def arrived_o(d, _, r=r):
            frm = lax.rem(me + d, SEQ)
            send(O.at[r, 0], Z.at[r, frm], os_sem.at[r, 0], or_sem.at[r, frm], seq=frm).wait_recv()
            return 0

        lax.fori_loop(1, SEQ, arrived_o, 0)
    m2 = jnp.dot(
        mall[...].reshape(256, 512), Z[...].reshape(512, HALF), preferred_element_type=F32
    )
    mix[...] = (m2[:128] + m2[128:]).astype(BF).reshape(EXP, ROWS, HALF)
    F[e] = mix[e]

    def f_copy(d):
        to = lax.rem(e + d, EXP)
        return send(mix.at[to], F.at[e], fs_sem.at[d], fr_sem.at[e], exp=to)

    for d in range(1, EXP):
        f_copy(d).start()
    for d in range(1, EXP):
        frm = lax.rem(e + d, EXP)
        send(mix.at[0], F.at[frm], fs_sem.at[0], fr_sem.at[frm], exp=frm).wait_recv()
    for j in range(EXP):
        cols = slice(j * HALF, (j + 1) * HALF)
        out[:, cols] = (stream[:, cols] + F[j].astype(F32)).astype(BF)

    def done_front(d, _):
        piece(d).wait_send()
        share(d).wait_send()
        return 0

    lax.fori_loop(1, SEQ, done_front, 0)
    for d in range(1, EXP):
        w_copy(d).wait_send()
    for a in sent:
        a.wait_send()
    for g in range(4):
        sib_copy(g).wait_send()
        for dz in (1, 2, 3):
            z_copy(g, dz).wait_send()
    for t in range(1, SEQ):
        p_copy(t).wait_send()


    def done(d, _):
        for q in range(4):
            d_copy(q, d).wait_send()
        for r in range(2):
            o_copy(r, d).wait_send()
        return 0

    lax.fori_loop(1, SEQ, done, 0)
    for ring in rings + h_rings:
        ring.done()
    for d in range(1, EXP):
        m_copy(d).wait_send()
        f_copy(d).wait_send()


def layer_of(
    queries, keys, values, cache_keys, cache_values, vertical, offsets, o_weight, residual,
    norm_gain, expert_ids, gate_weights, w_gate, w_up, w_down,
):
    dma = pltpu.SemaphoreType.DMA
    vm = pltpu.VMEM
    return pl.pallas_call(
        layer_kernel,
        out_shape=jax.ShapeDtypeStruct((ROWS, WIDTH), BF),
        in_specs=[SM, SM] + [HBM] * 7 + [VM] * 3 + [HBM] * 3,
        out_specs=VM,
        scratch_shapes=[
            vm((NV * BLK, HD), BF),
            vm((NV * BLK, HD), BF),
            vm((2, NV, BLK, HD), BF),
            vm((QLEN, DH), BF),
            vm((2, 4, 2 * BLK, HD), BF),
            vm((DH, OC), BF),
            vm((ROWS, WIDTH), BF),
            vm((2, NV, BLK, HD), BF),
            vm((2, NV, BLK, HD), BF),
            vm((SEQ, QLEN, DH), BF),
            vm((QLEN, OC), F32),
            vm((4, 4, 4, ROWS, OC), F32),
            vm((4, 4, 4, ROWS, OC), BF),
            vm((4, 4, 4, ROWS, OC), BF),
            vm((4, 4, 4, ROWS, OC), BF),
            vm((4, 4, 4, ROWS, OC), BF),
            vm((SEQ, ROWS, OC), BF),
            vm((SEQ, ROWS, OC), BF),
            vm((ROWS, WIDTH), F32),
            vm((640, WIDTH), BF),
            vm((EXP, 320, HALF), BF),
            vm((4, 64, OC), BF),
            vm((4, SEQ, ROWS, OC), BF),
            vm((4, SEQ, ROWS, OC), BF),
            vm((EXP, 64, WIDTH), BF),
            vm((2, 640, 256), F32),
            vm((2, EXP * 320, 256), BF),
            vm((2, SEQ, ROWS, HALF), BF),
            vm((2, SEQ, ROWS, HALF), BF),
            vm((2, ROWS, 512), BF),
            vm((2, EXP, ROWS, 512), BF),
            vm((EXP, ROWS, HALF), BF),
            vm((EXP, ROWS, HALF), BF),
            vm((256, 256), BF),
            dma((9,)),
            dma((SEQ,)), dma((SEQ,)), dma((SEQ,)), dma((SEQ,)),
            dma((4,)), dma((4,)),
            dma((40,)), dma((SEQ, 2, 3)),
            dma((4,)), dma((4,)),
            dma((4, 4)), dma((4, 4)),
            dma((SEQ,)), dma((SEQ,)),
            dma((EXP,)), dma((EXP,)),
            dma((4, SEQ)), dma((4, SEQ)),
            dma((4, 8)), dma((4, EXP, 3)),
            dma((2, 8)), dma((2, EXP, 3)),
            dma((2, SEQ)), dma((2, SEQ)),
            dma((EXP,)), dma((EXP,)),
            dma((EXP,)), dma((EXP,)),
        ],
        compiler_params=pltpu.CompilerParams(
            collective_id=0, has_side_effects=True, vmem_limit_bytes=62 * 2**20
        ),
        name="layer",
    )(
        vertical, offsets, cache_keys, cache_values, queries, keys, values, o_weight, residual,
        norm_gain.reshape(1, WIDTH), expert_ids.T, gate_weights.T,
        w_gate.transpose(0, 2, 1), w_up.transpose(0, 2, 1), w_down,
    )


def shards(
    queries,
    keys,
    values,
    cache_keys,
    cache_values,
    vertical,
    offsets,
    o_weight,
    residual,
    norm_gain,
    expert_ids,
    gate_weights,
    w_gate,
    w_up,
    w_down,
):
    return layer_of(
        queries, keys, values, cache_keys, cache_values, vertical, offsets, o_weight, residual,
        norm_gain, expert_ids, gate_weights, w_gate, w_up, w_down,
    )


def solution(mesh):
    in_specs = (
        P("seq", "exp"),
        P("seq", "exp"),
        P("seq", "exp"),
        P("seq", "exp"),
        P("seq", "exp"),
        P("exp", None),
        P("exp", None),
        P("exp", "seq"),
        P(("seq", "exp"), None),
        P(),
        P(("seq", "exp"), None),
        P(("seq", "exp"), None),
        P("seq", None, "exp"),
        P("seq", None, "exp"),
        P("seq", "exp", None),
    )
    out_specs = P(("seq", "exp"), None)
    return jax.shard_map(shards, mesh=mesh, in_specs=in_specs, out_specs=out_specs, check_vma=False)
```

```python
import functools
import math

import jax
import jax.numpy as jnp
from jax import lax
from jax.experimental import pallas as pl
from jax.experimental.pallas import tpu as pltpu
from jax.sharding import PartitionSpec as P

HD = 128
BLK = 64
NV = 16
MAXOFF = 6
SEQ = 16
EXP = 8
GROUP = 12
ROWS = 16
QLEN = 128
DH = 1536
HALF = 768
OC = 384
WIDTH = 6144
MESH = pl.DeviceIdType.MESH
BF = jnp.bfloat16
F32 = jnp.float32
VM = pl.BlockSpec(memory_space=pltpu.VMEM)
SM = pl.BlockSpec(memory_space=pltpu.SMEM)
HBM = pl.BlockSpec(memory_space=pl.ANY)


def greet(axis, me, size):
    barrier = pltpu.get_barrier_semaphore()

    def one(d, _):
        pl.semaphore_signal(
            barrier, inc=1, device_id={axis: lax.rem(me + d, size)}, device_id_type=MESH
        )
        return 0

    lax.fori_loop(1, size, one, 0)


def send(src, dst, s, r, **where):
    return pltpu.make_async_remote_copy(
        src_ref=src, dst_ref=dst, send_sem=s, recv_sem=r, device_id=where, device_id_type=MESH
    )


class Ring:
    def __init__(self, e, part, s_sem, r_sem):
        self.e, self.part, self.s_sem, self.r_sem = e, part, s_sem, r_sem
        self.z, self.c = e // 2, lax.rem(e, 2)
        self.sent = []

    def at(self, dz, dc=0):
        return lax.rem(self.z + dz + 4, 4) * 2 + (self.c if dc == 0 else 1 - self.c)

    def go(self, j, rows, to):
        ref = self.part(j, rows)
        a = send(ref, ref, self.s_sem(len(self.sent)), self.r_sem(j, rows), exp=to)
        a.start()
        self.sent.append(a)

    def wait(self, j, rows):
        ref = self.part(j, rows)
        send(ref, ref, self.s_sem(0), self.r_sem(j, rows), exp=self.at(0, 1)).wait_recv()

    def own(self):
        self.go(self.e, 2, self.at(1))
        self.go(self.e, 2, self.at(-1))
        self.go(self.e, 2, self.at(0, 1))

    def near(self):
        for dz in (-1, 1):
            j = self.at(dz)
            self.wait(j, 2)
            self.go(j, 0 if dz == -1 else 1, self.at(-dz))
            self.go(j, 2, self.at(0, 1))

    def far(self):
        j = self.at(2)
        self.wait(j, 0)
        self.wait(j, 1)
        self.go(j, 2, self.at(0, 1))

    def across(self):
        for dz in (0, 1, -1, 2):
            self.wait(self.at(dz, 1), 2)

    def done(self):
        for a in self.sent:
            a.wait_send()


def layer_kernel(
    vertical, offsets, ck_in, cv_in, q_in, k_in, v_in, w_in, res_in, gain, ids, gates, w_gate, w_up,
    w_down, out,
    cache, marks, sel, q, near, w, res, got, vert, K, V, near_o, near_top, G, P_, keep, sib_s, sib_r, z_s, z_r, last_s, last_r, fin, proj, stream,
    wt, wd, nst, outg, arr, X, acc, H, O, Z, mats, mall, mix, F, turn,
    l_sem, s_sem, r_sem, s2_sem, r2_sem, sh_sem, rh_sem,
    gs_sem, gr_sem, bs_sem, br_sem, zs_sem, zr_sem, es_sem, er_sem, ps_sem, pr_sem, ws_sem, wr_sem,
    ds_sem, dr_sem, xs_sem, xr_sem, hs_sem, hr_sem, os_sem, or_sem, ms_sem, mr_sem,
    fs_sem, fr_sem,
):
    me = lax.axis_index("seq")
    e = lax.axis_index("exp")
    y, x = me // 4, lax.rem(me, 4)
    z, c = e // 2, lax.rem(e, 2)
    def iota(shape, dim):
        return lax.broadcasted_iota(jnp.int32, shape, dim)

    def flag(mask):
        return jnp.where(mask, 1.0, 0.0).astype(F32)

    greet("seq", me, SEQ)
    greet("exp", e, EXP)

    loads = [
        pltpu.make_async_copy(a, b, l_sem.at[i])
        for i, (a, b) in enumerate(
            [(ck_in, cache.at[:, :HD]), (cv_in, cache.at[:, HD:]), (k_in, near.at[0, 3]), (v_in, near.at[1, 3]), (q_in, q),
             (w_in, w), (res_in, res), (w_gate.at[0], wt.at[:320]), (w_up.at[0], wt.at[320:])]
        )
    ]
    for a in loads:
        a.start()
    loads[0].wait()
    loads[1].wait()
    apart = iota((BLK, NV * BLK), 1) - iota((BLK, NV * BLK), 0)
    for j in range(NV):
        marks[j * BLK : (j + 1) * BLK, :] = flag(
            apart == (vertical[0, j] - me * NV) * BLK
        ).astype(BF)

    def pick(m, _):
        rows = pl.ds(pl.multiple_of(m * 256, 256), 256)
        picked = jnp.dot(marks[rows, :], cache[...], preferred_element_type=F32)
        sel[pl.ds(m * 4, 4)] = picked.astype(BF).reshape(4, BLK, 2 * HD)
        return 0

    lax.fori_loop(0, 4, pick, 0)
    got[me] = sel[me]
    loads[2].wait()
    loads[3].wait()
    pl.semaphore_wait(pltpu.get_barrier_semaphore(), SEQ - 1 + EXP - 1)

    def w_copy(d):
        to = lax.rem(e + d, EXP)
        cols = pl.ds(pl.multiple_of(to * HALF, HALF), HALF)
        return send(w_down.at[0, :, cols], wd.at[e], ws_sem.at[d], wr_sem.at[e], exp=to)

    def piece(d):
        to = lax.rem(me + d, SEQ)
        return send(sel.at[to], got.at[me], s_sem.at[d], r_sem.at[me], seq=to)

    def share(d):
        to = lax.rem(me + d, SEQ)
        return send(vert.at[me], vert.at[me], s2_sem.at[d], r2_sem.at[me], seq=to)

    def halo(d):
        to = lax.rem(me + d, SEQ)
        return send(near.at[:, 3], near.at[:, 3 - d], sh_sem.at[d], rh_sem.at[d], seq=to)

    def start_piece(d, _):
        piece(d).start()
        return 0

    def start_share(d, _):
        share(d).start()
        return 0

    def arrived_piece(d, _):
        frm = lax.rem(me + d, SEQ)
        send(sel.at[0], got.at[frm], s_sem.at[0], r_sem.at[frm], seq=frm).wait_recv()
        return 0

    def arrived_share(d, _):
        frm = lax.rem(me + d, SEQ)
        send(vert.at[me], vert.at[frm], s2_sem.at[0], r2_sem.at[frm], seq=frm).wait_recv()
        return 0

    lax.fori_loop(1, SEQ, start_piece, 0)
    for d in (1, 2, 3):
        halo(d).start()
    for d in range(1, EXP):
        w_copy(d).start()
    w_own = pltpu.make_async_copy(
        w_down.at[0, :, pl.ds(pl.multiple_of(e * HALF, HALF), HALF)], wd.at[e], ws_sem.at[0]
    )
    w_own.start()
    def column(row):
        same = iota((ROWS, ROWS), 0) == iota((ROWS, ROWS), 1)
        return jnp.sum(jnp.where(same, row.astype(F32), 0.0), axis=1, keepdims=True)

    first, second = column(ids[0:1, :]), column(ids[1:2, :])
    gate0, gate1 = column(gates[0:1, :]), column(gates[1:2, :])

    experts = iota((ROWS, SEQ), 1).astype(F32)
    hot0, hot1 = flag(experts == first), flag(experts == second)
    lower = flag(iota((ROWS, ROWS), 1) < iota((ROWS, ROWS), 0)).astype(BF)
    ones = jnp.ones((ROWS, ROWS), BF)
    before0 = jnp.dot(lower, hot0.astype(BF), preferred_element_type=F32)
    before1 = jnp.dot(lower, hot1.astype(BF), preferred_element_type=F32)
    before1 = before1 + jnp.dot(ones, hot0.astype(BF), preferred_element_type=F32)
    slot0 = jnp.sum(before0 * hot0, axis=1, keepdims=True)
    slot1 = jnp.sum(before1 * hot1, axis=1, keepdims=True)

    lanes = iota((4 * ROWS, 256), 1).astype(F32)
    quarter = (iota((4 * ROWS, 1), 0) >> 4).astype(F32) * 4.0
    t0 = jnp.concatenate([first * 16.0 + slot0] * 4, axis=0) + quarter
    t1 = jnp.concatenate([second * 16.0 + slot1] * 4, axis=0) + quarter
    spread = flag((lanes == t0) | (lanes == t1)).astype(BF)

    place = ((e // 4) * 256 + lax.rem(e, 4) * 4).astype(F32)
    lanes = iota((ROWS, 512), 1).astype(F32)
    weigh = jnp.where(lanes == first * 16.0 + slot0 + place, gate0, 0.0)
    weigh = weigh + jnp.where(lanes == second * 16.0 + slot1 + place, gate1, 0.0)
    high = weigh.astype(BF)
    mats[0] = high
    mats[1] = (weigh - high.astype(F32)).astype(BF)
    mall[:, e] = mats[...]

    def m_copy(d):
        to = lax.rem(e + d, EXP)
        return send(mats, mall.at[:, e], ms_sem.at[d], mr_sem.at[e], exp=to)

    for d in range(1, EXP):
        m_copy(d).start()

    pi, pj = iota((256, 256), 0), iota((256, 256), 1)
    sort = flag(
        ((pi >> 6) == ((pj & 15) >> 2)) & (((pi & 63) >> 2) == (pj >> 4)) & ((pi & 3) == (pj & 3))
    ).astype(BF)
    turn[...] = flag(
        ((pi >> 4) == ((pj & 63) >> 2)) & (((pi & 15) >> 2) == (pj >> 6)) & ((pi & 3) == (pj & 3))
    ).astype(BF)

    lax.fori_loop(1, SEQ, arrived_piece, 0)
    total = got[0].astype(F32)
    for j in range(1, SEQ):
        total = total + got[j].astype(F32)
    vert[me] = total.astype(BF)
    lax.fori_loop(1, SEQ, start_share, 0)

    loads[4].wait()
    for d in (1, 2, 3):
        halo(d).wait()
    qi = lax.broadcasted_iota(jnp.int32, (2 * BLK, 8 * BLK), 0)
    ki = lax.broadcasted_iota(jnp.int32, (2 * BLK, 8 * BLK), 1)
    spacing = (qi >> 6) + MAXOFF - (ki >> 6)
    banded = spacing == offsets[0, 0]
    for t in range(1, 4):
        banded = banded | (spacing == offsets[0, t])
    banded = banded & ((ki >> 6) + 2 * me >= MAXOFF)
    allowed = banded | ((spacing == 0) & ((ki & 63) <= (qi & 63)))
    K[: 8 * BLK, :] = near[0].reshape(8 * BLK, HD)
    V[: 8 * BLK, :HD] = near[1].reshape(8 * BLK, HD)
    V[:, HD:] = jnp.ones((24 * BLK, HD), BF)
    scale = math.log2(math.e) / math.sqrt(HD)
    nt = (((1,), (1,)), ((), ()))

    def near_head(h):
        qh = q[:, pl.ds(pl.multiple_of(h * HD, HD), HD)]
        sn = lax.dot_general(qh, K[: 8 * BLK, :], nt, preferred_element_type=F32)
        sn = jnp.where(allowed, sn, -jnp.inf)
        top = jnp.max(sn, axis=1, keepdims=True)
        en = jnp.exp2((sn - top) * scale).astype(BF)
        near_o[h] = jnp.dot(en, V[: 8 * BLK, :], preferred_element_type=F32)
        near_top[h] = jnp.broadcast_to(top, (QLEN, HD))

    def some_near(i, _):
        for k in range(3):
            near_head(i * 3 + k)
        return 0

    lax.fori_loop(0, GROUP // 3, some_near, 0)
    lax.fori_loop(1, SEQ, arrived_share, 0)
    K[8 * BLK :, :] = vert[:, :, :HD].reshape(NV * BLK, HD)
    V[8 * BLK :, :HD] = vert[:, :, HD:].reshape(NV * BLK, HD)

    def head(h):
        cols = pl.ds(pl.multiple_of(h * HD, HD), HD)
        qh = q[:, cols]
        sv = lax.dot_general(qh, K[8 * BLK :, :], nt, preferred_element_type=F32)
        near_m = near_top[h]
        top = jnp.maximum(near_m, jnp.max(sv, axis=1, keepdims=True))
        ev = jnp.exp2((sv - top[:, :1]) * scale).astype(BF)
        o = jnp.dot(ev, V[8 * BLK :, :], preferred_element_type=F32)
        fade = jnp.exp2((near_m - top) * scale)
        o = o + near_o[h] * jnp.concatenate([fade, fade], axis=1)
        o = o[:, :HD] / o[:, HD:]
        G[me, :, cols] = o.astype(BF)

    def some_heads(i, _):
        for k in range(3):
            head(i * 3 + k)
        return 0

    def at(dy, dx):
        return lax.rem(y + dy + 4, 4) * 4 + lax.rem(x + dx + 4, 4)

    def part(src, half, rows):
        cols = pl.ds(half * HALF, HALF)
        if rows == 2:
            return G.at[src, :, cols]
        return G.at[src, pl.ds(rows * BLK, BLK), cols]

    sent = []

    def forward(dy, dx, half, rows, ty, tx):
        src, to = at(dy, dx), at(ty, tx)
        ref = part(src, half, rows)
        a = send(ref, ref, gs_sem.at[len(sent)], gr_sem.at[src, half, rows], seq=to)
        a.start()
        sent.append(a)

    def swap(half, a, b):
        return (a, b) if half == 0 else (b, a)

    def arrive(dy, dx, half):
        a, b = swap(half, dy, dx)
        split = a == 2 or (a == 0 and b == 2)
        src = at(dy, dx)
        for rows in ((0, 1) if split else (2,)):
            ref = part(src, half, rows)
            send(ref, ref, gs_sem.at[0], gr_sem.at[src, half, rows], seq=src).wait_recv()
        if a == 0 and b in (1, -1):
            forward(dy, dx, half, 0 if b == -1 else 1, *swap(half, 0, -b))
        if a == 0:
            forward(dy, dx, half, 2, *swap(half, 1, 0))
            forward(dy, dx, half, 2, *swap(half, -1, 0))
        elif a in (1, -1):
            forward(dy, dx, half, 0 if a == -1 else 1, *swap(half, -a, 0))

    def launch(half):
        for b in (1, -1):
            forward(0, 0, half, 2, *swap(half, 0, b))
        for a in (1, -1):
            forward(0, 0, half, 2, *swap(half, a, 0))

    lax.fori_loop(0, GROUP // 6, some_heads, 0)
    launch(0)
    lax.fori_loop(GROUP // 6, GROUP // 3, some_heads, 0)
    launch(1)
    loads[5].wait()
    loads[6].wait()

    order = [(0, 0), (0, 1), (0, -1), (1, 0), (-1, 0), (0, 2), (2, 0), (1, 1), (1, -1), (-1, 1),
             (-1, -1), (1, 2), (-1, 2), (2, 1), (2, -1), (2, 2)]

    spans = [(0, 5), (5, 11), (11, 15)]

    def sib_copy(g):
        ts = pl.ds(spans[g][0], spans[g][1] - spans[g][0])
        return send(sib_s.at[:, ts], sib_r.at[:, ts], bs_sem.at[g], br_sem.at[g],
                    exp=z * 2 + 1 - c)

    def z_copy(g, dz):
        to = lax.rem(z + dz, 4)
        ts = pl.ds(spans[g][0], spans[g][1] - spans[g][0])
        return send(z_s.at[to, ts], z_r.at[z, ts], zs_sem.at[g, dz], zr_sem.at[g, z],
                    exp=to * 2 + c)

    def z_arrive(g, dz):
        frm = lax.rem(z + dz, 4)
        ts = pl.ds(spans[g][0], spans[g][1] - spans[g][0])
        send(z_s.at[frm, ts], z_r.at[frm, ts], zs_sem.at[g, dz], zr_sem.at[g, frm],
             exp=frm * 2 + c).wait_recv()
        return frm

    def e_copy(d):
        to = lax.rem(e + d, EXP)
        return send(last_s.at[to], last_r.at[e], es_sem.at[d], er_sem.at[e], exp=to)

    def p_copy(t):
        to = at(*order[t])
        return send(fin.at[t], proj.at[me], ps_sem.at[t], pr_sem.at[me], seq=to)

    def multiply(t):
        P_[...] = jnp.dot(G[at(*order[t])], w[...], preferred_element_type=F32)
        for zz in range(4):
            keep[zz, t] = P_[pl.ds(pl.multiple_of((zz * 2 + c) * ROWS, ROWS), ROWS), :]
            sib_s[zz, t] = P_[
                pl.ds(pl.multiple_of((zz * 2 + 1 - c) * ROWS, ROWS), ROWS), :
            ].astype(BF)
        if t in (4, 14):
            sib_copy(0 if t == 4 else 2).start()

    def pair(g):
        ts = slice(*spans[g])
        sib_copy(g).wait_recv()
        both = keep[:, ts] + sib_r[:, ts].astype(F32)
        keep[:, ts] = both
        z_s[:, ts] = both.astype(BF)
        for dz in (2, 1, 3):
            z_copy(g, dz).start()

    def finish(g):
        ts = slice(*spans[g])
        acc_ = keep[z, ts]
        for dz in (1, 3, 2):
            frm = z_arrive(g, dz)
            acc_ = acc_ + z_r[frm, ts].astype(F32)
        fin[ts] = acc_.astype(BF)
        for t in range(*spans[g]):
            if t > 0:
                p_copy(t).start()

    multiply(0)
    for dx in (1, -1):
        arrive(0, dx, 0)
        arrive(dx, 0, 1)
    for dx in (1, -1):
        arrive(0, dx, 1)
        arrive(dx, 0, 0)
    for t in (1, 2, 3, 4):
        multiply(t)
    arrive(0, 2, 0)
    arrive(2, 0, 1)
    pair(0)
    for dy in (1, -1):
        for dx in (1, -1):
            arrive(dy, dx, 0)
            arrive(dy, dx, 1)
    for t in (7, 8, 9, 10):
        multiply(t)
    arrive(0, 2, 1)
    arrive(2, 0, 0)
    for t in (5, 6):
        multiply(t)
    sib_copy(1).start()
    finish(0)
    pair(1)
    for s in (1, -1):
        arrive(s, 2, 0)
        arrive(2, s, 1)
    for s in (1, -1):
        arrive(s, 2, 1)
        arrive(2, s, 0)
    for t in (11, 12, 13, 14):
        multiply(t)
    finish(1)
    pair(2)
    arrive(2, 2, 0)
    arrive(2, 2, 1)
    P_[...] = jnp.dot(G[at(2, 2)], w[...], preferred_element_type=F32)
    last_s[...] = P_[...].astype(BF).reshape(EXP, ROWS, OC)
    for d in range(1, EXP):
        e_copy(d).start()
    last = P_[pl.ds(pl.multiple_of(e * ROWS, ROWS), ROWS), :]
    finish(2)
    for d in range(1, EXP):
        frm = lax.rem(e + d, EXP)
        send(last_s.at[0], last_r.at[frm], es_sem.at[0], er_sem.at[frm], exp=frm).wait_recv()
        last = last + last_r[frm].astype(F32)
    fin[15] = last.astype(BF)
    p_copy(15).start()

    proj[me] = fin[0]
    for s in range(1, SEQ):
        frm = lax.rem(me + s, SEQ)
        send(fin.at[0], proj.at[frm], ps_sem.at[0], pr_sem.at[frm], seq=frm).wait_recv()
    for s in range(SEQ):
        cols = slice(s * OC, s * OC + OC)
        stream[:, cols] = res[:, cols].astype(F32) + proj[s].astype(F32)

    st = stream[...]
    root = lax.rsqrt(jnp.mean(st * st, axis=1, keepdims=True) + 1e-06)
    for q in range(4):
        for s in range(4):
            cols = slice(q * DH + s * OC, q * DH + s * OC + OC)
            nst[q, s * ROWS : (s + 1) * ROWS, :] = (stream[:, cols] * root * gain[:, cols]).astype(BF)

    def d_copy(q, d):
        to = lax.rem(me + d, SEQ)
        return send(outg.at[q, to], arr.at[q, me], ds_sem.at[q, d], dr_sem.at[q, me], seq=to)


    def scatter(q):
        o = lax.dot_general(
            spread, nst[q], (((0,), (0,)), ((), ())), preferred_element_type=F32
        )
        outg[q] = o.astype(BF).reshape(SEQ, ROWS, OC)

        def start_d(d, _):
            d_copy(q, d).start()
            return 0

        lax.fori_loop(1, SEQ, start_d, 0)
        arr[q, me] = outg[q, me]

    def x_part(q):
        def part(j, rows):
            cols = pl.ds(q * DH, DH)
            if rows == 2:
                return X.at[j, :, cols]
            return X.at[j, pl.ds(rows * 32, 32), cols]

        return part

    rings = [
        Ring(e, x_part(q), lambda n, q=q: xs_sem.at[q, n], lambda j, r, q=q: xr_sem.at[q, j, r])
        for q in range(4)
    ]

    def begin(q):
        def arrived(d, _):
            frm = lax.rem(me + d, SEQ)
            send(outg.at[q, 0], arr.at[q, frm], ds_sem.at[q, 0], dr_sem.at[q, frm],
                 seq=frm).wait_recv()
            return 0

        lax.fori_loop(1, SEQ, arrived, 0)
        o = jnp.dot(sort, arr[q].reshape(256, OC), preferred_element_type=F32).astype(BF)
        for s in range(4):
            X[e, :, q * DH + s * OC : q * DH + s * OC + OC] = o[s * 64 : (s + 1) * 64]
        rings[q].own()

    def gate_up(q):
        rings[q].far()
        rings[q].across()
        if q == 0:
            loads[7].wait()
            loads[8].wait()
        cols = slice(q * DH, (q + 1) * DH)

        def some(m, _):
            xb = X[pl.ds(m * 4, 4), :, cols].reshape(256, DH)
            o = lax.dot_general(wt[:, cols], xb, nt, preferred_element_type=F32)
            if q > 0:
                o = o + acc[m]
            acc[m] = o
            return 0

        lax.fori_loop(0, 2, some, 0)

    scatter(0)
    scatter(1)
    begin(0)
    scatter(2)
    begin(1)
    scatter(3)
    rings[0].near()
    begin(2)
    rings[1].near()
    gate_up(0)
    begin(3)
    rings[2].near()
    gate_up(1)
    rings[3].near()
    gate_up(2)
    gate_up(3)

    def h_part(r):
        def part(j, rows):
            if rows == 2:
                return H.at[r, pl.ds(j * 320, 320), :]
            return H.at[r, pl.ds(j * 320 + rows * 160, 160), :]

        return part

    h_rings = [
        Ring(e, h_part(r), lambda n, r=r: hs_sem.at[r, n], lambda j, s, r=r: hr_sem.at[r, j, s])
        for r in range(2)
    ]
    for r in range(2):
        g, u = acc[r, :320], acc[r, 320:]
        hidden = (g / (1.0 + jnp.exp(-g)) * u).astype(BF)
        H[r, pl.ds(pl.multiple_of(e * 320, 64), 320), :] = lax.dot_general(
            hidden, turn[...], nt, preferred_element_type=F32
        ).astype(BF)
        h_rings[r].own()
    w_own.wait()
    for d in range(1, EXP):
        frm = lax.rem(e + d, EXP)
        send(wd.at[frm], wd.at[frm], ws_sem.at[0], wr_sem.at[frm], exp=frm).wait_recv()

    def o_copy(r, d):
        to = lax.rem(me + d, SEQ)
        return send(O.at[r, to], Z.at[r, me], os_sem.at[r, d], or_sem.at[r, me], seq=to)

    for r in range(2):
        h_rings[r].near()
    for r in range(2):
        h_rings[r].far()
        h_rings[r].across()
        o = lax.dot_general(
            H[r], wd[...].reshape(EXP * 320, HALF), (((0,), (0,)), ((), ())),
            preferred_element_type=F32,
        )
        O[r] = o.astype(BF).reshape(SEQ, ROWS, HALF)

        def start_o(d, _, r=r):
            o_copy(r, d).start()
            return 0

        lax.fori_loop(1, SEQ, start_o, 0)
        Z[r, me] = O[r, me]

    for d in range(1, EXP):
        frm = lax.rem(e + d, EXP)
        send(mats, mall.at[:, frm], ms_sem.at[0], mr_sem.at[frm], exp=frm).wait_recv()
    for r in range(2):
        def arrived_o(d, _, r=r):
            frm = lax.rem(me + d, SEQ)
            send(O.at[r, 0], Z.at[r, frm], os_sem.at[r, 0], or_sem.at[r, frm], seq=frm).wait_recv()
            return 0

        lax.fori_loop(1, SEQ, arrived_o, 0)
    m2 = jnp.dot(
        mall[...].reshape(256, 512), Z[...].reshape(512, HALF), preferred_element_type=F32
    )
    mix[...] = (m2[:128] + m2[128:]).astype(BF).reshape(EXP, ROWS, HALF)
    F[e] = mix[e]

    def f_copy(d):
        to = lax.rem(e + d, EXP)
        return send(mix.at[to], F.at[e], fs_sem.at[d], fr_sem.at[e], exp=to)

    for d in range(1, EXP):
        f_copy(d).start()
    for d in range(1, EXP):
        frm = lax.rem(e + d, EXP)
        send(mix.at[0], F.at[frm], fs_sem.at[0], fr_sem.at[frm], exp=frm).wait_recv()
    for j in range(EXP):
        cols = slice(j * HALF, (j + 1) * HALF)
        out[:, cols] = (stream[:, cols] + F[j].astype(F32)).astype(BF)

    def done_front(d, _):
        piece(d).wait_send()
        share(d).wait_send()
        return 0

    lax.fori_loop(1, SEQ, done_front, 0)
    for d in range(1, EXP):
        w_copy(d).wait_send()
    for a in sent:
        a.wait_send()
    for d in range(1, EXP):
        e_copy(d).wait_send()
    for g in range(3):
        sib_copy(g).wait_send()
        for dz in (1, 2, 3):
            z_copy(g, dz).wait_send()
    for t in range(1, SEQ):
        p_copy(t).wait_send()


    def done(d, _):
        for q in range(4):
            d_copy(q, d).wait_send()
        for r in range(2):
            o_copy(r, d).wait_send()
        return 0

    lax.fori_loop(1, SEQ, done, 0)
    for ring in rings + h_rings:
        ring.done()
    for d in range(1, EXP):
        m_copy(d).wait_send()
        f_copy(d).wait_send()


def layer_of(
    queries, keys, values, cache_keys, cache_values, vertical, offsets, o_weight, residual,
    norm_gain, expert_ids, gate_weights, w_gate, w_up, w_down,
):
    dma = pltpu.SemaphoreType.DMA
    vm = pltpu.VMEM
    return pl.pallas_call(
        layer_kernel,
        out_shape=jax.ShapeDtypeStruct((ROWS, WIDTH), BF),
        in_specs=[SM, SM] + [HBM] * 7 + [VM] * 3 + [HBM] * 3,
        out_specs=VM,
        scratch_shapes=[
            vm((NV * BLK, 2 * HD), BF),
            vm((NV * BLK, NV * BLK), BF),
            vm((NV, BLK, 2 * HD), BF),
            vm((QLEN, DH), BF),
            vm((2, 4, 2 * BLK, HD), BF),
            vm((DH, OC), BF),
            vm((ROWS, WIDTH), BF),
            vm((NV, BLK, 2 * HD), BF),
            vm((NV, BLK, 2 * HD), BF),
            vm((24 * BLK, HD), BF),
            vm((24 * BLK, 2 * HD), BF),
            vm((GROUP, QLEN, 2 * HD), F32),
            vm((GROUP, QLEN, HD), F32),
            vm((SEQ, QLEN, DH), BF),
            vm((QLEN, OC), F32),
            vm((4, SEQ, ROWS, OC), F32),
            vm((4, SEQ, ROWS, OC), BF),
            vm((4, SEQ, ROWS, OC), BF),
            vm((4, SEQ, ROWS, OC), BF),
            vm((4, SEQ, ROWS, OC), BF),
            vm((EXP, ROWS, OC), BF),
            vm((EXP, ROWS, OC), BF),
            vm((SEQ, ROWS, OC), BF),
            vm((SEQ, ROWS, OC), BF),
            vm((ROWS, WIDTH), F32),
            vm((640, WIDTH), BF),
            vm((EXP, 320, HALF), BF),
            vm((4, 64, OC), BF),
            vm((4, SEQ, ROWS, OC), BF),
            vm((4, SEQ, ROWS, OC), BF),
            vm((EXP, 64, WIDTH), BF),
            vm((2, 640, 256), F32),
            vm((2, EXP * 320, 256), BF),
            vm((2, SEQ, ROWS, HALF), BF),
            vm((2, SEQ, ROWS, HALF), BF),
            vm((2, ROWS, 512), BF),
            vm((2, EXP, ROWS, 512), BF),
            vm((EXP, ROWS, HALF), BF),
            vm((EXP, ROWS, HALF), BF),
            vm((256, 256), BF),
            dma((9,)),
            dma((SEQ,)), dma((SEQ,)), dma((SEQ,)), dma((SEQ,)),
            dma((4,)), dma((4,)),
            dma((40,)), dma((SEQ, 2, 3)),
            dma((4,)), dma((4,)),
            dma((4, 4)), dma((4, 4)),
            dma((EXP,)), dma((EXP,)),
            dma((SEQ,)), dma((SEQ,)),
            dma((EXP,)), dma((EXP,)),
            dma((4, SEQ)), dma((4, SEQ)),
            dma((4, 8)), dma((4, EXP, 3)),
            dma((2, 8)), dma((2, EXP, 3)),
            dma((2, SEQ)), dma((2, SEQ)),
            dma((EXP,)), dma((EXP,)),
            dma((EXP,)), dma((EXP,)),
        ],
        compiler_params=pltpu.CompilerParams(
            collective_id=0, has_side_effects=True, vmem_limit_bytes=62 * 2**20
        ),
        name="layer",
    )(
        vertical, offsets, cache_keys, cache_values, queries, keys, values, o_weight, residual,
        norm_gain.reshape(1, WIDTH), expert_ids.T, gate_weights.T,
        w_gate.transpose(0, 2, 1), w_up.transpose(0, 2, 1), w_down,
    )


def shards(
    queries,
    keys,
    values,
    cache_keys,
    cache_values,
    vertical,
    offsets,
    o_weight,
    residual,
    norm_gain,
    expert_ids,
    gate_weights,
    w_gate,
    w_up,
    w_down,
):
    return layer_of(
        queries, keys, values, cache_keys, cache_values, vertical, offsets, o_weight, residual,
        norm_gain, expert_ids, gate_weights, w_gate, w_up, w_down,
    )


def solution(mesh):
    in_specs = (
        P("seq", "exp"),
        P("seq", "exp"),
        P("seq", "exp"),
        P("seq", "exp"),
        P("seq", "exp"),
        P("exp", None),
        P("exp", None),
        P("exp", "seq"),
        P(("seq", "exp"), None),
        P(),
        P(("seq", "exp"), None),
        P(("seq", "exp"), None),
        P("seq", None, "exp"),
        P("seq", None, "exp"),
        P("seq", "exp", None),
    )
    out_specs = P(("seq", "exp"), None)
    return jax.shard_map(shards, mesh=mesh, in_specs=in_specs, out_specs=out_specs, check_vma=False)
```

```python
import functools
import math

import jax
import jax.numpy as jnp
from jax import lax
from jax.experimental import pallas as pl
from jax.experimental.pallas import tpu as pltpu
from jax.sharding import PartitionSpec as P

HD = 128
BLK = 64
NV = 16
MAXOFF = 6
SEQ = 16
EXP = 8
GROUP = 12
ROWS = 16
QLEN = 128
DH = 1536
HALF = 768
OC = 384
WIDTH = 6144
MESH = pl.DeviceIdType.MESH
BF = jnp.bfloat16
F32 = jnp.float32
VM = pl.BlockSpec(memory_space=pltpu.VMEM)
SM = pl.BlockSpec(memory_space=pltpu.SMEM)
HBM = pl.BlockSpec(memory_space=pl.ANY)


def greet(axis, me, size):
    barrier = pltpu.get_barrier_semaphore()

    def one(d, _):
        pl.semaphore_signal(
            barrier, inc=1, device_id={axis: lax.rem(me + d, size)}, device_id_type=MESH
        )
        return 0

    lax.fori_loop(1, size, one, 0)


def send(src, dst, s, r, **where):
    return pltpu.make_async_remote_copy(
        src_ref=src, dst_ref=dst, send_sem=s, recv_sem=r, device_id=where, device_id_type=MESH
    )


class Ring:
    def __init__(self, e, part, s_sem, r_sem):
        self.e, self.part, self.s_sem, self.r_sem = e, part, s_sem, r_sem
        self.z, self.c = e // 2, lax.rem(e, 2)
        self.sent = []

    def at(self, dz, dc=0):
        return lax.rem(self.z + dz + 4, 4) * 2 + (self.c if dc == 0 else 1 - self.c)

    def go(self, j, rows, to):
        ref = self.part(j, rows)
        a = send(ref, ref, self.s_sem(len(self.sent)), self.r_sem(j, rows), exp=to)
        a.start()
        self.sent.append(a)

    def wait(self, j, rows):
        ref = self.part(j, rows)
        send(ref, ref, self.s_sem(0), self.r_sem(j, rows), exp=self.at(0, 1)).wait_recv()

    def own(self):
        self.go(self.e, 2, self.at(1))
        self.go(self.e, 2, self.at(-1))
        self.go(self.e, 2, self.at(0, 1))

    def near(self):
        for dz in (-1, 1):
            j = self.at(dz)
            self.wait(j, 2)
            self.go(j, 0 if dz == -1 else 1, self.at(-dz))
            self.go(j, 2, self.at(0, 1))

    def far(self):
        j = self.at(2)
        self.wait(j, 0)
        self.wait(j, 1)
        self.go(j, 2, self.at(0, 1))

    def across(self):
        for dz in (0, 1, -1, 2):
            self.wait(self.at(dz, 1), 2)

    def done(self):
        for a in self.sent:
            a.wait_send()


def layer_kernel(
    vertical, offsets, ck_in, cv_in, q_in, k_in, v_in, w_in, res_in, gain, ids, gates, w_gate, w_up,
    w_down, out,
    cache, marks, sel, q, near, w, res, got, vert, K, V, near_o, near_top, G, P_, keep, sib_s, sib_r, z_s, z_r, last_s, last_r, fin, proj, stream,
    wt, wd, nst, outg, arr, X, spread_s, spreads, tokens, outc, arrc, acc, H, O, Z, mats, mall, mix, F, turn,
    l_sem, s_sem, r_sem, s2_sem, r2_sem, sh_sem, rh_sem,
    gs_sem, gr_sem, bs_sem, br_sem, zs_sem, zr_sem, es_sem, er_sem, ps_sem, pr_sem, ws_sem, wr_sem,
    ds_sem, dr_sem, xs_sem, xr_sem, hs_sem, hr_sem, os_sem, or_sem, ms_sem, mr_sem,
    fs_sem, fr_sem, us_sem, ur_sem, vs_sem, vr_sem, cs_sem, cr_sem, c2_sem,
):
    me = lax.axis_index("seq")
    e = lax.axis_index("exp")
    y, x = me // 4, lax.rem(me, 4)
    z, c = e // 2, lax.rem(e, 2)
    def iota(shape, dim):
        return lax.broadcasted_iota(jnp.int32, shape, dim)

    def flag(mask):
        return jnp.where(mask, 1.0, 0.0).astype(F32)

    greet("seq", me, SEQ)
    greet("exp", e, EXP)
    opposite = lax.rem(y + 2, 4) * 4 + lax.rem(x + 2, 4)
    for d in range(1, EXP):
        pl.semaphore_signal(
            pltpu.get_barrier_semaphore(), inc=1,
            device_id={"seq": opposite, "exp": lax.rem(e + d, EXP)}, device_id_type=MESH,
        )

    loads = [
        pltpu.make_async_copy(a, b, l_sem.at[i])
        for i, (a, b) in enumerate(
            [(ck_in, cache.at[:, :HD]), (cv_in, cache.at[:, HD:]), (k_in, near.at[0, 3]), (v_in, near.at[1, 3]), (q_in, q),
             (w_in, w), (res_in, res), (w_gate.at[0], wt.at[:320]), (w_up.at[0], wt.at[320:])]
        )
    ]
    for a in loads:
        a.start()
    loads[0].wait()
    loads[1].wait()
    apart = iota((BLK, NV * BLK), 1) - iota((BLK, NV * BLK), 0)
    for j in range(NV):
        marks[j * BLK : (j + 1) * BLK, :] = flag(
            apart == (vertical[0, j] - me * NV) * BLK
        ).astype(BF)

    def pick(m, _):
        rows = pl.ds(pl.multiple_of(m * 256, 256), 256)
        picked = jnp.dot(marks[rows, :], cache[...], preferred_element_type=F32)
        sel[pl.ds(m * 4, 4)] = picked.astype(BF).reshape(4, BLK, 2 * HD)
        return 0

    lax.fori_loop(0, 4, pick, 0)
    got[me] = sel[me]
    loads[2].wait()
    loads[3].wait()
    pl.semaphore_wait(pltpu.get_barrier_semaphore(), SEQ - 1 + 2 * (EXP - 1))

    def w_copy(d):
        to = lax.rem(e + d, EXP)
        cols = pl.ds(pl.multiple_of(to * HALF, HALF), HALF)
        return send(w_down.at[0, :, cols], wd.at[e], ws_sem.at[d], wr_sem.at[e], exp=to)

    def piece(d):
        to = lax.rem(me + d, SEQ)
        return send(sel.at[to], got.at[me], s_sem.at[d], r_sem.at[me], seq=to)

    def share(d):
        to = lax.rem(me + d, SEQ)
        return send(vert.at[me], vert.at[me], s2_sem.at[d], r2_sem.at[me], seq=to)

    def halo(d):
        to = lax.rem(me + d, SEQ)
        return send(near.at[:, 3], near.at[:, 3 - d], sh_sem.at[d], rh_sem.at[d], seq=to)

    def start_piece(d, _):
        piece(d).start()
        return 0

    def start_share(d, _):
        share(d).start()
        return 0

    def arrived_piece(d, _):
        frm = lax.rem(me + d, SEQ)
        send(sel.at[0], got.at[frm], s_sem.at[0], r_sem.at[frm], seq=frm).wait_recv()
        return 0

    def arrived_share(d, _):
        frm = lax.rem(me + d, SEQ)
        send(vert.at[me], vert.at[frm], s2_sem.at[0], r2_sem.at[frm], seq=frm).wait_recv()
        return 0

    lax.fori_loop(1, SEQ, start_piece, 0)
    for d in (1, 2, 3):
        halo(d).start()
    for d in range(1, EXP):
        w_copy(d).start()
    w_own = pltpu.make_async_copy(
        w_down.at[0, :, pl.ds(pl.multiple_of(e * HALF, HALF), HALF)], wd.at[e], ws_sem.at[0]
    )
    w_own.start()
    def column(row):
        same = iota((ROWS, ROWS), 0) == iota((ROWS, ROWS), 1)
        return jnp.sum(jnp.where(same, row.astype(F32), 0.0), axis=1, keepdims=True)

    first, second = column(ids[0:1, :]), column(ids[1:2, :])
    gate0, gate1 = column(gates[0:1, :]), column(gates[1:2, :])

    experts = iota((ROWS, SEQ), 1).astype(F32)
    hot0, hot1 = flag(experts == first), flag(experts == second)
    lower = flag(iota((ROWS, ROWS), 1) < iota((ROWS, ROWS), 0)).astype(BF)
    ones = jnp.ones((ROWS, ROWS), BF)
    before0 = jnp.dot(lower, hot0.astype(BF), preferred_element_type=F32)
    before1 = jnp.dot(lower, hot1.astype(BF), preferred_element_type=F32)
    before1 = before1 + jnp.dot(ones, hot0.astype(BF), preferred_element_type=F32)
    slot0 = jnp.sum(before0 * hot0, axis=1, keepdims=True)
    slot1 = jnp.sum(before1 * hot1, axis=1, keepdims=True)

    lanes = iota((4 * ROWS, 256), 1).astype(F32)
    quarter = (iota((4 * ROWS, 1), 0) >> 4).astype(F32) * 4.0
    t0 = jnp.concatenate([first * 16.0 + slot0] * 4, axis=0) + quarter
    t1 = jnp.concatenate([second * 16.0 + slot1] * 4, axis=0) + quarter
    spread = flag((lanes == t0) | (lanes == t1)).astype(BF)

    quad, member = e // 4, lax.rem(e, 4)
    spread_s[...] = spread

    def u_copy(zz):
        return send(spread_s, spreads.at[member], us_sem.at[zz], ur_sem.at[member],
                    exp=zz * 2 + quad)

    def v_copy(zz):
        return send(nst.at[3], tokens.at[member], vs_sem.at[zz], vr_sem.at[member],
                    exp=zz * 2 + quad)

    def to_quad(act):
        for zz in range(4):
            @pl.when(zz * 2 + quad != e)
            def _():
                act(zz)

    place = ((e // 4) * 256 + lax.rem(e, 4) * 4).astype(F32)
    lanes = iota((ROWS, 512), 1).astype(F32)
    weigh = jnp.where(lanes == first * 16.0 + slot0 + place, gate0, 0.0)
    weigh = weigh + jnp.where(lanes == second * 16.0 + slot1 + place, gate1, 0.0)
    high = weigh.astype(BF)
    mats[0] = high
    mats[1] = (weigh - high.astype(F32)).astype(BF)
    mall[:, e] = mats[...]

    def m_copy(d):
        to = lax.rem(e + d, EXP)
        return send(mats, mall.at[:, e], ms_sem.at[d], mr_sem.at[e], exp=to)

    for d in range(1, EXP):
        m_copy(d).start()
    to_quad(lambda zz: u_copy(zz).start())

    @pl.when(quad == c)
    def _():
        spreads[member] = spread

    pi, pj = iota((256, 256), 0), iota((256, 256), 1)
    sort = flag(
        ((pi >> 6) == ((pj & 15) >> 2)) & (((pi & 63) >> 2) == (pj >> 4)) & ((pi & 3) == (pj & 3))
    ).astype(BF)
    turn[...] = flag(
        ((pi >> 4) == ((pj & 63) >> 2)) & (((pi & 15) >> 2) == (pj >> 6)) & ((pi & 3) == (pj & 3))
    ).astype(BF)

    lax.fori_loop(1, SEQ, arrived_piece, 0)
    total = got[0].astype(F32)
    for j in range(1, SEQ):
        total = total + got[j].astype(F32)
    vert[me] = total.astype(BF)
    lax.fori_loop(1, SEQ, start_share, 0)

    loads[4].wait()
    for d in (1, 2, 3):
        halo(d).wait()
    qi = lax.broadcasted_iota(jnp.int32, (2 * BLK, 8 * BLK), 0)
    ki = lax.broadcasted_iota(jnp.int32, (2 * BLK, 8 * BLK), 1)
    spacing = (qi >> 6) + MAXOFF - (ki >> 6)
    banded = spacing == offsets[0, 0]
    for t in range(1, 4):
        banded = banded | (spacing == offsets[0, t])
    banded = banded & ((ki >> 6) + 2 * me >= MAXOFF)
    allowed = banded | ((spacing == 0) & ((ki & 63) <= (qi & 63)))
    K[: 8 * BLK, :] = near[0].reshape(8 * BLK, HD)
    V[: 8 * BLK, :HD] = near[1].reshape(8 * BLK, HD)
    V[:, HD:] = jnp.ones((24 * BLK, HD), BF)
    scale = math.log2(math.e) / math.sqrt(HD)
    nt = (((1,), (1,)), ((), ()))

    def near_head(h):
        qh = q[:, pl.ds(pl.multiple_of(h * HD, HD), HD)]
        sn = lax.dot_general(qh, K[: 8 * BLK, :], nt, preferred_element_type=F32)
        sn = jnp.where(allowed, sn, -jnp.inf)
        top = jnp.max(sn, axis=1, keepdims=True)
        en = jnp.exp2((sn - top) * scale).astype(BF)
        near_o[h] = jnp.dot(en, V[: 8 * BLK, :], preferred_element_type=F32)
        near_top[h] = jnp.broadcast_to(top, (QLEN, HD))

    def some_near(i, _):
        for k in range(3):
            near_head(i * 3 + k)
        return 0

    lax.fori_loop(0, GROUP // 3, some_near, 0)
    lax.fori_loop(1, SEQ, arrived_share, 0)
    K[8 * BLK :, :] = vert[:, :, :HD].reshape(NV * BLK, HD)
    V[8 * BLK :, :HD] = vert[:, :, HD:].reshape(NV * BLK, HD)

    def head(h):
        cols = pl.ds(pl.multiple_of(h * HD, HD), HD)
        qh = q[:, cols]
        sv = lax.dot_general(qh, K[8 * BLK :, :], nt, preferred_element_type=F32)
        near_m = near_top[h]
        top = jnp.maximum(near_m, jnp.max(sv, axis=1, keepdims=True))
        ev = jnp.exp2((sv - top[:, :1]) * scale).astype(BF)
        o = jnp.dot(ev, V[8 * BLK :, :], preferred_element_type=F32)
        fade = jnp.exp2((near_m - top) * scale)
        o = o + near_o[h] * jnp.concatenate([fade, fade], axis=1)
        o = o[:, :HD] / o[:, HD:]
        G[me, :, cols] = o.astype(BF)

    def some_heads(i, _):
        for k in range(3):
            head(i * 3 + k)
        return 0

    def at(dy, dx):
        return lax.rem(y + dy + 4, 4) * 4 + lax.rem(x + dx + 4, 4)

    def part(src, half, rows):
        cols = pl.ds(half * HALF, HALF)
        if rows == 2:
            return G.at[src, :, cols]
        return G.at[src, pl.ds(rows * BLK, BLK), cols]

    sent = []

    def forward(dy, dx, half, rows, ty, tx):
        src, to = at(dy, dx), at(ty, tx)
        ref = part(src, half, rows)
        a = send(ref, ref, gs_sem.at[len(sent)], gr_sem.at[src, half, rows], seq=to)
        a.start()
        sent.append(a)

    def swap(half, a, b):
        return (a, b) if half == 0 else (b, a)

    def arrive(dy, dx, half):
        a, b = swap(half, dy, dx)
        split = a == 2 or (a == 0 and b == 2)
        src = at(dy, dx)
        for rows in ((0, 1) if split else (2,)):
            ref = part(src, half, rows)
            send(ref, ref, gs_sem.at[0], gr_sem.at[src, half, rows], seq=src).wait_recv()
        if a == 0 and b in (1, -1):
            forward(dy, dx, half, 0 if b == -1 else 1, *swap(half, 0, -b))
        if a == 0:
            forward(dy, dx, half, 2, *swap(half, 1, 0))
            forward(dy, dx, half, 2, *swap(half, -1, 0))
        elif a in (1, -1):
            forward(dy, dx, half, 0 if a == -1 else 1, *swap(half, -a, 0))

    def launch(half):
        for b in (1, -1):
            forward(0, 0, half, 2, *swap(half, 0, b))
        for a in (1, -1):
            forward(0, 0, half, 2, *swap(half, a, 0))

    lax.fori_loop(0, GROUP // 6, some_heads, 0)
    launch(0)
    lax.fori_loop(GROUP // 6, GROUP // 3, some_heads, 0)
    launch(1)
    loads[5].wait()
    loads[6].wait()

    order = [(0, 0), (0, 1), (0, -1), (1, 0), (-1, 0), (0, 2), (2, 0), (1, 1), (1, -1), (-1, 1),
             (-1, -1), (1, 2), (-1, 2), (2, 1), (2, -1), (2, 2)]

    spans = [(0, 5), (5, 11), (11, 15)]

    def sib_copy(g):
        ts = pl.ds(spans[g][0], spans[g][1] - spans[g][0])
        return send(sib_s.at[:, ts], sib_r.at[:, ts], bs_sem.at[g], br_sem.at[g],
                    exp=z * 2 + 1 - c)

    def z_copy(g, dz):
        to = lax.rem(z + dz, 4)
        ts = pl.ds(spans[g][0], spans[g][1] - spans[g][0])
        return send(z_s.at[to, ts], z_r.at[z, ts], zs_sem.at[g, dz], zr_sem.at[g, z],
                    exp=to * 2 + c)

    def z_arrive(g, dz):
        frm = lax.rem(z + dz, 4)
        ts = pl.ds(spans[g][0], spans[g][1] - spans[g][0])
        send(z_s.at[frm, ts], z_r.at[frm, ts], zs_sem.at[g, dz], zr_sem.at[g, frm],
             exp=frm * 2 + c).wait_recv()
        return frm

    def e_copy(d):
        to = lax.rem(e + d, EXP)
        return send(
            last_s.at[to], last_r.at[e], es_sem.at[d], er_sem.at[e], seq=opposite, exp=to
        )

    def p_copy(t):
        to = at(*order[t])
        return send(fin.at[t], proj.at[me], ps_sem.at[t], pr_sem.at[me], seq=to)

    def multiply(t):
        P_[...] = jnp.dot(G[at(*order[t])], w[...], preferred_element_type=F32)
        for zz in range(4):
            keep[zz, t] = P_[pl.ds(pl.multiple_of((zz * 2 + c) * ROWS, ROWS), ROWS), :]
            sib_s[zz, t] = P_[
                pl.ds(pl.multiple_of((zz * 2 + 1 - c) * ROWS, ROWS), ROWS), :
            ].astype(BF)
        if t in (4, 14):
            sib_copy(0 if t == 4 else 2).start()

    def pair(g):
        ts = slice(*spans[g])
        sib_copy(g).wait_recv()
        both = keep[:, ts] + sib_r[:, ts].astype(F32)
        keep[:, ts] = both
        z_s[:, ts] = both.astype(BF)
        for dz in (2, 1, 3):
            z_copy(g, dz).start()

    def finish(g):
        ts = slice(*spans[g])
        acc_ = keep[z, ts]
        for dz in (1, 3, 2):
            frm = z_arrive(g, dz)
            acc_ = acc_ + z_r[frm, ts].astype(F32)
        fin[ts] = acc_.astype(BF)
        for t in range(*spans[g]):
            if t > 0:
                p_copy(t).start()

    multiply(0)
    for dx in (1, -1):
        arrive(0, dx, 0)
        arrive(dx, 0, 1)
    for dx in (1, -1):
        arrive(0, dx, 1)
        arrive(dx, 0, 0)
    for t in (1, 2, 3, 4):
        multiply(t)
    arrive(0, 2, 0)
    arrive(2, 0, 1)
    pair(0)
    for dy in (1, -1):
        for dx in (1, -1):
            arrive(dy, dx, 0)
            arrive(dy, dx, 1)
    for t in (7, 8, 9, 10):
        multiply(t)
    arrive(0, 2, 1)
    arrive(2, 0, 0)
    for t in (5, 6):
        multiply(t)
    sib_copy(1).start()
    finish(0)
    pair(1)
    for s in (1, -1):
        arrive(s, 2, 0)
        arrive(2, s, 1)
    for s in (1, -1):
        arrive(s, 2, 1)
        arrive(2, s, 0)
    for t in (11, 12, 13, 14):
        multiply(t)
    finish(1)
    pair(2)
    arrive(2, 2, 0)
    arrive(2, 2, 1)
    P_[...] = jnp.dot(G[at(2, 2)], w[...], preferred_element_type=F32)
    last_s[...] = P_[...].astype(BF).reshape(EXP, ROWS, OC)
    for d in range(EXP):
        e_copy(d).start()
    finish(2)
    proj[me] = fin[0]
    for t in range(1, SEQ - 1):
        frm = at(*order[t])
        send(fin.at[0], proj.at[frm], ps_sem.at[0], pr_sem.at[frm], seq=frm).wait_recv()
    last = jnp.zeros((ROWS, OC), F32)
    for d in range(EXP):
        frm = lax.rem(e + d, EXP)
        send(
            last_s.at[0], last_r.at[frm], es_sem.at[0], er_sem.at[frm], seq=opposite, exp=frm
        ).wait_recv()
        last = last + last_r[frm].astype(F32)
    proj[opposite] = last.astype(BF)
    for s in range(SEQ):
        cols = slice(s * OC, s * OC + OC)
        stream[:, cols] = res[:, cols].astype(F32) + proj[s].astype(F32)

    st = stream[...]
    root = lax.rsqrt(jnp.mean(st * st, axis=1, keepdims=True) + 1e-06)
    for q in range(4):
        for s in range(4):
            cols = slice(q * DH + s * OC, q * DH + s * OC + OC)
            nst[q, s * ROWS : (s + 1) * ROWS, :] = (stream[:, cols] * root * gain[:, cols]).astype(BF)

    def d_copy(q, d):
        to = lax.rem(me + d, SEQ)
        return send(outg.at[q, to], arr.at[q, me], ds_sem.at[q, d], dr_sem.at[q, me], seq=to)


    def scatter(q):
        o = lax.dot_general(
            spread, nst[q], (((0,), (0,)), ((), ())), preferred_element_type=F32
        )
        outg[q] = o.astype(BF).reshape(SEQ, ROWS, OC)

        def start_d(d, _):
            d_copy(q, d).start()
            return 0

        lax.fori_loop(1, SEQ, start_d, 0)
        arr[q, me] = outg[q, me]

    def x_part(q):
        def part(j, rows):
            cols = pl.ds(q * DH, DH)
            if rows == 2:
                return X.at[j, :, cols]
            return X.at[j, pl.ds(rows * 32, 32), cols]

        return part

    rings = [
        Ring(e, x_part(q), lambda n, q=q: xs_sem.at[q, n], lambda j, r, q=q: xr_sem.at[q, j, r])
        for q in range(3)
    ]

    def begin(q):
        def arrived(d, _):
            frm = lax.rem(me + d, SEQ)
            send(outg.at[q, 0], arr.at[q, frm], ds_sem.at[q, 0], dr_sem.at[q, frm],
                 seq=frm).wait_recv()
            return 0

        lax.fori_loop(1, SEQ, arrived, 0)
        o = jnp.dot(sort, arr[q].reshape(256, OC), preferred_element_type=F32).astype(BF)
        for s in range(4):
            X[e, :, q * DH + s * OC : q * DH + s * OC + OC] = o[s * 64 : (s + 1) * 64]
        rings[q].own()

    def gate_up(q):
        if q < 3:
            rings[q].far()
            rings[q].across()
        if q == 0:
            loads[7].wait()
            loads[8].wait()
        cols = slice(q * DH, (q + 1) * DH)

        def some(m, _):
            xb = X[pl.ds(m * 4, 4), :, cols].reshape(256, DH)
            o = lax.dot_general(wt[:, cols], xb, nt, preferred_element_type=F32)
            if q > 0:
                o = o + acc[m]
            acc[m] = o
            return 0

        lax.fori_loop(0, 2, some, 0)

    def c_copy(d):
        to = lax.rem(me + d, SEQ)
        return send(outc.at[to], arrc.at[0, me], cs_sem.at[d], cr_sem.at[me], seq=to)

    def c2_copy():
        return send(arrc.at[0], arrc.at[1], c2_sem.at[0], c2_sem.at[1], exp=z * 2 + 1 - c)

    def cross():
        for k in range(4):
            frm = 4 * c + k

            @pl.when(frm != e)
            def _(k=k, frm=frm):
                send(spread_s, spreads.at[k], us_sem.at[0], ur_sem.at[k], exp=frm).wait_recv()
                send(nst.at[3], tokens.at[k], vs_sem.at[0], vr_sem.at[k], exp=frm).wait_recv()

            o = lax.dot_general(
                spreads[k], tokens[k], (((0,), (0,)), ((), ())), preferred_element_type=F32
            )
            outc[:, k] = o.astype(BF).reshape(SEQ, ROWS, OC)

        def start_c(d, _):
            c_copy(d).start()
            return 0

        lax.fori_loop(1, SEQ, start_c, 0)
        arrc[0, me] = outc[me]

    def cross_in():
        def arrived_c(d, _):
            frm = lax.rem(me + d, SEQ)
            send(outc.at[0], arrc.at[0, frm], cs_sem.at[0], cr_sem.at[frm], seq=frm).wait_recv()
            return 0

        lax.fori_loop(1, SEQ, arrived_c, 0)
        c2_copy().start()

    def settle(side, core):
        def one(k, _):
            o = jnp.dot(sort, arrc[side, :, k].reshape(256, OC), preferred_element_type=F32)
            o = o.astype(BF)
            for s in range(4):
                X[core * 4 + k, :, 3 * DH + s * OC : 3 * DH + s * OC + OC] = o[s * 64 : (s + 1) * 64]
            return 0

        lax.fori_loop(0, 4, one, 0)

    to_quad(lambda zz: v_copy(zz).start())

    @pl.when(quad == c)
    def _():
        tokens[member] = nst[3]

    scatter(0)
    scatter(1)
    begin(0)
    scatter(2)
    cross()
    begin(1)
    rings[0].near()
    begin(2)
    rings[1].near()
    gate_up(0)
    rings[2].near()
    cross_in()
    settle(0, c)
    gate_up(1)
    c2_copy().wait_recv()
    settle(1, 1 - c)
    gate_up(3)
    gate_up(2)

    def h_part(r):
        def part(j, rows):
            if rows == 2:
                return H.at[r, pl.ds(j * 320, 320), :]
            return H.at[r, pl.ds(j * 320 + rows * 160, 160), :]

        return part

    h_rings = [
        Ring(e, h_part(r), lambda n, r=r: hs_sem.at[r, n], lambda j, s, r=r: hr_sem.at[r, j, s])
        for r in range(2)
    ]
    for r in range(2):
        g, u = acc[r, :320], acc[r, 320:]
        hidden = (g / (1.0 + jnp.exp(-g)) * u).astype(BF)
        H[r, pl.ds(pl.multiple_of(e * 320, 64), 320), :] = lax.dot_general(
            hidden, turn[...], nt, preferred_element_type=F32
        ).astype(BF)
        h_rings[r].own()
    w_own.wait()
    for d in range(1, EXP):
        frm = lax.rem(e + d, EXP)
        send(wd.at[frm], wd.at[frm], ws_sem.at[0], wr_sem.at[frm], exp=frm).wait_recv()

    def o_copy(r, d):
        to = lax.rem(me + d, SEQ)
        return send(O.at[r, to], Z.at[r, me], os_sem.at[r, d], or_sem.at[r, me], seq=to)

    for r in range(2):
        h_rings[r].near()
    for r in range(2):
        h_rings[r].far()
        h_rings[r].across()
        o = lax.dot_general(
            H[r], wd[...].reshape(EXP * 320, HALF), (((0,), (0,)), ((), ())),
            preferred_element_type=F32,
        )
        O[r] = o.astype(BF).reshape(SEQ, ROWS, HALF)

        def start_o(d, _, r=r):
            o_copy(r, d).start()
            return 0

        lax.fori_loop(1, SEQ, start_o, 0)
        Z[r, me] = O[r, me]

    for d in range(1, EXP):
        frm = lax.rem(e + d, EXP)
        send(mats, mall.at[:, frm], ms_sem.at[0], mr_sem.at[frm], exp=frm).wait_recv()
    for r in range(2):
        def arrived_o(d, _, r=r):
            frm = lax.rem(me + d, SEQ)
            send(O.at[r, 0], Z.at[r, frm], os_sem.at[r, 0], or_sem.at[r, frm], seq=frm).wait_recv()
            return 0

        lax.fori_loop(1, SEQ, arrived_o, 0)
    m2 = jnp.dot(
        mall[...].reshape(256, 512), Z[...].reshape(512, HALF), preferred_element_type=F32
    )
    mix[...] = (m2[:128] + m2[128:]).astype(BF).reshape(EXP, ROWS, HALF)
    F[e] = mix[e]

    def f_copy(d):
        to = lax.rem(e + d, EXP)
        return send(mix.at[to], F.at[e], fs_sem.at[d], fr_sem.at[e], exp=to)

    for d in range(1, EXP):
        f_copy(d).start()
    for d in range(1, EXP):
        frm = lax.rem(e + d, EXP)
        send(mix.at[0], F.at[frm], fs_sem.at[0], fr_sem.at[frm], exp=frm).wait_recv()
    for j in range(EXP):
        cols = slice(j * HALF, (j + 1) * HALF)
        out[:, cols] = (stream[:, cols] + F[j].astype(F32)).astype(BF)

    def done_front(d, _):
        piece(d).wait_send()
        share(d).wait_send()
        return 0

    lax.fori_loop(1, SEQ, done_front, 0)
    for d in range(1, EXP):
        w_copy(d).wait_send()
    for a in sent:
        a.wait_send()
    for d in range(EXP):
        e_copy(d).wait_send()
    for g in range(3):
        sib_copy(g).wait_send()
        for dz in (1, 2, 3):
            z_copy(g, dz).wait_send()
    for t in range(1, SEQ - 1):
        p_copy(t).wait_send()


    def done(d, _):
        for q in range(3):
            d_copy(q, d).wait_send()
        c_copy(d).wait_send()
        for r in range(2):
            o_copy(r, d).wait_send()
        return 0

    lax.fori_loop(1, SEQ, done, 0)
    to_quad(lambda zz: u_copy(zz).wait_send())
    to_quad(lambda zz: v_copy(zz).wait_send())
    c2_copy().wait_send()
    for ring in rings + h_rings:
        ring.done()
    for d in range(1, EXP):
        m_copy(d).wait_send()
        f_copy(d).wait_send()


def layer_of(
    queries, keys, values, cache_keys, cache_values, vertical, offsets, o_weight, residual,
    norm_gain, expert_ids, gate_weights, w_gate, w_up, w_down,
):
    dma = pltpu.SemaphoreType.DMA
    vm = pltpu.VMEM
    return pl.pallas_call(
        layer_kernel,
        out_shape=jax.ShapeDtypeStruct((ROWS, WIDTH), BF),
        in_specs=[SM, SM] + [HBM] * 7 + [VM] * 3 + [HBM] * 3,
        out_specs=VM,
        scratch_shapes=[
            vm((NV * BLK, 2 * HD), BF),
            vm((NV * BLK, NV * BLK), BF),
            vm((NV, BLK, 2 * HD), BF),
            vm((QLEN, DH), BF),
            vm((2, 4, 2 * BLK, HD), BF),
            vm((DH, OC), BF),
            vm((ROWS, WIDTH), BF),
            vm((NV, BLK, 2 * HD), BF),
            vm((NV, BLK, 2 * HD), BF),
            vm((24 * BLK, HD), BF),
            vm((24 * BLK, 2 * HD), BF),
            vm((GROUP, QLEN, 2 * HD), F32),
            vm((GROUP, QLEN, HD), F32),
            vm((SEQ, QLEN, DH), BF),
            vm((QLEN, OC), F32),
            vm((4, SEQ, ROWS, OC), F32),
            vm((4, SEQ, ROWS, OC), BF),
            vm((4, SEQ, ROWS, OC), BF),
            vm((4, SEQ, ROWS, OC), BF),
            vm((4, SEQ, ROWS, OC), BF),
            vm((EXP, ROWS, OC), BF),
            vm((EXP, ROWS, OC), BF),
            vm((SEQ, ROWS, OC), BF),
            vm((SEQ, ROWS, OC), BF),
            vm((ROWS, WIDTH), F32),
            vm((640, WIDTH), BF),
            vm((EXP, 320, HALF), BF),
            vm((4, 64, OC), BF),
            vm((4, SEQ, ROWS, OC), BF),
            vm((4, SEQ, ROWS, OC), BF),
            vm((EXP, 64, WIDTH), BF),
            vm((64, 256), BF),
            vm((4, 64, 256), BF),
            vm((4, 64, OC), BF),
            vm((SEQ, 4, ROWS, OC), BF),
            vm((2, SEQ, 4, ROWS, OC), BF),
            vm((2, 640, 256), F32),
            vm((2, EXP * 320, 256), BF),
            vm((2, SEQ, ROWS, HALF), BF),
            vm((2, SEQ, ROWS, HALF), BF),
            vm((2, ROWS, 512), BF),
            vm((2, EXP, ROWS, 512), BF),
            vm((EXP, ROWS, HALF), BF),
            vm((EXP, ROWS, HALF), BF),
            vm((256, 256), BF),
            dma((9,)),
            dma((SEQ,)), dma((SEQ,)), dma((SEQ,)), dma((SEQ,)),
            dma((4,)), dma((4,)),
            dma((40,)), dma((SEQ, 2, 3)),
            dma((4,)), dma((4,)),
            dma((4, 4)), dma((4, 4)),
            dma((EXP,)), dma((EXP,)),
            dma((SEQ,)), dma((SEQ,)),
            dma((EXP,)), dma((EXP,)),
            dma((4, SEQ)), dma((4, SEQ)),
            dma((4, 8)), dma((4, EXP, 3)),
            dma((2, 8)), dma((2, EXP, 3)),
            dma((2, SEQ)), dma((2, SEQ)),
            dma((EXP,)), dma((EXP,)),
            dma((EXP,)), dma((EXP,)),
            dma((4,)), dma((4,)),
            dma((4,)), dma((4,)),
            dma((SEQ,)), dma((SEQ,)),
            dma((2,)),
        ],
        compiler_params=pltpu.CompilerParams(
            collective_id=0, has_side_effects=True, vmem_limit_bytes=62 * 2**20
        ),
        name="layer",
    )(
        vertical, offsets, cache_keys, cache_values, queries, keys, values, o_weight, residual,
        norm_gain.reshape(1, WIDTH), expert_ids.T, gate_weights.T,
        w_gate.transpose(0, 2, 1), w_up.transpose(0, 2, 1), w_down,
    )


def shards(
    queries,
    keys,
    values,
    cache_keys,
    cache_values,
    vertical,
    offsets,
    o_weight,
    residual,
    norm_gain,
    expert_ids,
    gate_weights,
    w_gate,
    w_up,
    w_down,
):
    return layer_of(
        queries, keys, values, cache_keys, cache_values, vertical, offsets, o_weight, residual,
        norm_gain, expert_ids, gate_weights, w_gate, w_up, w_down,
    )


def solution(mesh):
    in_specs = (
        P("seq", "exp"),
        P("seq", "exp"),
        P("seq", "exp"),
        P("seq", "exp"),
        P("seq", "exp"),
        P("exp", None),
        P("exp", None),
        P("exp", "seq"),
        P(("seq", "exp"), None),
        P(),
        P(("seq", "exp"), None),
        P(("seq", "exp"), None),
        P("seq", None, "exp"),
        P("seq", None, "exp"),
        P("seq", "exp", None),
    )
    out_specs = P(("seq", "exp"), None)
    return jax.shard_map(shards, mesh=mesh, in_specs=in_specs, out_specs=out_specs, check_vma=False)
```

```python
import functools
import math

import jax
import jax.numpy as jnp
from jax import lax
from jax.experimental import pallas as pl
from jax.experimental.pallas import tpu as pltpu
from jax.sharding import PartitionSpec as P

HD = 128
BLK = 64
NV = 16
MAXOFF = 6
SEQ = 16
EXP = 8
GROUP = 12
ROWS = 16
QLEN = 128
DH = 1536
HALF = 768
OC = 384
WIDTH = 6144
MESH = pl.DeviceIdType.MESH
BF = jnp.bfloat16
F32 = jnp.float32
VM = pl.BlockSpec(memory_space=pltpu.VMEM)
SM = pl.BlockSpec(memory_space=pltpu.SMEM)
HBM = pl.BlockSpec(memory_space=pl.ANY)


def greet(axis, me, size):
    barrier = pltpu.get_barrier_semaphore()

    def one(d, _):
        pl.semaphore_signal(
            barrier, inc=1, device_id={axis: lax.rem(me + d, size)}, device_id_type=MESH
        )
        return 0

    lax.fori_loop(1, size, one, 0)


def send(src, dst, s, r, **where):
    return pltpu.make_async_remote_copy(
        src_ref=src, dst_ref=dst, send_sem=s, recv_sem=r, device_id=where, device_id_type=MESH
    )


class Ring:
    def __init__(self, e, part, s_sem, r_sem):
        self.e, self.part, self.s_sem, self.r_sem = e, part, s_sem, r_sem
        self.z, self.c = e // 2, lax.rem(e, 2)
        self.sent = []

    def at(self, dz, dc=0):
        return lax.rem(self.z + dz + 4, 4) * 2 + (self.c if dc == 0 else 1 - self.c)

    def go(self, j, rows, to):
        ref = self.part(j, rows)
        a = send(ref, ref, self.s_sem(len(self.sent)), self.r_sem(j, rows), exp=to)
        a.start()
        self.sent.append(a)

    def wait(self, j, rows):
        ref = self.part(j, rows)
        send(ref, ref, self.s_sem(0), self.r_sem(j, rows), exp=self.at(0, 1)).wait_recv()

    def own(self):
        self.go(self.e, 2, self.at(1))
        self.go(self.e, 2, self.at(-1))
        self.go(self.e, 2, self.at(0, 1))

    def near(self):
        for dz in (-1, 1):
            j = self.at(dz)
            self.wait(j, 2)
            self.go(j, 0 if dz == -1 else 1, self.at(-dz))
            self.go(j, 2, self.at(0, 1))

    def far(self):
        j = self.at(2)
        self.wait(j, 0)
        self.wait(j, 1)
        self.go(j, 2, self.at(0, 1))

    def across(self):
        for dz in (0, 1, -1, 2):
            self.wait(self.at(dz, 1), 2)

    def done(self):
        for a in self.sent:
            a.wait_send()


def layer_kernel(
    vertical, offsets, ck_in, cv_in, q_in, k_in, v_in, w_in, res_in, gain, ids, gates, w_gate, w_up,
    w_down, out,
    cache, marks, sel, q, near, w, res, got, vert, K, V, near_o, near_top, G, P_, keep, sib_s, sib_r, z_s, z_r, last_s, last_r, fin, proj, stream,
    wt, wd, nst, outg, arr, X, spread_s, spreads, tokens, outc, arrc, acc, H, O, Z, mats, mall, mix, F, turn,
    l_sem, s_sem, r_sem, s2_sem, r2_sem, sh_sem, rh_sem,
    gs_sem, gr_sem, bs_sem, br_sem, zs_sem, zr_sem, es_sem, er_sem, ps_sem, pr_sem, ws_sem, wr_sem,
    ds_sem, dr_sem, xs_sem, xr_sem, hs_sem, hr_sem, os_sem, or_sem, ms_sem, mr_sem,
    fs_sem, fr_sem, us_sem, ur_sem, vs_sem, vr_sem, cs_sem, cr_sem, c2_sem,
):
    me = lax.axis_index("seq")
    e = lax.axis_index("exp")
    y, x = me // 4, lax.rem(me, 4)
    z, c = e // 2, lax.rem(e, 2)
    def iota(shape, dim):
        return lax.broadcasted_iota(jnp.int32, shape, dim)

    def flag(mask):
        return jnp.where(mask, 1.0, 0.0).astype(F32)

    greet("seq", me, SEQ)
    greet("exp", e, EXP)
    opposite = lax.rem(y + 2, 4) * 4 + lax.rem(x + 2, 4)
    for d in range(1, EXP):
        pl.semaphore_signal(
            pltpu.get_barrier_semaphore(), inc=1,
            device_id={"seq": opposite, "exp": lax.rem(e + d, EXP)}, device_id_type=MESH,
        )

    loads = [
        pltpu.make_async_copy(a, b, l_sem.at[i])
        for i, (a, b) in enumerate(
            [(ck_in, cache.at[:, :HD]), (cv_in, cache.at[:, HD:]), (k_in, near.at[0, 3]), (v_in, near.at[1, 3]), (q_in, q),
             (w_in, w), (res_in, res), (w_gate.at[0], wt.at[:320]), (w_up.at[0], wt.at[320:])]
        )
    ]
    for a in loads:
        a.start()
    loads[0].wait()
    loads[1].wait()
    apart = iota((BLK, NV * BLK), 1) - iota((BLK, NV * BLK), 0)
    for j in range(NV):
        marks[j * BLK : (j + 1) * BLK, :] = flag(
            apart == (vertical[0, j] - me * NV) * BLK
        ).astype(BF)

    def pick(m, _):
        rows = pl.ds(pl.multiple_of(m * 256, 256), 256)
        picked = jnp.dot(marks[rows, :], cache[...], preferred_element_type=F32)
        sel[pl.ds(m * 4, 4)] = picked.astype(BF).reshape(4, BLK, 2 * HD)
        return 0

    lax.fori_loop(0, 4, pick, 0)
    got[me] = sel[me]
    loads[2].wait()
    loads[3].wait()
    pl.semaphore_wait(pltpu.get_barrier_semaphore(), SEQ - 1 + 2 * (EXP - 1))

    def w_copy(d):
        to = lax.rem(e + d, EXP)
        cols = pl.ds(pl.multiple_of(to * HALF, HALF), HALF)
        return send(w_down.at[0, :, cols], wd.at[e], ws_sem.at[d], wr_sem.at[e], exp=to)

    def piece(d):
        to = lax.rem(me + d, SEQ)
        return send(sel.at[to], got.at[me], s_sem.at[d], r_sem.at[me], seq=to)

    def share(d):
        to = lax.rem(me + d, SEQ)
        return send(vert.at[me], vert.at[me], s2_sem.at[d], r2_sem.at[me], seq=to)

    def halo(d):
        to = lax.rem(me + d, SEQ)
        return send(near.at[:, 3], near.at[:, 3 - d], sh_sem.at[d], rh_sem.at[d], seq=to)

    def start_piece(d, _):
        piece(d).start()
        return 0

    def start_share(d, _):
        share(d).start()
        return 0

    def arrived_piece(d, _):
        frm = lax.rem(me + d, SEQ)
        send(sel.at[0], got.at[frm], s_sem.at[0], r_sem.at[frm], seq=frm).wait_recv()
        return 0

    def arrived_share(d, _):
        frm = lax.rem(me + d, SEQ)
        send(vert.at[me], vert.at[frm], s2_sem.at[0], r2_sem.at[frm], seq=frm).wait_recv()
        return 0

    lax.fori_loop(1, SEQ, start_piece, 0)
    for d in (1, 2, 3):
        halo(d).start()
    for d in range(1, EXP):
        w_copy(d).start()
    w_own = pltpu.make_async_copy(
        w_down.at[0, :, pl.ds(pl.multiple_of(e * HALF, HALF), HALF)], wd.at[e], ws_sem.at[0]
    )
    w_own.start()
    def column(row):
        same = iota((ROWS, ROWS), 0) == iota((ROWS, ROWS), 1)
        return jnp.sum(jnp.where(same, row.astype(F32), 0.0), axis=1, keepdims=True)

    first, second = column(ids[0:1, :]), column(ids[1:2, :])
    gate0, gate1 = column(gates[0:1, :]), column(gates[1:2, :])

    experts = iota((ROWS, SEQ), 1).astype(F32)
    hot0, hot1 = flag(experts == first), flag(experts == second)
    lower = flag(iota((ROWS, ROWS), 1) < iota((ROWS, ROWS), 0)).astype(BF)
    ones = jnp.ones((ROWS, ROWS), BF)
    before0 = jnp.dot(lower, hot0.astype(BF), preferred_element_type=F32)
    before1 = jnp.dot(lower, hot1.astype(BF), preferred_element_type=F32)
    before1 = before1 + jnp.dot(ones, hot0.astype(BF), preferred_element_type=F32)
    slot0 = jnp.sum(before0 * hot0, axis=1, keepdims=True)
    slot1 = jnp.sum(before1 * hot1, axis=1, keepdims=True)

    lanes = iota((4 * ROWS, 256), 1).astype(F32)
    quarter = (iota((4 * ROWS, 1), 0) >> 4).astype(F32) * 4.0
    t0 = jnp.concatenate([first * 16.0 + slot0] * 4, axis=0) + quarter
    t1 = jnp.concatenate([second * 16.0 + slot1] * 4, axis=0) + quarter
    spread = flag((lanes == t0) | (lanes == t1)).astype(BF)

    quad, member = e // 4, lax.rem(e, 4)
    spread_s[...] = spread

    def u_copy(zz):
        return send(spread_s, spreads.at[member], us_sem.at[zz], ur_sem.at[member],
                    exp=zz * 2 + quad)

    def v_copy(zz):
        return send(nst.at[3], tokens.at[member], vs_sem.at[zz], vr_sem.at[member],
                    exp=zz * 2 + quad)

    def to_quad(act):
        for zz in range(4):
            @pl.when(zz * 2 + quad != e)
            def _():
                act(zz)

    lanes = iota((ROWS, 256), 1).astype(F32)
    for h in range(2):
        place = (h * 8 + lax.rem(e, 2) * 4).astype(F32)
        weigh = jnp.where(lanes == first * 16.0 + slot0 + place, gate0, 0.0)
        weigh = weigh + jnp.where(lanes == second * 16.0 + slot1 + place, gate1, 0.0)
        high = weigh.astype(BF)
        mats[h, 0] = high
        mats[h, 1] = (weigh - high.astype(F32)).astype(BF)
    mall[e] = mats[...]

    def m_copy(d):
        to = lax.rem(e + d, EXP)
        return send(mats, mall.at[e], ms_sem.at[d], mr_sem.at[e], exp=to)

    for d in range(1, EXP):
        m_copy(d).start()
    to_quad(lambda zz: u_copy(zz).start())

    @pl.when(quad == c)
    def _():
        spreads[member] = spread

    pi, pj = iota((256, 256), 0), iota((256, 256), 1)
    sort = flag(
        ((pi >> 6) == ((pj & 15) >> 2)) & (((pi & 63) >> 2) == (pj >> 4)) & ((pi & 3) == (pj & 3))
    ).astype(BF)
    pi, pj = iota((128, 128), 0), iota((128, 128), 1)
    turn[...] = flag(
        ((pi >> 3) == ((pj & 63) >> 2)) & (((pi & 7) >> 2) == (pj >> 6)) & ((pi & 3) == (pj & 3))
    ).astype(BF)

    lax.fori_loop(1, SEQ, arrived_piece, 0)
    total = got[0].astype(F32)
    for j in range(1, SEQ):
        total = total + got[j].astype(F32)
    vert[me] = total.astype(BF)
    lax.fori_loop(1, SEQ, start_share, 0)

    loads[4].wait()
    for d in (1, 2, 3):
        halo(d).wait()
    qi = lax.broadcasted_iota(jnp.int32, (2 * BLK, 8 * BLK), 0)
    ki = lax.broadcasted_iota(jnp.int32, (2 * BLK, 8 * BLK), 1)
    spacing = (qi >> 6) + MAXOFF - (ki >> 6)
    banded = spacing == offsets[0, 0]
    for t in range(1, 4):
        banded = banded | (spacing == offsets[0, t])
    banded = banded & ((ki >> 6) + 2 * me >= MAXOFF)
    allowed = banded | ((spacing == 0) & ((ki & 63) <= (qi & 63)))
    K[: 8 * BLK, :] = near[0].reshape(8 * BLK, HD)
    V[: 8 * BLK, :HD] = near[1].reshape(8 * BLK, HD)
    V[:, HD:] = jnp.ones((24 * BLK, HD), BF)
    scale = math.log2(math.e) / math.sqrt(HD)
    nt = (((1,), (1,)), ((), ()))

    def near_head(h):
        qh = q[:, pl.ds(pl.multiple_of(h * HD, HD), HD)]
        sn = lax.dot_general(qh, K[: 8 * BLK, :], nt, preferred_element_type=F32)
        sn = jnp.where(allowed, sn, -jnp.inf)
        top = jnp.max(sn, axis=1, keepdims=True)
        en = jnp.exp2((sn - top) * scale).astype(BF)
        near_o[h] = jnp.dot(en, V[: 8 * BLK, :], preferred_element_type=F32)
        near_top[h] = jnp.broadcast_to(top, (QLEN, HD))

    def some_near(i, _):
        for k in range(3):
            near_head(i * 3 + k)
        return 0

    lax.fori_loop(0, GROUP // 3, some_near, 0)
    lax.fori_loop(1, SEQ, arrived_share, 0)
    K[8 * BLK :, :] = vert[:, :, :HD].reshape(NV * BLK, HD)
    V[8 * BLK :, :HD] = vert[:, :, HD:].reshape(NV * BLK, HD)

    def head(h):
        cols = pl.ds(pl.multiple_of(h * HD, HD), HD)
        qh = q[:, cols]
        sv = lax.dot_general(qh, K[8 * BLK :, :], nt, preferred_element_type=F32)
        near_m = near_top[h]
        top = jnp.maximum(near_m, jnp.max(sv, axis=1, keepdims=True))
        ev = jnp.exp2((sv - top[:, :1]) * scale).astype(BF)
        o = jnp.dot(ev, V[8 * BLK :, :], preferred_element_type=F32)
        fade = jnp.exp2((near_m - top) * scale)
        o = o + near_o[h] * jnp.concatenate([fade, fade], axis=1)
        o = o[:, :HD] / o[:, HD:]
        G[me, :, cols] = o.astype(BF)

    def some_heads(i, _):
        for k in range(3):
            head(i * 3 + k)
        return 0

    def at(dy, dx):
        return lax.rem(y + dy + 4, 4) * 4 + lax.rem(x + dx + 4, 4)

    def part(src, half, rows):
        cols = pl.ds(half * HALF, HALF)
        if rows == 2:
            return G.at[src, :, cols]
        return G.at[src, pl.ds(rows * BLK, BLK), cols]

    sent = []

    def forward(dy, dx, half, rows, ty, tx):
        src, to = at(dy, dx), at(ty, tx)
        ref = part(src, half, rows)
        a = send(ref, ref, gs_sem.at[len(sent)], gr_sem.at[src, half, rows], seq=to)
        a.start()
        sent.append(a)

    def swap(half, a, b):
        return (a, b) if half == 0 else (b, a)

    def arrive(dy, dx, half):
        a, b = swap(half, dy, dx)
        split = a == 2 or (a == 0 and b == 2)
        src = at(dy, dx)
        for rows in ((0, 1) if split else (2,)):
            ref = part(src, half, rows)
            send(ref, ref, gs_sem.at[0], gr_sem.at[src, half, rows], seq=src).wait_recv()
        if a == 0 and b in (1, -1):
            forward(dy, dx, half, 0 if b == -1 else 1, *swap(half, 0, -b))
        if a == 0:
            forward(dy, dx, half, 2, *swap(half, 1, 0))
            forward(dy, dx, half, 2, *swap(half, -1, 0))
        elif a in (1, -1):
            forward(dy, dx, half, 0 if a == -1 else 1, *swap(half, -a, 0))

    def launch(half):
        for b in (1, -1):
            forward(0, 0, half, 2, *swap(half, 0, b))
        for a in (1, -1):
            forward(0, 0, half, 2, *swap(half, a, 0))

    lax.fori_loop(0, GROUP // 6, some_heads, 0)
    launch(0)
    lax.fori_loop(GROUP // 6, GROUP // 3, some_heads, 0)
    launch(1)
    loads[5].wait()
    loads[6].wait()

    order = [(0, 0), (0, 1), (0, -1), (1, 0), (-1, 0), (0, 2), (2, 0), (1, 1), (1, -1), (-1, 1),
             (-1, -1), (1, 2), (-1, 2), (2, 1), (2, -1), (2, 2)]

    spans = [(0, 5), (5, 11), (11, 15)]

    def sib_copy(g):
        ts = pl.ds(spans[g][0], spans[g][1] - spans[g][0])
        return send(sib_s.at[:, ts], sib_r.at[:, ts], bs_sem.at[g], br_sem.at[g],
                    exp=z * 2 + 1 - c)

    def z_copy(g, dz):
        to = lax.rem(z + dz, 4)
        ts = pl.ds(spans[g][0], spans[g][1] - spans[g][0])
        return send(z_s.at[to, ts], z_r.at[z, ts], zs_sem.at[g, dz], zr_sem.at[g, z],
                    exp=to * 2 + c)

    def z_arrive(g, dz):
        frm = lax.rem(z + dz, 4)
        ts = pl.ds(spans[g][0], spans[g][1] - spans[g][0])
        send(z_s.at[frm, ts], z_r.at[frm, ts], zs_sem.at[g, dz], zr_sem.at[g, frm],
             exp=frm * 2 + c).wait_recv()
        return frm

    def e_copy(d):
        to = lax.rem(e + d, EXP)
        return send(
            last_s.at[to], last_r.at[e], es_sem.at[d], er_sem.at[e], seq=opposite, exp=to
        )

    def p_copy(t):
        to = at(*order[t])
        return send(fin.at[t], proj.at[me], ps_sem.at[t], pr_sem.at[me], seq=to)

    def multiply(t):
        P_[...] = jnp.dot(G[at(*order[t])], w[...], preferred_element_type=F32)
        for zz in range(4):
            keep[zz, t] = P_[pl.ds(pl.multiple_of((zz * 2 + c) * ROWS, ROWS), ROWS), :]
            sib_s[zz, t] = P_[
                pl.ds(pl.multiple_of((zz * 2 + 1 - c) * ROWS, ROWS), ROWS), :
            ].astype(BF)
        if t in (4, 14):
            sib_copy(0 if t == 4 else 2).start()

    def pair(g):
        ts = slice(*spans[g])
        sib_copy(g).wait_recv()
        both = keep[:, ts] + sib_r[:, ts].astype(F32)
        keep[:, ts] = both
        z_s[:, ts] = both.astype(BF)
        for dz in (2, 1, 3):
            z_copy(g, dz).start()

    def finish(g):
        ts = slice(*spans[g])
        acc_ = keep[z, ts]
        for dz in (1, 3, 2):
            frm = z_arrive(g, dz)
            acc_ = acc_ + z_r[frm, ts].astype(F32)
        fin[ts] = acc_.astype(BF)
        for t in range(*spans[g]):
            if t > 0:
                p_copy(t).start()

    multiply(0)
    for dx in (1, -1):
        arrive(0, dx, 0)
        arrive(dx, 0, 1)
    for dx in (1, -1):
        arrive(0, dx, 1)
        arrive(dx, 0, 0)
    for t in (1, 2, 3, 4):
        multiply(t)
    arrive(0, 2, 0)
    arrive(2, 0, 1)
    pair(0)
    for dy in (1, -1):
        for dx in (1, -1):
            arrive(dy, dx, 0)
            arrive(dy, dx, 1)
    for t in (7, 8, 9, 10):
        multiply(t)
    arrive(0, 2, 1)
    arrive(2, 0, 0)
    for t in (5, 6):
        multiply(t)
    sib_copy(1).start()
    finish(0)
    pair(1)
    for s in (1, -1):
        arrive(s, 2, 0)
        arrive(2, s, 1)
    for s in (1, -1):
        arrive(s, 2, 1)
        arrive(2, s, 0)
    for t in (11, 12, 13, 14):
        multiply(t)
    finish(1)
    pair(2)
    arrive(2, 2, 0)
    arrive(2, 2, 1)
    P_[...] = jnp.dot(G[at(2, 2)], w[...], preferred_element_type=F32)
    last_s[...] = P_[...].astype(BF).reshape(EXP, ROWS, OC)
    for d in range(EXP):
        e_copy(d).start()
    finish(2)
    proj[me] = fin[0]
    for t in range(1, SEQ - 1):
        frm = at(*order[t])
        send(fin.at[0], proj.at[frm], ps_sem.at[0], pr_sem.at[frm], seq=frm).wait_recv()
    last = jnp.zeros((ROWS, OC), F32)
    for d in range(EXP):
        frm = lax.rem(e + d, EXP)
        send(
            last_s.at[0], last_r.at[frm], es_sem.at[0], er_sem.at[frm], seq=opposite, exp=frm
        ).wait_recv()
        last = last + last_r[frm].astype(F32)
    proj[opposite] = last.astype(BF)
    for s in range(SEQ):
        cols = slice(s * OC, s * OC + OC)
        stream[:, cols] = res[:, cols].astype(F32) + proj[s].astype(F32)

    st = stream[...]
    root = lax.rsqrt(jnp.mean(st * st, axis=1, keepdims=True) + 1e-06)
    for q in range(4):
        for s in range(4):
            cols = slice(q * DH + s * OC, q * DH + s * OC + OC)
            nst[q, s * ROWS : (s + 1) * ROWS, :] = (stream[:, cols] * root * gain[:, cols]).astype(BF)

    def d_copy(q, d):
        to = lax.rem(me + d, SEQ)
        return send(outg.at[q, to], arr.at[q, me], ds_sem.at[q, d], dr_sem.at[q, me], seq=to)


    def scatter(q):
        o = lax.dot_general(
            spread, nst[q], (((0,), (0,)), ((), ())), preferred_element_type=F32
        )
        outg[q] = o.astype(BF).reshape(SEQ, ROWS, OC)

        def start_d(d, _):
            d_copy(q, d).start()
            return 0

        lax.fori_loop(1, SEQ, start_d, 0)
        arr[q, me] = outg[q, me]

    def x_part(q):
        def part(j, rows):
            cols = pl.ds(q * DH, DH)
            if rows == 2:
                return X.at[j, :, cols]
            return X.at[j, pl.ds(rows * 32, 32), cols]

        return part

    rings = [
        Ring(e, x_part(q), lambda n, q=q: xs_sem.at[q, n], lambda j, r, q=q: xr_sem.at[q, j, r])
        for q in range(3)
    ]

    def begin(q):
        def arrived(d, _):
            frm = lax.rem(me + d, SEQ)
            send(outg.at[q, 0], arr.at[q, frm], ds_sem.at[q, 0], dr_sem.at[q, frm],
                 seq=frm).wait_recv()
            return 0

        lax.fori_loop(1, SEQ, arrived, 0)
        o = jnp.dot(sort, arr[q].reshape(256, OC), preferred_element_type=F32).astype(BF)
        for s in range(4):
            X[e, :, q * DH + s * OC : q * DH + s * OC + OC] = o[s * 64 : (s + 1) * 64]
        rings[q].own()

    def gate_up(q):
        if q < 3:
            rings[q].far()
            rings[q].across()
        if q == 0:
            loads[7].wait()
            loads[8].wait()
        cols = slice(q * DH, (q + 1) * DH)

        def some(m, _):
            xb = X[pl.ds(m * 4, 4), :, cols].reshape(256, DH)
            o = lax.dot_general(wt[:, cols], xb, nt, preferred_element_type=F32)
            if q > 0:
                o = o + acc[m]
            acc[m] = o
            return 0

        lax.fori_loop(0, 2, some, 0)

    def c_copy(d):
        to = lax.rem(me + d, SEQ)
        return send(outc.at[to], arrc.at[0, me], cs_sem.at[d], cr_sem.at[me], seq=to)

    def c2_copy():
        return send(arrc.at[0], arrc.at[1], c2_sem.at[0], c2_sem.at[1], exp=z * 2 + 1 - c)

    def cross():
        for k in range(4):
            frm = 4 * c + k

            @pl.when(frm != e)
            def _(k=k, frm=frm):
                send(spread_s, spreads.at[k], us_sem.at[0], ur_sem.at[k], exp=frm).wait_recv()
                send(nst.at[3], tokens.at[k], vs_sem.at[0], vr_sem.at[k], exp=frm).wait_recv()

            o = lax.dot_general(
                spreads[k], tokens[k], (((0,), (0,)), ((), ())), preferred_element_type=F32
            )
            outc[:, k] = o.astype(BF).reshape(SEQ, ROWS, OC)

        def start_c(d, _):
            c_copy(d).start()
            return 0

        lax.fori_loop(1, SEQ, start_c, 0)
        arrc[0, me] = outc[me]

    def cross_in():
        def arrived_c(d, _):
            frm = lax.rem(me + d, SEQ)
            send(outc.at[0], arrc.at[0, frm], cs_sem.at[0], cr_sem.at[frm], seq=frm).wait_recv()
            return 0

        lax.fori_loop(1, SEQ, arrived_c, 0)
        c2_copy().start()

    def settle(side, core):
        def one(k, _):
            o = jnp.dot(sort, arrc[side, :, k].reshape(256, OC), preferred_element_type=F32)
            o = o.astype(BF)
            for s in range(4):
                X[core * 4 + k, :, 3 * DH + s * OC : 3 * DH + s * OC + OC] = o[s * 64 : (s + 1) * 64]
            return 0

        lax.fori_loop(0, 4, one, 0)

    to_quad(lambda zz: v_copy(zz).start())

    @pl.when(quad == c)
    def _():
        tokens[member] = nst[3]

    scatter(0)
    scatter(1)
    begin(0)
    scatter(2)
    cross()
    begin(1)
    rings[0].near()
    begin(2)
    rings[1].near()
    gate_up(0)
    rings[2].near()
    cross_in()
    settle(0, c)
    gate_up(1)
    c2_copy().wait_recv()
    settle(1, 1 - c)
    gate_up(3)
    gate_up(2)

    def h_part(r):
        def part(j, rows):
            if rows == 2:
                return H.at[r, pl.ds(j * 320, 320), :]
            return H.at[r, pl.ds(j * 320 + rows * 160, 160), :]

        return part

    h_rings = [
        Ring(e, h_part(r), lambda n, r=r: hs_sem.at[r, n], lambda j, s, r=r: hr_sem.at[r, j, s])
        for r in range(4)
    ]
    for r in range(4):
        cols = slice(r % 2 * 128, r % 2 * 128 + 128)
        g, u = acc[r // 2, :320, cols], acc[r // 2, 320:, cols]
        hidden = (g / (1.0 + jnp.exp(-g)) * u).astype(BF)
        H[r, pl.ds(pl.multiple_of(e * 320, 64), 320), :] = lax.dot_general(
            hidden, turn[...], nt, preferred_element_type=F32
        ).astype(BF)
        if r < 2:
            h_rings[r].own()
    h_rings[0].near()
    h_rings[2].own()
    h_rings[1].near()
    w_own.wait()
    for d in range(1, EXP):
        frm = lax.rem(e + d, EXP)
        send(wd.at[frm], wd.at[frm], ws_sem.at[0], wr_sem.at[frm], exp=frm).wait_recv()

    def o_copy(r, d):
        to = lax.rem(me + d, SEQ)
        return send(O.at[r, to], Z.at[r, me], os_sem.at[r, d], or_sem.at[r, me], seq=to)

    def outward(r):
        h_rings[r].far()
        h_rings[r].across()
        o = lax.dot_general(
            H[r], wd[...].reshape(EXP * 320, HALF), (((0,), (0,)), ((), ())),
            preferred_element_type=F32,
        ).reshape(SEQ, 8, HALF)
        O[r] = jnp.concatenate([o[:, :, :OC], o[:, :, OC:]], axis=1).astype(BF)

        def start_o(d, _):
            o_copy(r, d).start()
            return 0

        lax.fori_loop(1, SEQ, start_o, 0)
        Z[r, me] = O[r, me]

    def f_copy(j):
        return send(mix.at[j], F.at[e], fs_sem.at[j], fr_sem.at[e], exp=j)

    def blend(r):
        def arrived_o(d, _):
            frm = lax.rem(me + d, SEQ)
            send(O.at[r, 0], Z.at[r, frm], os_sem.at[r, 0], or_sem.at[r, frm], seq=frm).wait_recv()
            return 0

        lax.fori_loop(1, SEQ, arrived_o, 0)
        m = jnp.dot(
            mall[2 * r : 2 * r + 2].reshape(128, 256), Z[r].reshape(256, OC),
            preferred_element_type=F32,
        ).reshape(2, 2, 2, ROWS, OC)
        for k in range(2):
            for h in range(2):
                mix[2 * r + k, :, h * OC : (h + 1) * OC] = (m[k, h, 0] + m[k, h, 1]).astype(BF)

            @pl.when(e != 2 * r + k)
            def _(j=2 * r + k):
                f_copy(j).start()

    outward(0)
    h_rings[3].own()
    h_rings[2].near()
    outward(1)
    h_rings[3].near()
    for d in range(1, EXP):
        frm = lax.rem(e + d, EXP)
        send(mats, mall.at[frm], ms_sem.at[0], mr_sem.at[frm], exp=frm).wait_recv()
    outward(2)
    blend(0)
    outward(3)
    for r in (1, 2, 3):
        blend(r)
    F[e] = mix[e]
    for d in range(1, EXP):
        frm = lax.rem(e + d, EXP)
        send(mix.at[0], F.at[frm], fs_sem.at[0], fr_sem.at[frm], exp=frm).wait_recv()
    for j in range(EXP):
        cols = slice(j * HALF, (j + 1) * HALF)
        out[:, cols] = (stream[:, cols] + F[j].astype(F32)).astype(BF)

    def done_front(d, _):
        piece(d).wait_send()
        share(d).wait_send()
        return 0

    lax.fori_loop(1, SEQ, done_front, 0)
    for d in range(1, EXP):
        w_copy(d).wait_send()
    for a in sent:
        a.wait_send()
    for d in range(EXP):
        e_copy(d).wait_send()
    for g in range(3):
        sib_copy(g).wait_send()
        for dz in (1, 2, 3):
            z_copy(g, dz).wait_send()
    for t in range(1, SEQ - 1):
        p_copy(t).wait_send()


    def done(d, _):
        for q in range(3):
            d_copy(q, d).wait_send()
        c_copy(d).wait_send()
        for r in range(4):
            o_copy(r, d).wait_send()
        return 0

    lax.fori_loop(1, SEQ, done, 0)
    to_quad(lambda zz: u_copy(zz).wait_send())
    to_quad(lambda zz: v_copy(zz).wait_send())
    c2_copy().wait_send()
    for ring in rings + h_rings:
        ring.done()
    for d in range(1, EXP):
        m_copy(d).wait_send()
        f_copy(lax.rem(e + d, EXP)).wait_send()


def layer_of(
    queries, keys, values, cache_keys, cache_values, vertical, offsets, o_weight, residual,
    norm_gain, expert_ids, gate_weights, w_gate, w_up, w_down,
):
    dma = pltpu.SemaphoreType.DMA
    vm = pltpu.VMEM
    return pl.pallas_call(
        layer_kernel,
        out_shape=jax.ShapeDtypeStruct((ROWS, WIDTH), BF),
        in_specs=[SM, SM] + [HBM] * 7 + [VM] * 3 + [HBM] * 3,
        out_specs=VM,
        scratch_shapes=[
            vm((NV * BLK, 2 * HD), BF),
            vm((NV * BLK, NV * BLK), BF),
            vm((NV, BLK, 2 * HD), BF),
            vm((QLEN, DH), BF),
            vm((2, 4, 2 * BLK, HD), BF),
            vm((DH, OC), BF),
            vm((ROWS, WIDTH), BF),
            vm((NV, BLK, 2 * HD), BF),
            vm((NV, BLK, 2 * HD), BF),
            vm((24 * BLK, HD), BF),
            vm((24 * BLK, 2 * HD), BF),
            vm((GROUP, QLEN, 2 * HD), F32),
            vm((GROUP, QLEN, HD), F32),
            vm((SEQ, QLEN, DH), BF),
            vm((QLEN, OC), F32),
            vm((4, SEQ, ROWS, OC), F32),
            vm((4, SEQ, ROWS, OC), BF),
            vm((4, SEQ, ROWS, OC), BF),
            vm((4, SEQ, ROWS, OC), BF),
            vm((4, SEQ, ROWS, OC), BF),
            vm((EXP, ROWS, OC), BF),
            vm((EXP, ROWS, OC), BF),
            vm((SEQ, ROWS, OC), BF),
            vm((SEQ, ROWS, OC), BF),
            vm((ROWS, WIDTH), F32),
            vm((640, WIDTH), BF),
            vm((EXP, 320, HALF), BF),
            vm((4, 64, OC), BF),
            vm((4, SEQ, ROWS, OC), BF),
            vm((4, SEQ, ROWS, OC), BF),
            vm((EXP, 64, WIDTH), BF),
            vm((64, 256), BF),
            vm((4, 64, 256), BF),
            vm((4, 64, OC), BF),
            vm((SEQ, 4, ROWS, OC), BF),
            vm((2, SEQ, 4, ROWS, OC), BF),
            vm((2, 640, 256), F32),
            vm((4, EXP * 320, 128), BF),
            vm((4, SEQ, ROWS, OC), BF),
            vm((4, SEQ, ROWS, OC), BF),
            vm((2, 2, ROWS, 256), BF),
            vm((EXP, 2, 2, ROWS, 256), BF),
            vm((EXP, ROWS, HALF), BF),
            vm((EXP, ROWS, HALF), BF),
            vm((128, 128), BF),
            dma((9,)),
            dma((SEQ,)), dma((SEQ,)), dma((SEQ,)), dma((SEQ,)),
            dma((4,)), dma((4,)),
            dma((40,)), dma((SEQ, 2, 3)),
            dma((4,)), dma((4,)),
            dma((4, 4)), dma((4, 4)),
            dma((EXP,)), dma((EXP,)),
            dma((SEQ,)), dma((SEQ,)),
            dma((EXP,)), dma((EXP,)),
            dma((4, SEQ)), dma((4, SEQ)),
            dma((4, 8)), dma((4, EXP, 3)),
            dma((4, 8)), dma((4, EXP, 3)),
            dma((4, SEQ)), dma((4, SEQ)),
            dma((EXP,)), dma((EXP,)),
            dma((EXP,)), dma((EXP,)),
            dma((4,)), dma((4,)),
            dma((4,)), dma((4,)),
            dma((SEQ,)), dma((SEQ,)),
            dma((2,)),
        ],
        compiler_params=pltpu.CompilerParams(
            collective_id=0, has_side_effects=True, vmem_limit_bytes=62 * 2**20
        ),
        name="layer",
    )(
        vertical, offsets, cache_keys, cache_values, queries, keys, values, o_weight, residual,
        norm_gain.reshape(1, WIDTH), expert_ids.T, gate_weights.T,
        w_gate.transpose(0, 2, 1), w_up.transpose(0, 2, 1), w_down,
    )


def shards(
    queries,
    keys,
    values,
    cache_keys,
    cache_values,
    vertical,
    offsets,
    o_weight,
    residual,
    norm_gain,
    expert_ids,
    gate_weights,
    w_gate,
    w_up,
    w_down,
):
    return layer_of(
        queries, keys, values, cache_keys, cache_values, vertical, offsets, o_weight, residual,
        norm_gain, expert_ids, gate_weights, w_gate, w_up, w_down,
    )


def solution(mesh):
    in_specs = (
        P("seq", "exp"),
        P("seq", "exp"),
        P("seq", "exp"),
        P("seq", "exp"),
        P("seq", "exp"),
        P("exp", None),
        P("exp", None),
        P("exp", "seq"),
        P(("seq", "exp"), None),
        P(),
        P(("seq", "exp"), None),
        P(("seq", "exp"), None),
        P("seq", None, "exp"),
        P("seq", None, "exp"),
        P("seq", "exp", None),
    )
    out_specs = P(("seq", "exp"), None)
    return jax.shard_map(shards, mesh=mesh, in_specs=in_specs, out_specs=out_specs, check_vma=False)
```

```python
import functools
import math

import jax
import jax.numpy as jnp
from jax import lax
from jax.experimental import pallas as pl
from jax.experimental.pallas import tpu as pltpu
from jax.sharding import PartitionSpec as P

HD = 128
BLK = 64
NV = 16
MAXOFF = 6
SEQ = 16
EXP = 8
GROUP = 12
ROWS = 16
QLEN = 128
DH = 1536
HALF = 768
OC = 384
WIDTH = 6144
MESH = pl.DeviceIdType.MESH
BF = jnp.bfloat16
F32 = jnp.float32
VM = pl.BlockSpec(memory_space=pltpu.VMEM)
SM = pl.BlockSpec(memory_space=pltpu.SMEM)
HBM = pl.BlockSpec(memory_space=pl.ANY)


def greet(axis, me, size):
    barrier = pltpu.get_barrier_semaphore()

    def one(d, _):
        pl.semaphore_signal(
            barrier, inc=1, device_id={axis: lax.rem(me + d, size)}, device_id_type=MESH
        )
        return 0

    lax.fori_loop(1, size, one, 0)


def send(src, dst, s, r, **where):
    return pltpu.make_async_remote_copy(
        src_ref=src, dst_ref=dst, send_sem=s, recv_sem=r, device_id=where, device_id_type=MESH
    )


class Ring:
    def __init__(self, e, part, s_sem, r_sem):
        self.e, self.part, self.s_sem, self.r_sem = e, part, s_sem, r_sem
        self.z, self.c = e // 2, lax.rem(e, 2)
        self.sent = []

    def at(self, dz, dc=0):
        return lax.rem(self.z + dz + 4, 4) * 2 + (self.c if dc == 0 else 1 - self.c)

    def go(self, j, rows, to):
        ref = self.part(j, rows)
        a = send(ref, ref, self.s_sem(len(self.sent)), self.r_sem(j, rows), exp=to)
        a.start()
        self.sent.append(a)

    def wait(self, j, rows):
        ref = self.part(j, rows)
        send(ref, ref, self.s_sem(0), self.r_sem(j, rows), exp=self.at(0, 1)).wait_recv()

    def own(self):
        self.go(self.e, 2, self.at(1))
        self.go(self.e, 2, self.at(-1))
        self.go(self.e, 2, self.at(0, 1))

    def near(self):
        for dz in (-1, 1):
            j = self.at(dz)
            self.wait(j, 2)
            self.go(j, 0 if dz == -1 else 1, self.at(-dz))
            self.go(j, 2, self.at(0, 1))

    def far(self):
        j = self.at(2)
        self.wait(j, 0)
        self.wait(j, 1)
        self.go(j, 2, self.at(0, 1))

    def across(self):
        for dz in (0, 1, -1, 2):
            self.wait(self.at(dz, 1), 2)

    def done(self):
        for a in self.sent:
            a.wait_send()


def layer_kernel(
    vertical, offsets, ck_in, cv_in, q_in, k_in, v_in, w_in, res_in, gain, ids, gates, w_gate, w_up,
    w_down, out,
    cache, marks, sel, q, near, w, res, got, vert, K, V, near_o, near_top, G, P_, keep, sib_s, sib_r, z_s, z_r, last_s, last_r, fin, proj, stream,
    wt, wd, nst, outg, arr, X, spread_s, spreads, tokens, outc, arrc, acc, H, O, Z, mats, mall, mix, F, turn,
    l_sem, s_sem, r_sem, s2_sem, r2_sem, sh_sem, rh_sem,
    gs_sem, gr_sem, bs_sem, br_sem, zs_sem, zr_sem, es_sem, er_sem, ps_sem, pr_sem, ws_sem, wr_sem,
    ds_sem, dr_sem, xs_sem, xr_sem, hs_sem, hr_sem, os_sem, or_sem, ms_sem, mr_sem,
    fs_sem, fr_sem, us_sem, ur_sem, vs_sem, vr_sem, cs_sem, cr_sem, c2_sem,
):
    me = lax.axis_index("seq")
    e = lax.axis_index("exp")
    y, x = me // 4, lax.rem(me, 4)
    z, c = e // 2, lax.rem(e, 2)
    def iota(shape, dim):
        return lax.broadcasted_iota(jnp.int32, shape, dim)

    def flag(mask):
        return jnp.where(mask, 1.0, 0.0).astype(F32)

    greet("seq", me, SEQ)
    greet("exp", e, EXP)
    opposite = lax.rem(y + 2, 4) * 4 + lax.rem(x + 2, 4)
    for d in range(1, EXP):
        pl.semaphore_signal(
            pltpu.get_barrier_semaphore(), inc=1,
            device_id={"seq": opposite, "exp": lax.rem(e + d, EXP)}, device_id_type=MESH,
        )

    loads = [
        pltpu.make_async_copy(a, b, l_sem.at[i])
        for i, (a, b) in enumerate(
            [(ck_in, cache.at[:, :HD]), (cv_in, cache.at[:, HD:]), (k_in, near.at[0, 3]), (v_in, near.at[1, 3]), (q_in, q),
             (w_in, w), (res_in, res), (w_gate.at[0], wt.at[:320]), (w_up.at[0], wt.at[320:])]
        )
    ]
    for a in loads:
        a.start()
    loads[0].wait()
    loads[1].wait()
    apart = iota((BLK, NV * BLK), 1) - iota((BLK, NV * BLK), 0)
    for j in range(NV):
        marks[j * BLK : (j + 1) * BLK, :] = flag(
            apart == (vertical[0, j] - me * NV) * BLK
        ).astype(BF)

    def pick(m, _):
        rows = pl.ds(pl.multiple_of(m * 256, 256), 256)
        picked = jnp.dot(marks[rows, :], cache[...], preferred_element_type=F32)
        sel[pl.ds(m * 4, 4)] = picked.astype(BF).reshape(4, BLK, 2 * HD)
        return 0

    lax.fori_loop(0, 4, pick, 0)
    got[me] = sel[me]
    loads[2].wait()
    loads[3].wait()
    pl.semaphore_wait(pltpu.get_barrier_semaphore(), SEQ - 1 + 2 * (EXP - 1))

    def w_copy(d):
        to = lax.rem(e + d, EXP)
        cols = pl.ds(pl.multiple_of(to * HALF, HALF), HALF)
        return send(w_down.at[0, :, cols], wd.at[e], ws_sem.at[d], wr_sem.at[e], exp=to)

    def piece(d):
        to = lax.rem(me + d, SEQ)
        return send(sel.at[to], got.at[me], s_sem.at[d], r_sem.at[me], seq=to)

    def share(d):
        to = lax.rem(me + d, SEQ)
        return send(vert.at[me], vert.at[me], s2_sem.at[d], r2_sem.at[me], seq=to)

    def halo(d):
        to = lax.rem(me + d, SEQ)
        return send(near.at[:, 3], near.at[:, 3 - d], sh_sem.at[d], rh_sem.at[d], seq=to)

    def start_piece(d, _):
        piece(d).start()
        return 0

    def start_share(d, _):
        share(d).start()
        return 0

    def arrived_piece(d, _):
        frm = lax.rem(me + d, SEQ)
        send(sel.at[0], got.at[frm], s_sem.at[0], r_sem.at[frm], seq=frm).wait_recv()
        return 0

    def arrived_share(d, _):
        frm = lax.rem(me + d, SEQ)
        send(vert.at[me], vert.at[frm], s2_sem.at[0], r2_sem.at[frm], seq=frm).wait_recv()
        return 0

    lax.fori_loop(1, SEQ, start_piece, 0)
    for d in (1, 2, 3):
        halo(d).start()
    for d in range(1, EXP):
        w_copy(d).start()
    w_own = pltpu.make_async_copy(
        w_down.at[0, :, pl.ds(pl.multiple_of(e * HALF, HALF), HALF)], wd.at[e], ws_sem.at[0]
    )
    w_own.start()
    def column(row):
        same = iota((ROWS, ROWS), 0) == iota((ROWS, ROWS), 1)
        return jnp.sum(jnp.where(same, row.astype(F32), 0.0), axis=1, keepdims=True)

    first, second = column(ids[0:1, :]), column(ids[1:2, :])
    gate0, gate1 = column(gates[0:1, :]), column(gates[1:2, :])

    experts = iota((ROWS, SEQ), 1).astype(F32)
    hot0, hot1 = flag(experts == first), flag(experts == second)
    lower = flag(iota((ROWS, ROWS), 1) < iota((ROWS, ROWS), 0)).astype(BF)
    ones = jnp.ones((ROWS, ROWS), BF)
    before0 = jnp.dot(lower, hot0.astype(BF), preferred_element_type=F32)
    before1 = jnp.dot(lower, hot1.astype(BF), preferred_element_type=F32)
    before1 = before1 + jnp.dot(ones, hot0.astype(BF), preferred_element_type=F32)
    slot0 = jnp.sum(before0 * hot0, axis=1, keepdims=True)
    slot1 = jnp.sum(before1 * hot1, axis=1, keepdims=True)

    lanes = iota((4 * ROWS, 256), 1).astype(F32)
    quarter = (iota((4 * ROWS, 1), 0) >> 4).astype(F32) * 4.0
    t0 = jnp.concatenate([first * 16.0 + slot0] * 4, axis=0) + quarter
    t1 = jnp.concatenate([second * 16.0 + slot1] * 4, axis=0) + quarter
    spread = flag((lanes == t0) | (lanes == t1)).astype(BF)

    quad, member = e // 4, lax.rem(e, 4)
    spread_s[...] = spread

    def u_copy(zz):
        return send(spread_s, spreads.at[member], us_sem.at[zz], ur_sem.at[member],
                    exp=zz * 2 + quad)

    def v_copy(zz):
        return send(nst.at[3], tokens.at[member], vs_sem.at[zz], vr_sem.at[member],
                    exp=zz * 2 + quad)

    def to_quad(act):
        for zz in range(4):
            @pl.when(zz * 2 + quad != e)
            def _():
                act(zz)

    lanes = iota((ROWS, 256), 1).astype(F32)
    for h in range(2):
        place = (h * 8 + lax.rem(e, 2) * 4).astype(F32)
        weigh = jnp.where(lanes == first * 16.0 + slot0 + place, gate0, 0.0)
        weigh = weigh + jnp.where(lanes == second * 16.0 + slot1 + place, gate1, 0.0)
        high = weigh.astype(BF)
        mats[h, 0] = high
        mats[h, 1] = (weigh - high.astype(F32)).astype(BF)
    mall[e] = mats[...]

    def m_copy(d):
        to = lax.rem(e + d, EXP)
        return send(mats, mall.at[e], ms_sem.at[d], mr_sem.at[e], exp=to)

    for d in range(1, EXP):
        m_copy(d).start()
    to_quad(lambda zz: u_copy(zz).start())

    @pl.when(quad == c)
    def _():
        spreads[member] = spread

    pi, pj = iota((256, 256), 0), iota((256, 256), 1)
    sort = flag(
        ((pi >> 6) == ((pj & 15) >> 2)) & (((pi & 63) >> 2) == (pj >> 4)) & ((pi & 3) == (pj & 3))
    ).astype(BF)
    pi, pj = iota((128, 128), 0), iota((128, 128), 1)
    turn[...] = flag(
        ((pi >> 3) == ((pj & 63) >> 2)) & (((pi & 7) >> 2) == (pj >> 6)) & ((pi & 3) == (pj & 3))
    ).astype(BF)

    lax.fori_loop(1, SEQ, arrived_piece, 0)
    total = got[0].astype(F32)
    for j in range(1, SEQ):
        total = total + got[j].astype(F32)
    vert[me] = total.astype(BF)
    lax.fori_loop(1, SEQ, start_share, 0)

    loads[4].wait()
    for d in (1, 2, 3):
        halo(d).wait()
    qi = lax.broadcasted_iota(jnp.int32, (2 * BLK, 8 * BLK), 0)
    ki = lax.broadcasted_iota(jnp.int32, (2 * BLK, 8 * BLK), 1)
    spacing = (qi >> 6) + MAXOFF - (ki >> 6)
    banded = spacing == offsets[0, 0]
    for t in range(1, 4):
        banded = banded | (spacing == offsets[0, t])
    banded = banded & ((ki >> 6) + 2 * me >= MAXOFF)
    allowed = banded | ((spacing == 0) & ((ki & 63) <= (qi & 63)))
    K[: 8 * BLK, :] = near[0].reshape(8 * BLK, HD)
    V[: 8 * BLK, :HD] = near[1].reshape(8 * BLK, HD)
    V[:, HD:] = jnp.ones((24 * BLK, HD), BF)
    scale = math.log2(math.e) / math.sqrt(HD)
    nt = (((1,), (1,)), ((), ()))

    def near_head(h):
        qh = q[:, pl.ds(pl.multiple_of(h * HD, HD), HD)]
        sn = lax.dot_general(qh, K[: 8 * BLK, :], nt, preferred_element_type=F32)
        sn = jnp.where(allowed, sn, -jnp.inf)
        top = jnp.max(sn, axis=1, keepdims=True)
        en = jnp.exp2((sn - top) * scale).astype(BF)
        near_o[h] = jnp.dot(en, V[: 8 * BLK, :], preferred_element_type=F32)
        near_top[h] = jnp.broadcast_to(top, (QLEN, HD))

    def some_near(i, _):
        for k in range(6):
            near_head(i * 6 + k)
        return 0

    lax.fori_loop(0, GROUP // 6, some_near, 0)
    lax.fori_loop(1, SEQ, arrived_share, 0)
    K[8 * BLK :, :] = vert[:, :, :HD].reshape(NV * BLK, HD)
    V[8 * BLK :, :HD] = vert[:, :, HD:].reshape(NV * BLK, HD)

    def head(h):
        cols = pl.ds(pl.multiple_of(h * HD, HD), HD)
        qh = q[:, cols]
        sv = lax.dot_general(qh, K[8 * BLK :, :], nt, preferred_element_type=F32)
        near_m = near_top[h]
        top = jnp.maximum(near_m, jnp.max(sv, axis=1, keepdims=True))
        ev = jnp.exp2((sv - top[:, :1]) * scale).astype(BF)
        o = jnp.dot(ev, V[8 * BLK :, :], preferred_element_type=F32)
        fade = jnp.exp2((near_m - top) * scale)
        o = o + near_o[h] * jnp.concatenate([fade, fade], axis=1)
        o = o[:, :HD] / o[:, HD:]
        G[me, :, cols] = o.astype(BF)

    def some_heads(i, _):
        for k in range(6):
            head(i * 6 + k)
        return 0

    def at(dy, dx):
        return lax.rem(y + dy + 4, 4) * 4 + lax.rem(x + dx + 4, 4)

    def part(src, half, rows):
        cols = pl.ds(half * HALF, HALF)
        if rows == 2:
            return G.at[src, :, cols]
        return G.at[src, pl.ds(rows * BLK, BLK), cols]

    sent = []

    def forward(dy, dx, half, rows, ty, tx):
        src, to = at(dy, dx), at(ty, tx)
        ref = part(src, half, rows)
        a = send(ref, ref, gs_sem.at[len(sent)], gr_sem.at[src, half, rows], seq=to)
        a.start()
        sent.append(a)

    def swap(half, a, b):
        return (a, b) if half == 0 else (b, a)

    def arrive(dy, dx, half):
        a, b = swap(half, dy, dx)
        split = a == 2 or (a == 0 and b == 2)
        src = at(dy, dx)
        for rows in ((0, 1) if split else (2,)):
            ref = part(src, half, rows)
            send(ref, ref, gs_sem.at[0], gr_sem.at[src, half, rows], seq=src).wait_recv()
        if a == 0 and b in (1, -1):
            forward(dy, dx, half, 0 if b == -1 else 1, *swap(half, 0, -b))
        if a == 0:
            forward(dy, dx, half, 2, *swap(half, 1, 0))
            forward(dy, dx, half, 2, *swap(half, -1, 0))
        elif a in (1, -1):
            forward(dy, dx, half, 0 if a == -1 else 1, *swap(half, -a, 0))

    def launch(half):
        for b in (1, -1):
            forward(0, 0, half, 2, *swap(half, 0, b))
        for a in (1, -1):
            forward(0, 0, half, 2, *swap(half, a, 0))

    lax.fori_loop(0, 1, some_heads, 0)
    launch(0)
    lax.fori_loop(1, 2, some_heads, 0)
    launch(1)
    loads[5].wait()
    loads[6].wait()

    order = [(0, 0), (0, 1), (0, -1), (1, 0), (-1, 0), (0, 2), (2, 0), (1, 1), (1, -1), (-1, 1),
             (-1, -1), (1, 2), (-1, 2), (2, 1), (2, -1), (2, 2)]

    spans = [(0, 5), (5, 11), (11, 15)]

    def sib_copy(g):
        ts = pl.ds(spans[g][0], spans[g][1] - spans[g][0])
        return send(sib_s.at[:, ts], sib_r.at[:, ts], bs_sem.at[g], br_sem.at[g],
                    exp=z * 2 + 1 - c)

    def z_copy(g, dz):
        to = lax.rem(z + dz, 4)
        ts = pl.ds(spans[g][0], spans[g][1] - spans[g][0])
        return send(z_s.at[to, ts], z_r.at[z, ts], zs_sem.at[g, dz], zr_sem.at[g, z],
                    exp=to * 2 + c)

    def z_arrive(g, dz):
        frm = lax.rem(z + dz, 4)
        ts = pl.ds(spans[g][0], spans[g][1] - spans[g][0])
        send(z_s.at[frm, ts], z_r.at[frm, ts], zs_sem.at[g, dz], zr_sem.at[g, frm],
             exp=frm * 2 + c).wait_recv()
        return frm

    def e_copy(d):
        to = lax.rem(e + d, EXP)
        return send(
            last_s.at[to], last_r.at[e], es_sem.at[d], er_sem.at[e], seq=opposite, exp=to
        )

    def p_copy(t):
        to = at(*order[t])
        return send(fin.at[t], proj.at[me], ps_sem.at[t], pr_sem.at[me], seq=to)

    def multiply(t):
        P_[...] = jnp.dot(G[at(*order[t])], w[...], preferred_element_type=F32)
        for zz in range(4):
            keep[zz, t] = P_[pl.ds(pl.multiple_of((zz * 2 + c) * ROWS, ROWS), ROWS), :]
            sib_s[zz, t] = P_[
                pl.ds(pl.multiple_of((zz * 2 + 1 - c) * ROWS, ROWS), ROWS), :
            ].astype(BF)
        if t in (4, 14):
            sib_copy(0 if t == 4 else 2).start()

    def pair(g):
        ts = slice(*spans[g])
        sib_copy(g).wait_recv()
        both = keep[:, ts] + sib_r[:, ts].astype(F32)
        keep[:, ts] = both
        z_s[:, ts] = both.astype(BF)
        for dz in (2, 1, 3):
            z_copy(g, dz).start()

    def finish(g):
        ts = slice(*spans[g])
        acc_ = keep[z, ts]
        for dz in (1, 3, 2):
            frm = z_arrive(g, dz)
            acc_ = acc_ + z_r[frm, ts].astype(F32)
        fin[ts] = acc_.astype(BF)
        for t in range(*spans[g]):
            if t > 0:
                p_copy(t).start()

    multiply(0)
    for dx in (1, -1):
        arrive(0, dx, 0)
        arrive(dx, 0, 1)
    for dx in (1, -1):
        arrive(0, dx, 1)
        arrive(dx, 0, 0)
    for t in (1, 2, 3, 4):
        multiply(t)
    arrive(0, 2, 0)
    arrive(2, 0, 1)
    pair(0)
    for dy in (1, -1):
        for dx in (1, -1):
            arrive(dy, dx, 0)
            arrive(dy, dx, 1)
    for t in (7, 8, 9, 10):
        multiply(t)
    arrive(0, 2, 1)
    arrive(2, 0, 0)
    for t in (5, 6):
        multiply(t)
    sib_copy(1).start()
    finish(0)
    pair(1)
    for s in (1, -1):
        arrive(s, 2, 0)
        arrive(2, s, 1)
    for s in (1, -1):
        arrive(s, 2, 1)
        arrive(2, s, 0)
    for t in (11, 12, 13, 14):
        multiply(t)
    finish(1)
    pair(2)
    arrive(2, 2, 0)
    arrive(2, 2, 1)
    P_[...] = jnp.dot(G[at(2, 2)], w[...], preferred_element_type=F32)
    last_s[...] = P_[...].astype(BF).reshape(EXP, ROWS, OC)
    for d in range(EXP):
        e_copy(d).start()
    finish(2)
    proj[me] = fin[0]
    for t in range(1, SEQ - 1):
        frm = at(*order[t])
        send(fin.at[0], proj.at[frm], ps_sem.at[0], pr_sem.at[frm], seq=frm).wait_recv()
    last = jnp.zeros((ROWS, OC), F32)
    for d in range(EXP):
        frm = lax.rem(e + d, EXP)
        send(
            last_s.at[0], last_r.at[frm], es_sem.at[0], er_sem.at[frm], seq=opposite, exp=frm
        ).wait_recv()
        last = last + last_r[frm].astype(F32)
    proj[opposite] = last.astype(BF)
    for s in range(SEQ):
        cols = slice(s * OC, s * OC + OC)
        stream[:, cols] = res[:, cols].astype(F32) + proj[s].astype(F32)

    st = stream[...]
    root = lax.rsqrt(jnp.mean(st * st, axis=1, keepdims=True) + 1e-06)
    for q in range(4):
        for s in range(4):
            cols = slice(q * DH + s * OC, q * DH + s * OC + OC)
            nst[q, s * ROWS : (s + 1) * ROWS, :] = (stream[:, cols] * root * gain[:, cols]).astype(BF)

    def d_copy(q, d):
        to = lax.rem(me + d, SEQ)
        return send(outg.at[q, to], arr.at[q, me], ds_sem.at[q, d], dr_sem.at[q, me], seq=to)


    def scatter(q):
        o = lax.dot_general(
            spread, nst[q], (((0,), (0,)), ((), ())), preferred_element_type=F32
        )
        outg[q] = o.astype(BF).reshape(SEQ, ROWS, OC)

        def start_d(d, _):
            d_copy(q, d).start()
            return 0

        lax.fori_loop(1, SEQ, start_d, 0)
        arr[q, me] = outg[q, me]

    def x_part(q):
        def part(j, rows):
            cols = pl.ds(q * DH, DH)
            if rows == 2:
                return X.at[j, :, cols]
            return X.at[j, pl.ds(rows * 32, 32), cols]

        return part

    rings = [
        Ring(e, x_part(q), lambda n, q=q: xs_sem.at[q, n], lambda j, r, q=q: xr_sem.at[q, j, r])
        for q in range(3)
    ]

    def begin(q):
        def arrived(d, _):
            frm = lax.rem(me + d, SEQ)
            send(outg.at[q, 0], arr.at[q, frm], ds_sem.at[q, 0], dr_sem.at[q, frm],
                 seq=frm).wait_recv()
            return 0

        lax.fori_loop(1, SEQ, arrived, 0)
        o = jnp.dot(sort, arr[q].reshape(256, OC), preferred_element_type=F32).astype(BF)
        for s in range(4):
            X[e, :, q * DH + s * OC : q * DH + s * OC + OC] = o[s * 64 : (s + 1) * 64]
        rings[q].own()

    def gate_up(q):
        if q < 3:
            rings[q].far()
            rings[q].across()
        if q == 0:
            loads[7].wait()
            loads[8].wait()
        cols = slice(q * DH, (q + 1) * DH)

        def some(m, _):
            xb = X[pl.ds(m * 4, 4), :, cols].reshape(256, DH)
            o = lax.dot_general(wt[:, cols], xb, nt, preferred_element_type=F32)
            if q > 0:
                o = o + acc[m]
            acc[m] = o
            return 0

        lax.fori_loop(0, 2, some, 0)

    def c_copy(d):
        to = lax.rem(me + d, SEQ)
        return send(outc.at[to], arrc.at[0, me], cs_sem.at[d], cr_sem.at[me], seq=to)

    def c2_copy():
        return send(arrc.at[0], arrc.at[1], c2_sem.at[0], c2_sem.at[1], exp=z * 2 + 1 - c)

    def cross():
        for k in range(4):
            frm = 4 * c + k

            @pl.when(frm != e)
            def _(k=k, frm=frm):
                send(spread_s, spreads.at[k], us_sem.at[0], ur_sem.at[k], exp=frm).wait_recv()
                send(nst.at[3], tokens.at[k], vs_sem.at[0], vr_sem.at[k], exp=frm).wait_recv()

            o = lax.dot_general(
                spreads[k], tokens[k], (((0,), (0,)), ((), ())), preferred_element_type=F32
            )
            outc[:, k] = o.astype(BF).reshape(SEQ, ROWS, OC)

        def start_c(d, _):
            c_copy(d).start()
            return 0

        lax.fori_loop(1, SEQ, start_c, 0)
        arrc[0, me] = outc[me]

    def cross_in():
        def arrived_c(d, _):
            frm = lax.rem(me + d, SEQ)
            send(outc.at[0], arrc.at[0, frm], cs_sem.at[0], cr_sem.at[frm], seq=frm).wait_recv()
            return 0

        lax.fori_loop(1, SEQ, arrived_c, 0)
        c2_copy().start()

    def settle(side, core):
        def one(k, _):
            o = jnp.dot(sort, arrc[side, :, k].reshape(256, OC), preferred_element_type=F32)
            o = o.astype(BF)
            for s in range(4):
                X[core * 4 + k, :, 3 * DH + s * OC : 3 * DH + s * OC + OC] = o[s * 64 : (s + 1) * 64]
            return 0

        lax.fori_loop(0, 4, one, 0)

    to_quad(lambda zz: v_copy(zz).start())

    @pl.when(quad == c)
    def _():
        tokens[member] = nst[3]

    scatter(0)
    scatter(1)
    begin(0)
    scatter(2)
    cross()
    begin(1)
    rings[0].near()
    begin(2)
    rings[1].near()
    gate_up(0)
    rings[2].near()
    cross_in()
    settle(0, c)
    gate_up(1)
    c2_copy().wait_recv()
    settle(1, 1 - c)
    gate_up(3)
    gate_up(2)

    def h_part(r):
        def part(j, rows):
            if rows == 2:
                return H.at[r, pl.ds(j * 320, 320), :]
            return H.at[r, pl.ds(j * 320 + rows * 160, 160), :]

        return part

    h_rings = [
        Ring(e, h_part(r), lambda n, r=r: hs_sem.at[r, n], lambda j, s, r=r: hr_sem.at[r, j, s])
        for r in range(4)
    ]
    for r in range(4):
        cols = slice(r % 2 * 128, r % 2 * 128 + 128)
        g, u = acc[r // 2, :320, cols], acc[r // 2, 320:, cols]
        hidden = (g / (1.0 + jnp.exp(-g)) * u).astype(BF)
        H[r, pl.ds(pl.multiple_of(e * 320, 64), 320), :] = lax.dot_general(
            hidden, turn[...], nt, preferred_element_type=F32
        ).astype(BF)
        if r < 2:
            h_rings[r].own()
    h_rings[0].near()
    h_rings[2].own()
    h_rings[1].near()
    w_own.wait()
    for d in range(1, EXP):
        frm = lax.rem(e + d, EXP)
        send(wd.at[frm], wd.at[frm], ws_sem.at[0], wr_sem.at[frm], exp=frm).wait_recv()

    def o_copy(r, d):
        to = lax.rem(me + d, SEQ)
        return send(O.at[r, to], Z.at[r, me], os_sem.at[r, d], or_sem.at[r, me], seq=to)

    def outward(r):
        h_rings[r].far()
        h_rings[r].across()
        o = lax.dot_general(
            H[r], wd[...].reshape(EXP * 320, HALF), (((0,), (0,)), ((), ())),
            preferred_element_type=F32,
        ).reshape(SEQ, 8, HALF)
        O[r] = jnp.concatenate([o[:, :, :OC], o[:, :, OC:]], axis=1).astype(BF)

        def start_o(d, _):
            o_copy(r, d).start()
            return 0

        lax.fori_loop(1, SEQ, start_o, 0)
        Z[r, me] = O[r, me]

    def f_copy(j):
        return send(mix.at[j], F.at[e], fs_sem.at[j], fr_sem.at[e], exp=j)

    def blend(r):
        def arrived_o(d, _):
            frm = lax.rem(me + d, SEQ)
            send(O.at[r, 0], Z.at[r, frm], os_sem.at[r, 0], or_sem.at[r, frm], seq=frm).wait_recv()
            return 0

        lax.fori_loop(1, SEQ, arrived_o, 0)
        m = jnp.dot(
            mall[2 * r : 2 * r + 2].reshape(128, 256), Z[r].reshape(256, OC),
            preferred_element_type=F32,
        ).reshape(2, 2, 2, ROWS, OC)
        for k in range(2):
            for h in range(2):
                mix[2 * r + k, :, h * OC : (h + 1) * OC] = (m[k, h, 0] + m[k, h, 1]).astype(BF)

            @pl.when(e != 2 * r + k)
            def _(j=2 * r + k):
                f_copy(j).start()

    outward(0)
    h_rings[3].own()
    h_rings[2].near()
    outward(1)
    h_rings[3].near()
    for d in range(1, EXP):
        frm = lax.rem(e + d, EXP)
        send(mats, mall.at[frm], ms_sem.at[0], mr_sem.at[frm], exp=frm).wait_recv()
    outward(2)
    blend(0)
    outward(3)
    for r in (1, 2, 3):
        blend(r)
    F[e] = mix[e]
    for d in range(1, EXP):
        frm = lax.rem(e + d, EXP)
        send(mix.at[0], F.at[frm], fs_sem.at[0], fr_sem.at[frm], exp=frm).wait_recv()
    for j in range(EXP):
        cols = slice(j * HALF, (j + 1) * HALF)
        out[:, cols] = (stream[:, cols] + F[j].astype(F32)).astype(BF)

    def done_front(d, _):
        piece(d).wait_send()
        share(d).wait_send()
        return 0

    lax.fori_loop(1, SEQ, done_front, 0)
    for d in range(1, EXP):
        w_copy(d).wait_send()
    for a in sent:
        a.wait_send()
    for d in range(EXP):
        e_copy(d).wait_send()
    for g in range(3):
        sib_copy(g).wait_send()
        for dz in (1, 2, 3):
            z_copy(g, dz).wait_send()
    for t in range(1, SEQ - 1):
        p_copy(t).wait_send()


    def done(d, _):
        for q in range(3):
            d_copy(q, d).wait_send()
        c_copy(d).wait_send()
        for r in range(4):
            o_copy(r, d).wait_send()
        return 0

    lax.fori_loop(1, SEQ, done, 0)
    to_quad(lambda zz: u_copy(zz).wait_send())
    to_quad(lambda zz: v_copy(zz).wait_send())
    c2_copy().wait_send()
    for ring in rings + h_rings:
        ring.done()
    for d in range(1, EXP):
        m_copy(d).wait_send()
        f_copy(lax.rem(e + d, EXP)).wait_send()


def layer_of(
    queries, keys, values, cache_keys, cache_values, vertical, offsets, o_weight, residual,
    norm_gain, expert_ids, gate_weights, w_gate, w_up, w_down,
):
    dma = pltpu.SemaphoreType.DMA
    vm = pltpu.VMEM
    return pl.pallas_call(
        layer_kernel,
        out_shape=jax.ShapeDtypeStruct((ROWS, WIDTH), BF),
        in_specs=[SM, SM] + [HBM] * 7 + [VM] * 3 + [HBM] * 3,
        out_specs=VM,
        scratch_shapes=[
            vm((NV * BLK, 2 * HD), BF),
            vm((NV * BLK, NV * BLK), BF),
            vm((NV, BLK, 2 * HD), BF),
            vm((QLEN, DH), BF),
            vm((2, 4, 2 * BLK, HD), BF),
            vm((DH, OC), BF),
            vm((ROWS, WIDTH), BF),
            vm((NV, BLK, 2 * HD), BF),
            vm((NV, BLK, 2 * HD), BF),
            vm((24 * BLK, HD), BF),
            vm((24 * BLK, 2 * HD), BF),
            vm((GROUP, QLEN, 2 * HD), F32),
            vm((GROUP, QLEN, HD), F32),
            vm((SEQ, QLEN, DH), BF),
            vm((QLEN, OC), F32),
            vm((4, SEQ, ROWS, OC), F32),
            vm((4, SEQ, ROWS, OC), BF),
            vm((4, SEQ, ROWS, OC), BF),
            vm((4, SEQ, ROWS, OC), BF),
            vm((4, SEQ, ROWS, OC), BF),
            vm((EXP, ROWS, OC), BF),
            vm((EXP, ROWS, OC), BF),
            vm((SEQ, ROWS, OC), BF),
            vm((SEQ, ROWS, OC), BF),
            vm((ROWS, WIDTH), F32),
            vm((640, WIDTH), BF),
            vm((EXP, 320, HALF), BF),
            vm((4, 64, OC), BF),
            vm((4, SEQ, ROWS, OC), BF),
            vm((4, SEQ, ROWS, OC), BF),
            vm((EXP, 64, WIDTH), BF),
            vm((64, 256), BF),
            vm((4, 64, 256), BF),
            vm((4, 64, OC), BF),
            vm((SEQ, 4, ROWS, OC), BF),
            vm((2, SEQ, 4, ROWS, OC), BF),
            vm((2, 640, 256), F32),
            vm((4, EXP * 320, 128), BF),
            vm((4, SEQ, ROWS, OC), BF),
            vm((4, SEQ, ROWS, OC), BF),
            vm((2, 2, ROWS, 256), BF),
            vm((EXP, 2, 2, ROWS, 256), BF),
            vm((EXP, ROWS, HALF), BF),
            vm((EXP, ROWS, HALF), BF),
            vm((128, 128), BF),
            dma((9,)),
            dma((SEQ,)), dma((SEQ,)), dma((SEQ,)), dma((SEQ,)),
            dma((4,)), dma((4,)),
            dma((40,)), dma((SEQ, 2, 3)),
            dma((4,)), dma((4,)),
            dma((4, 4)), dma((4, 4)),
            dma((EXP,)), dma((EXP,)),
            dma((SEQ,)), dma((SEQ,)),
            dma((EXP,)), dma((EXP,)),
            dma((4, SEQ)), dma((4, SEQ)),
            dma((4, 8)), dma((4, EXP, 3)),
            dma((4, 8)), dma((4, EXP, 3)),
            dma((4, SEQ)), dma((4, SEQ)),
            dma((EXP,)), dma((EXP,)),
            dma((EXP,)), dma((EXP,)),
            dma((4,)), dma((4,)),
            dma((4,)), dma((4,)),
            dma((SEQ,)), dma((SEQ,)),
            dma((2,)),
        ],
        compiler_params=pltpu.CompilerParams(
            collective_id=0, has_side_effects=True, vmem_limit_bytes=62 * 2**20
        ),
        name="layer",
    )(
        vertical, offsets, cache_keys, cache_values, queries, keys, values, o_weight, residual,
        norm_gain.reshape(1, WIDTH), expert_ids.T, gate_weights.T,
        w_gate.transpose(0, 2, 1), w_up.transpose(0, 2, 1), w_down,
    )


def shards(
    queries,
    keys,
    values,
    cache_keys,
    cache_values,
    vertical,
    offsets,
    o_weight,
    residual,
    norm_gain,
    expert_ids,
    gate_weights,
    w_gate,
    w_up,
    w_down,
):
    return layer_of(
        queries, keys, values, cache_keys, cache_values, vertical, offsets, o_weight, residual,
        norm_gain, expert_ids, gate_weights, w_gate, w_up, w_down,
    )


def solution(mesh):
    in_specs = (
        P("seq", "exp"),
        P("seq", "exp"),
        P("seq", "exp"),
        P("seq", "exp"),
        P("seq", "exp"),
        P("exp", None),
        P("exp", None),
        P("exp", "seq"),
        P(("seq", "exp"), None),
        P(),
        P(("seq", "exp"), None),
        P(("seq", "exp"), None),
        P("seq", None, "exp"),
        P("seq", None, "exp"),
        P("seq", "exp", None),
    )
    out_specs = P(("seq", "exp"), None)
    return jax.shard_map(shards, mesh=mesh, in_specs=in_specs, out_specs=out_specs, check_vma=False)
```
